32 devices in a mesh: rows: 4 (over z), seq: 8 (over y, x, core).
Axes of the slice: x: 2, y: 2, z: 4, core: 2. Of those that a mesh axis runs over, the one named last changes fastest.
Arguments:
- inputs: bfloat16 [16, 4096, 1280], P('rows', 'seq'), may hold values from -6 to 6
- starts: int32 [16, 16], P('rows'), may hold values from 0 to 4095, as said below
- types: int32 [16, 4096], P('rows', 'seq'), may hold values from 0 to 29
- norm_gain_in: float32 [1280], replicated, may hold values from 0.25 to 1.75
- norm_bias_in: float32 [1280], replicated, may hold values from -2 to 2
- proj_down: bfloat16 [1280, 640], replicated, may hold values from -0.15625 to 0.15625
- proj_down_bias: float32 [640], replicated, may hold values from -2 to 2
- norm_gain_mid: float32 [640], replicated, may hold values from 0.25 to 1.75
- norm_bias_mid: float32 [640], replicated, may hold values from -2 to 2
- conv_weight: bfloat16 [5, 640, 640], replicated, may hold values from -0.109375 to 0.109375
- conv_bias: float32 [640], replicated, may hold values from -2 to 2
- norm_gain_out: float32 [640], replicated, may hold values from 0.25 to 1.75
- norm_bias_out: float32 [640], replicated, may hold values from -2 to 2
- proj_up: bfloat16 [640, 1280], replicated, may hold values from -0.3125 to 0.3125
- proj_up_bias: float32 [1280], replicated, may hold values from -1.5 to 1.5
- cotangent: bfloat16 [16, 4096, 1280], P('rows', 'seq'), may hold values from -6 to 6
Outputs:
- output: bfloat16 [16, 4096, 1280], P('rows', 'seq')
- input_grad: bfloat16 [16, 4096, 1280], P('rows', 'seq')
- grad_gain_in: float32 [1280], replicated
- grad_bias_in: float32 [1280], replicated
- grad_down: float32 [1280, 640], replicated
- grad_down_bias: float32 [640], replicated
- grad_gain_mid: float32 [640], replicated
- grad_bias_mid: float32 [640], replicated
- grad_conv: float32 [5, 640, 640], replicated
- grad_conv_bias: float32 [640], replicated
- grad_gain_out: float32 [640], replicated
- grad_bias_out: float32 [640], replicated
- grad_up: float32 [640, 1280], replicated
- grad_up_bias: float32 [1280], replicated
- type_counts: int32 [30], replicated
The draws below stay inside these ranges and needn't reach their ends.
Inputs may be any that keep to these rules, and one draw needn't show every extreme that they name: In every row starts rise strictly from starts[r, 0] = 0; protein j of row r covers positions starts[r, j] up to the next start (or the row's end).
All inputs are finite; a program needn't handle non-finite values.
Results may differ from the reference program's by a relative error of at most 0.0068.
Values may be sent and summed in bfloat16 or wider, within the bound.
No kernel may reach another device: no remote copies, remote signals or barrier semaphores. Data moves between devices by JAX's collectives and lax.ppermute only.
A program may use at most 192 MiB of HBM per device.

```python
import math
import jax
import jax.numpy as jnp
import numpy as np
from jax import lax

D = 1280
INNER = 640
KERNEL_TAPS = 5
DILATION_STEP = 128
TYPES = 30
STRETCH = 512
GROUP_ROWS = 4
ROWS = 16
ROW_LEN = 4096
PROTS = 16


def draw_starts(key, part):
    key = jax.random.fold_in(key, 7)
    key_rows, key_pick, key_gaps, key_last = jax.random.split(key, 4)

    def spread_row(subkey):
        picked = jax.random.permutation(subkey, ROW_LEN - 1)[:PROTS - 1] + 1
        return jnp.concatenate([jnp.zeros((1,), jnp.int32), jnp.sort(picked).astype(jnp.int32)])
    spread = jax.vmap(spread_row)(jax.random.split(key_rows, ROWS))
    gaps = jax.random.randint(key_gaps, (ROWS, PROTS - 2), 1, 3).astype(jnp.int32)
    last = jax.random.randint(key_last, (ROWS, 1), 1, STRETCH // 4 + 1).astype(jnp.int32)
    tail = jnp.sum(gaps, axis=1, keepdims=True) + last
    offsets = jnp.concatenate([jnp.zeros((ROWS, 1), jnp.int32), jnp.cumsum(gaps, axis=1).astype(jnp.int32)], axis=1)
    spanning = jnp.concatenate([jnp.zeros((ROWS, 1), jnp.int32), ROW_LEN - tail + offsets], axis=1)
    pick = jax.random.randint(key_pick, (ROWS // GROUP_ROWS,), 0, GROUP_ROWS).astype(jnp.int32)
    chosen = jnp.arange(ROWS, dtype=jnp.int32) % GROUP_ROWS == jnp.repeat(pick, GROUP_ROWS)
    return jnp.where(chosen[:, None], spanning, spread).astype(jnp.int32)


def touch_ends(values, own_key, least, high):
    spot = [jax.random.randint(jax.random.fold_in(own_key, axis), (), 0, length) for axis, length in enumerate(values.shape)]
    main_axis = values.shape.index(max(values.shape))
    next_to = spot[:main_axis] + [(spot[main_axis] + 1) % values.shape[main_axis]] + spot[main_axis + 1:]
    return values.at[tuple(spot)].set(least).at[tuple(next_to)].set(high)


def levels(key, extent, pieces, smallest, high):
    loudness = 1.0
    for dim, parts in pieces:
        heights = jax.random.uniform(jax.random.fold_in(jax.random.fold_in(key, 6), dim), (parts,), jnp.float32, smallest / len(pieces), high / len(pieces))
        loudness = loudness * jnp.repeat(jnp.exp(heights), extent[dim] // parts).reshape((-1,) + (1,) * (len(extent) - 1 - dim))
    return loudness


def cumulative_ranks(number_of, skew):
    portions = [(1 << 20) // math.isqrt(standing ** skew) + 1 for standing in range(1, number_of + 1)]
    scale = 1 + sum(portions) // (1 << 30)
    return np.cumsum(np.array([max(1, weight // scale) for weight in portions]))


def ranked(rng, shape, count, skew):
    table = cumulative_ranks(count, skew)
    ticket = jax.random.randint(jax.random.fold_in(rng, 1), shape, 0, int(table[count - 1]))
    rank = jnp.searchsorted(jnp.asarray(table, jnp.int32), ticket, side="right")
    return jax.random.permutation(jax.random.fold_in(rng, 2), count)[rank].astype(jnp.int32)


def bell_draw(key, dims, scale, limit, shards=(), kind=jnp.bfloat16):
    values = scale * jax.random.normal(key, dims, jnp.float32)
    if shards:
        values = values * levels(key, dims, shards, -0.22, 0.18)
    return jnp.clip(values, -limit, limit).astype(kind)


def setup_inputs(seed: int = 0) -> dict:
    streams_of = jax.random.split(jax.random.key(seed), 17)
    return {
        "inputs": bell_draw(streams_of[0], (ROWS, ROW_LEN, D), 1.0, 6.0, ((0, 4), (1, 8))),
        "starts": draw_starts(jax.random.fold_in(streams_of[16], 71), 0),
        "types": touch_ends(ranked(streams_of[2], (ROWS, ROW_LEN), TYPES, 2), jax.random.fold_in(streams_of[2], 3), 0, TYPES - 1).astype(jnp.int32),
        "norm_gain_in": jnp.clip(1.0 + 0.15 * jax.random.normal(streams_of[3], (D,), jnp.float32), 0.25, 1.75),
        "norm_bias_in": bell_draw(streams_of[4], (D,), 0.4, 2.0, (), jnp.float32),
        "proj_down": bell_draw(streams_of[5], (D, INNER), D ** -0.5, 0.15625),
        "proj_down_bias": bell_draw(streams_of[6], (INNER,), 0.4, 2.0, (), jnp.float32),
        "norm_gain_mid": jnp.clip(1.0 + 0.15 * jax.random.normal(streams_of[7], (INNER,), jnp.float32), 0.25, 1.75),
        "norm_bias_mid": bell_draw(streams_of[8], (INNER,), 0.4, 2.0, (), jnp.float32),
        "conv_weight": bell_draw(streams_of[9], (KERNEL_TAPS, INNER, INNER), (KERNEL_TAPS * INNER) ** -0.5, 0.109375),
        "conv_bias": bell_draw(streams_of[10], (INNER,), 0.4, 2.0, (), jnp.float32),
        "norm_gain_out": jnp.clip(1.0 + 0.15 * jax.random.normal(streams_of[11], (INNER,), jnp.float32), 0.25, 1.75),
        "norm_bias_out": bell_draw(streams_of[12], (INNER,), 0.4, 2.0, (), jnp.float32),
        "proj_up": bell_draw(streams_of[13], (INNER, D), (INNER // 2) ** -0.5, 0.3125),
        "proj_up_bias": bell_draw(streams_of[14], (D,), 0.3, 1.5, (), jnp.float32),
        "cotangent": bell_draw(streams_of[15], (ROWS, ROW_LEN, D), 1.0, 6.0, ((0, 4), (1, 8))),
    }


@jax.custom_vjp
def low(v):
    return lax.optimization_barrier(v.astype(jnp.bfloat16)).astype(jnp.float32)

@jax.custom_vjp
def low_back(v):
    return v

def low_keep(v):
    return (low(v), None)

def low_pass(kept, grad):
    return (grad,)

def back_keep(v):
    return (v, None)

def back_low(kept, grad):
    return (low(grad),)
low.defvjp(low_keep, low_pass)
low_back.defvjp(back_keep, back_low)

def norm_gelu(values, gain_vec, bias_vec):
    average = lax.optimization_barrier(jnp.mean(values, axis=-1, keepdims=True))
    centred = values - average
    spread = lax.optimization_barrier(jnp.mean(centred * centred, axis=-1, keepdims=True))
    return jax.nn.gelu(centred * lax.rsqrt(spread + 1e-05) * gain_vec + bias_vec, approximate=False)

def tap_masks(start_row):
    tap_places = jnp.arange(ROW_LEN, dtype=jnp.int32)
    protein = lax.optimization_barrier(jnp.sum((start_row[None, :] <= tap_places[:, None]).astype(jnp.int32), axis=1)).astype(jnp.int32)
    result = []
    for current_tap in range(KERNEL_TAPS):
        target_rows = tap_places + (current_tap - KERNEL_TAPS // 2) * DILATION_STEP
        inside = (target_rows >= 0) & (target_rows < ROW_LEN)
        clipped = jnp.clip(target_rows, 0, ROW_LEN - 1).astype(jnp.int32)
        result.append(inside & (jnp.take(protein, clipped) == protein))
    return jnp.stack(result)

def moved(field, tap_shift):
    kernel_reach = KERNEL_TAPS // 2 * DILATION_STEP
    padded_rows = jnp.pad(field, ((kernel_reach, kernel_reach), (0, 0)))
    return padded_rows[kernel_reach + tap_shift:kernel_reach + tap_shift + ROW_LEN]

def row_forward(row_in, param_set, mask_vals):
    gain_a, bias_a, down_w, down_b, gain_b, bias_b, conv_w, conv_b, gain_c, bias_c, up_w, up_b = param_set
    high = lax.Precision.HIGHEST
    first_act = low(norm_gelu(row_in, gain_a, bias_a))
    hidden = low_back(jnp.dot(first_act, down_w, precision=high) + down_b)
    conv_in = low(norm_gelu(hidden, gain_b, bias_b))
    mixed = conv_b + jnp.zeros((ROW_LEN, INNER), jnp.float32)
    for current_tap in range(KERNEL_TAPS):
        tap_shift = (current_tap - KERNEL_TAPS // 2) * DILATION_STEP
        mixed = mixed + mask_vals[current_tap][:, None] * jnp.dot(moved(conv_in, tap_shift), conv_w[current_tap], precision=high)
    mixed = low_back(mixed)
    last_act = low(norm_gelu(mixed, gain_c, bias_c))
    return row_in + jnp.dot(last_act, up_w, precision=high) + up_b

def reference(inputs, starts, types, norm_gain_in, norm_bias_in, proj_down, proj_down_bias, norm_gain_mid, norm_bias_mid, conv_weight, conv_bias, norm_gain_out, norm_bias_out, proj_up, proj_up_bias, cotangent):
    params = tuple((item.astype(jnp.float32) for item in (norm_gain_in, norm_bias_in, proj_down, proj_down_bias, norm_gain_mid, norm_bias_mid, conv_weight, conv_bias, norm_gain_out, norm_bias_out, proj_up, proj_up_bias)))
    kinds = jnp.arange(TYPES, dtype=jnp.int32)

    def step(totals, row_items):
        row_in, row_cot, start_row, type_row = row_items
        mask_bool = tap_masks(start_row)
        mask_vals = mask_bool.astype(jnp.float32)

        def inner(values, param_set):
            return row_forward(values, param_set, mask_vals)
        result, pull = jax.vjp(inner, row_in.astype(jnp.float32), params)
        grad_in, grad_params = pull(row_cot.astype(jnp.float32))
        full = jnp.all(mask_bool, axis=0)
        tally = lax.optimization_barrier(jnp.sum(((type_row[:, None] == kinds[None, :]) & full[:, None]).astype(jnp.int32), axis=0)).astype(jnp.int32)
        grad_sums = jax.tree.map(lambda total, part: total + part, totals[0], grad_params)
        return ((grad_sums, (totals[1] + tally).astype(jnp.int32)), (result.astype(jnp.bfloat16), grad_in.astype(jnp.bfloat16)))
    start_totals = (jax.tree.map(jnp.zeros_like, params), jnp.zeros((TYPES,), jnp.int32))
    (grads, counts), (outputs, input_grads) = lax.scan(step, start_totals, (inputs, cotangent, starts, types))
    return (outputs, input_grads, grads[0], grads[1], grads[2], grads[3], grads[4], grads[5], grads[6], grads[7], grads[8], grads[9], grads[10], grads[11], counts)
```

```python
from functools import reduce

import jax
import jax.numpy as jnp
from jax import lax
from jax.sharding import PartitionSpec as P

DILATION_STEP = 128
TYPES = 30


def extended(cells, sides, width):
    for axis, dim in sides:
        count = lax.axis_size(axis)
        ends = count - 1
        head = lax.slice_in_dim(cells, 0, width, axis=dim)
        tail = lax.slice_in_dim(cells, cells.shape[dim] - width, cells.shape[dim], axis=dim)
        cells = jnp.concatenate(
            [
                lax.ppermute(tail, axis, [(i, (i + 1) % count) for i in range(ends)]),
                cells,
                lax.ppermute(head, axis, [((i + 1) % count, i) for i in range(ends)]),
            ],
            axis=dim,
        )
    return cells


def bits_of(size):
    count = size.bit_length() - 1
    assert size == 1 << count
    return [1 << place for place in range(count)]


def exchange_plan():
    seq, rows = lax.axis_size("seq"), lax.axis_size("rows")
    here, row = lax.axis_index("seq"), lax.axis_index("rows")
    core = here & 1
    plan = [("seq", [(i, i ^ 1) for i in range(seq)], core)]
    even = bits_of(seq)[1:]
    for first, second in zip(even, even[::-1]):
        pairs = [(i, i ^ (second if i & 1 else first)) for i in range(seq)]
        side = jnp.where(core == 1, (here & second) != 0, (here & first) != 0)
        plan.append(("seq", pairs, side.astype(jnp.int32)))
    for bit in bits_of(rows):
        plan.append(("rows", [(i, i ^ bit) for i in range(rows)], ((row & bit) != 0).astype(jnp.int32)))
    return plan


def half_rows(count):
    return -(-count // 16) * 8


def scatter_sum(cells, plan):
    counts = []
    for axis, pairs, side in plan:
        count = cells.shape[0]
        half = half_rows(count)
        counts.append(count)
        sent = lax.dynamic_slice_in_dim(cells, (1 - side) * (count - half), half, axis=0)
        kept = lax.dynamic_slice_in_dim(cells, side * (count - half), half, axis=0)
        got = lax.ppermute(sent.astype(jnp.bfloat16), axis, pairs)
        cells = kept.astype(jnp.float32) + got.astype(jnp.float32)
    return cells.astype(jnp.bfloat16), counts


def gather_sum(cells, plan, counts):
    for (axis, pairs, side), count in zip(plan[::-1], counts[::-1]):
        half = cells.shape[0]
        got = lax.ppermute(cells, axis, pairs)
        low = jnp.where(side == 0, cells, got)
        high = jnp.where(side == 0, got, cells)
        cells = jnp.concatenate([low[: count - half], high], axis=0)
    return cells


def sum_everywhere(cells, plan):
    piece, counts = scatter_sum(cells, plan)
    return gather_sum(piece, plan, counts).astype(jnp.float32)


def sum_small(cells, plan):
    for axis, pairs, _ in plan:
        cells = cells + lax.ppermute(cells, axis, pairs)
    return cells


def norm_gelu(values, gain_vec, bias_vec):
    average = jnp.mean(values, axis=-1, keepdims=True)
    centred = values - average
    spread = jnp.mean(centred * centred, axis=-1, keepdims=True)
    return jax.nn.gelu(centred * lax.rsqrt(spread + 1e-05) * gain_vec + bias_vec, approximate=False)


def local(
    inputs,
    starts,
    types,
    norm_gain_in,
    norm_bias_in,
    proj_down,
    proj_down_bias,
    norm_gain_mid,
    norm_bias_mid,
    conv_weight,
    conv_bias,
    norm_gain_out,
    norm_bias_out,
    proj_up,
    proj_up_bias,
    cotangent,
):
    groups, dilated_span, width = inputs.shape
    kernel_taps = conv_weight.shape[0]
    kernel_reach = kernel_taps // 2 * DILATION_STEP
    row_length = dilated_span * lax.axis_size("seq")
    first = lax.axis_index("seq") * dilated_span
    tap_places = first - kernel_reach + jnp.arange(dilated_span + 2 * kernel_reach, dtype=jnp.int32)
    protein = jnp.sum((starts[:, None, :] <= tap_places[None, :, None]).astype(jnp.int32), axis=2)
    inside = (tap_places >= 0) & (tap_places < row_length)
    centre = protein[:, kernel_reach : kernel_reach + dilated_span]
    mask_list = []
    for current_tap in range(kernel_taps):
        window_begin = current_tap * DILATION_STEP
        mask_list.append(
            (protein[:, window_begin : window_begin + dilated_span] == centre)
            & inside[None, window_begin : window_begin + dilated_span]
        )
    mask_float = [item.astype(jnp.float32)[:, :, None] for item in mask_list]
    mask_low = [item.astype(jnp.bfloat16)[:, :, None] for item in mask_list]
    full = reduce(jnp.logical_and, mask_list)
    kinds = types[:, :, None] == jnp.arange(TYPES, dtype=jnp.int32)[None, None, :]
    tally = jnp.sum((kinds & full[:, :, None]).astype(jnp.float32), axis=(0, 1))
    x_full = inputs.astype(jnp.float32)
    act_in, pull_in = jax.vjp(norm_gelu, x_full, norm_gain_in, norm_bias_in)
    act_in_low = act_in.astype(jnp.bfloat16)
    hidden = (
        jnp.einsum("gcd,di->gci", act_in_low, proj_down, preferred_element_type=jnp.float32)
        + proj_down_bias
    )
    act_mid, pull_mid = jax.vjp(norm_gelu, hidden, norm_gain_mid, norm_bias_mid)
    conv_in = act_mid.astype(jnp.bfloat16)
    padded_rows = extended(conv_in, (("seq", 1),), kernel_reach)
    mixed = jnp.zeros((groups, dilated_span, conv_in.shape[2]), jnp.float32) + conv_bias
    for current_tap in range(kernel_taps):
        window_begin = current_tap * DILATION_STEP
        product = jnp.einsum(
            "gci,io->gco",
            padded_rows[:, window_begin : window_begin + dilated_span],
            conv_weight[current_tap],
            preferred_element_type=jnp.float32,
        )
        mixed = mixed + mask_float[current_tap] * product
    act_out, pull_out = jax.vjp(norm_gelu, mixed, norm_gain_out, norm_bias_out)
    act_out_low = act_out.astype(jnp.bfloat16)
    result = (
        x_full
        + jnp.einsum("gci,id->gcd", act_out_low, proj_up, preferred_element_type=jnp.float32)
        + proj_up_bias
    )
    output = result.astype(jnp.bfloat16)
    grad_up = jnp.einsum("gci,gcd->id", act_out_low, cotangent, preferred_element_type=jnp.float32)
    grad_up_bias = jnp.sum(cotangent.astype(jnp.float32), axis=(0, 1))
    grad_act_out = jnp.einsum("gcd,id->gci", cotangent, proj_up, preferred_element_type=jnp.float32)
    grad_mixed, grad_gain_out, grad_bias_out = pull_out(grad_act_out)
    grad_mixed_low = grad_mixed.astype(jnp.bfloat16)
    grad_conv_bias = jnp.sum(grad_mixed_low.astype(jnp.float32), axis=(0, 1))
    masked_grads = [grad_mixed_low * mask_low[current_tap] for current_tap in range(kernel_taps)]
    grad_conv = jnp.stack(
        [
            jnp.einsum(
                "gci,gco->io",
                padded_rows[
                    :, current_tap * DILATION_STEP : current_tap * DILATION_STEP + dilated_span
                ],
                masked_grads[current_tap],
                preferred_element_type=jnp.float32,
            )
            for current_tap in range(kernel_taps)
        ]
    )
    grad_padded = extended(grad_mixed_low, (("seq", 1),), kernel_reach)
    grad_conv_in = jnp.zeros((groups, dilated_span, conv_in.shape[2]), jnp.float32)
    for current_tap in range(kernel_taps):
        window_begin = 2 * kernel_reach - current_tap * DILATION_STEP
        term = jnp.einsum(
            "gco,io->gci",
            grad_padded[:, window_begin : window_begin + dilated_span],
            conv_weight[current_tap],
            preferred_element_type=jnp.float32,
        )
        grad_conv_in = grad_conv_in + mask_float[kernel_taps - 1 - current_tap] * term
    grad_hidden, grad_gain_mid, grad_bias_mid = pull_mid(grad_conv_in)
    grad_hidden_low = grad_hidden.astype(jnp.bfloat16)
    grad_down = jnp.einsum(
        "gcd,gci->di", act_in_low, grad_hidden_low, preferred_element_type=jnp.float32
    )
    grad_down_bias = jnp.sum(grad_hidden_low.astype(jnp.float32), axis=(0, 1))
    grad_act_in = jnp.einsum(
        "gci,di->gcd", grad_hidden_low, proj_down, preferred_element_type=jnp.float32
    )
    grad_x, grad_gain_in, grad_bias_in = pull_in(grad_act_in)
    input_grad = (cotangent.astype(jnp.float32) + grad_x).astype(jnp.bfloat16)
    plan = exchange_plan()
    total_up = sum_everywhere(grad_up, plan)
    total_conv = sum_everywhere(grad_conv.reshape(-1, grad_conv.shape[-1]), plan).reshape(grad_conv.shape)
    total_down = sum_everywhere(grad_down, plan)
    vectors = [
        grad_gain_in,
        grad_bias_in,
        grad_down_bias,
        grad_gain_mid,
        grad_bias_mid,
        grad_conv_bias,
        grad_gain_out,
        grad_bias_out,
        grad_up_bias,
        tally,
    ]
    ends = [0]
    for item in vectors:
        ends.append(ends[-1] + item.shape[0])
    flat = jnp.concatenate(vectors)
    flat = jnp.pad(flat, (0, -flat.shape[0] % 1024)).reshape(-1, 128)
    flat = sum_small(flat, plan).reshape(-1)
    sums = [flat[begin:end] for begin, end in zip(ends, ends[1:])]
    return (
        output,
        input_grad,
        sums[0],
        sums[1],
        total_down,
        sums[2],
        sums[3],
        sums[4],
        total_conv,
        sums[5],
        sums[6],
        sums[7],
        total_up,
        sums[8],
        sums[9].astype(jnp.int32),
    )


def solution(mesh):
    return jax.shard_map(
        local,
        mesh=mesh,
        in_specs=(
            P("rows", "seq", None),
            P("rows", None),
            P("rows", "seq"),
            P(),
            P(),
            P(),
            P(),
            P(),
            P(),
            P(),
            P(),
            P(),
            P(),
            P(),
            P(),
            P("rows", "seq", None),
        ),
        out_specs=(
            P("rows", "seq", None),
            P("rows", "seq", None),
            P(),
            P(),
            P(),
            P(),
            P(),
            P(),
            P(),
            P(),
            P(),
            P(),
            P(),
            P(),
            P(),
        ),
        check_vma=False,
    )
```

```python
import functools

import jax
import jax.numpy as jnp
from jax import lax
from jax.experimental import pallas as pl
from jax.experimental.pallas import tpu as pltpu
from jax.sharding import PartitionSpec as P

DILATION_STEP = 128
TYPES = 30
LANES = 128
SUB = 256
LOW = jnp.bfloat16
WIDE = jnp.float32
NN = (((1,), (0,)), ((), ()))
NT = (((1,), (1,)), ((), ()))
TN = (((0,), (0,)), ((), ()))


def bits_of(size):
    count = size.bit_length() - 1
    assert size == 1 << count
    return [1 << place for place in range(count)]


def exchange_plan():
    seq, rows = lax.axis_size("seq"), lax.axis_size("rows")
    here, row = lax.axis_index("seq"), lax.axis_index("rows")
    core = here & 1
    plan = [("seq", [(i, i ^ 1) for i in range(seq)], core)]
    even = bits_of(seq)[1:]
    for first, second in zip(even, even[::-1]):
        pairs = [(i, i ^ (second if i & 1 else first)) for i in range(seq)]
        side = jnp.where(core == 1, (here & second) != 0, (here & first) != 0)
        plan.append(("seq", pairs, side.astype(jnp.int32)))
    for bit in bits_of(rows):
        plan.append(("rows", [(i, i ^ bit) for i in range(rows)], ((row & bit) != 0).astype(jnp.int32)))
    return plan


def half_rows(count):
    return -(-count // 16) * 8


def scatter_sum(cells, plan):
    counts = []
    for axis, pairs, side in plan:
        count = cells.shape[0]
        half = half_rows(count)
        counts.append(count)
        sent = lax.dynamic_slice_in_dim(cells, (1 - side) * (count - half), half, axis=0)
        kept = lax.dynamic_slice_in_dim(cells, side * (count - half), half, axis=0)
        got = lax.ppermute(sent.astype(jnp.bfloat16), axis, pairs)
        cells = kept.astype(jnp.float32) + got.astype(jnp.float32)
    return cells.astype(jnp.bfloat16), counts


def gather_sum(cells, plan, counts):
    for (axis, pairs, side), count in zip(plan[::-1], counts[::-1]):
        half = cells.shape[0]
        got = lax.ppermute(cells, axis, pairs)
        low = jnp.where(side == 0, cells, got)
        high = jnp.where(side == 0, got, cells)
        cells = jnp.concatenate([low[: count - half], high], axis=0)
    return cells


def sum_everywhere(cells, plan):
    piece, counts = scatter_sum(cells, plan)
    return gather_sum(piece, plan, counts).astype(jnp.float32)


def sum_small(cells, plan):
    for axis, pairs, _ in plan:
        cells = cells + lax.ppermute(cells, axis, pairs)
    return cells


def dot(left, right, dims):
    return lax.dot_general(left, right, dims, preferred_element_type=WIDE)


def gelu_parts(u):
    phi = 0.5 + 0.5 * lax.erf(u * 0.7071067811865476)
    bell = jnp.exp2(u * u * -0.7213475204444817)
    return u * phi, phi + (u * 0.3989422804014327) * bell


def fold(values):
    return jnp.sum(values.reshape(-1, 8, values.shape[-1]), axis=0)


def column_mean(rows, count):
    total = jnp.zeros((8, LANES), WIDE)
    for i in range(count // 64):
        total = total + fold(rows(i))
    return jnp.sum(total, axis=0, keepdims=True) * (1.0 / count)


def identity(size):
    row = lax.broadcasted_iota(jnp.int32, (size, size), 0)
    return (row == lax.broadcasted_iota(jnp.int32, (size, size), 1)).astype(LOW)


def column(vector):
    size = vector.shape[0]
    return jnp.broadcast_to(vector[...].reshape(1, size), (LANES, size)).T


def enter_kernel(begun, steps, *refs):
    x, e, gain, bias, up = refs[:5]
    if begun:
        down, mid = refs[5:7]
        a1, s1, xh1, r1, z, s2, xh2, r2, ga3, h = refs[7:]
    else:
        straight, conv, down_bias, gain_mid, bias_mid = refs[5:10]
        a1, s1, xh1, r1, z, s2, xh2, r2, ga3, down, mid, ahead, h = refs[10:]
    span, width = x.shape
    inner = h.shape[0]
    gain_row, bias_row = gain[...].reshape(1, width), bias[...].reshape(1, width)

    if not begun:
        unit = identity(inner)

        @pl.when(pl.program_id(0) == 0)
        def _():
            down[...] = dot(unit, straight[...], NT).astype(LOW)
            mid[0] = column(down_bias)
            mid[1] = column(gain_mid)
            mid[2] = column(bias_mid)

        taps = conv.shape[0]
        share = -(-taps // steps)
        for j in range(share):
            k = jnp.minimum(pl.program_id(0) * share + j, taps - 1)
            ahead[:, pl.ds(pl.multiple_of(k * inner, LANES), inner)] = dot(unit, conv[k], NT).astype(LOW)

    def first(i):
        rows = pl.ds(i * 16, 16)
        v = x[rows, :].astype(WIDE)
        v = v - jnp.sum(v, axis=-1, keepdims=True) * (1.0 / width)
        r = lax.rsqrt(jnp.sum(v * v, axis=-1, keepdims=True) * (1.0 / width) + 1e-05)
        xh = v * r
        act, slope = gelu_parts(xh * gain_row + bias_row)
        a1[rows, :] = act.astype(LOW)
        s1[rows, :] = slope.astype(LOW)
        xh1[rows, :] = xh.astype(LOW)
        r1[rows, :] = jnp.broadcast_to(r, (16, LANES))

    def project(t):
        cols = pl.ds(t * SUB, SUB)
        product = dot(down[...], a1[cols, :], NT)
        for j in range(SUB // LANES):
            h[:, pl.ds(t * SUB + j * LANES, LANES)] = product[:, j * LANES : (j + 1) * LANES] + mid[0]
        ga3[:, cols] = dot(up[...], e[cols, :], NT)

    def second(j):
        cols = pl.ds(j * LANES, LANES)
        m = column_mean(lambda i: h[pl.ds(i * 64, 64), cols], inner)

        def squares(i):
            c = h[pl.ds(i * 64, 64), cols] - m
            return c * c

        r = lax.rsqrt(column_mean(squares, inner) + 1e-05)
        for i in range(inner // 32):
            rows = pl.ds(i * 32, 32)
            xh = (h[rows, cols] - m) * r
            act, slope = gelu_parts(xh * mid[1, rows, :] + mid[2, rows, :])
            z[rows, cols] = act.astype(LOW)
            s2[rows, cols] = slope.astype(LOW)
            xh2[rows, cols] = xh.astype(LOW)
        r2[:, cols] = jnp.broadcast_to(r, (8, LANES))

    for t in range(span // SUB):
        for i in range(SUB // 16):
            first(t * SUB // 16 + i)
        project(t)
        if t:
            for j in range(SUB // LANES):
                second((t - 1) * SUB // LANES + j)
    for j in range(SUB // LANES):
        second((span // SUB - 1) * SUB // LANES + j)


def windows(left, centre, right, mask, out, t):
    inner, span = centre.shape
    reach = left.shape[1] // LANES
    taps = 2 * reach + 1
    for k in range(taps):
        for j in range(SUB // LANES):
            block = t * (SUB // LANES) + k + j
            if block < reach:
                source = left[:, pl.ds(block * LANES, LANES)]
            elif block < reach + span // LANES:
                source = centre[:, pl.ds((block - reach) * LANES, LANES)]
            else:
                source = right[:, pl.ds((block - reach) * LANES - span, LANES)]
            cols = pl.ds(t * SUB + j * LANES, LANES)
            if k != reach:
                keep = mask[k if k < reach else k - 1, :, cols]
                source = (source.reshape(-1, 16, LANES) * keep[None]).reshape(inner, LANES)
            out[k * inner : (k + 1) * inner, cols] = source


def turn_kernel(begun, *refs):
    zl, zc, zr, mask, conv, ga3, x, e, up, up_bias, conv_bias, gain_out, bias_out = refs[:13]
    refs = refs[13:]
    if begun:
        (_, before), refs = refs[:2], refs[2:]
    y, gy, grad_up, vec, taps, act3, dy, xh3, out3 = refs
    inner, span = zc.shape
    width = x.shape[1]

    @pl.when(pl.program_id(0) == 0)
    def _():
        grad_up[...] = before[...] if begun else jnp.zeros_like(grad_up)
        vec[...] = jnp.zeros_like(vec)
        out3[0] = column(conv_bias)
        out3[1] = column(gain_out)
        out3[2] = column(bias_out)

    def third(j):
        cols = pl.ds(j * LANES, LANES)
        m = column_mean(lambda i: dy[pl.ds(i * 64, 64), cols], inner)

        def squares(i):
            c = dy[pl.ds(i * 64, 64), cols] - m
            return c * c

        r = lax.rsqrt(column_mean(squares, inner) + 1e-05)
        sum_one = jnp.zeros((8, LANES), WIDE)
        sum_two = jnp.zeros((8, LANES), WIDE)
        for i in range(inner // 32):
            rows = pl.ds(i * 32, 32)
            gain = out3[1, rows, :]
            xh = (dy[rows, cols] - m) * r
            act, slope = gelu_parts(xh * gain + out3[2, rows, :])
            act3[rows, cols] = act.astype(LOW)
            d = ga3[rows, cols] * slope
            vec[0, rows, :] += d
            vec[1, rows, :] += d * xh
            d = d * gain
            sum_one = sum_one + fold(d)
            sum_two = sum_two + fold(d * xh)
            dy[rows, cols] = d
            xh3[rows, cols] = xh
        one = jnp.sum(sum_one, axis=0, keepdims=True) * (1.0 / inner)
        two = jnp.sum(sum_two, axis=0, keepdims=True) * (1.0 / inner)
        for i in range(inner // 32):
            rows = pl.ds(i * 32, 32)
            low = (r * (dy[rows, cols] - one - xh3[rows, cols] * two)).astype(LOW)
            gy[rows, cols] = low
            vec[2, rows, :] += low.astype(WIDE)

    def convolve(t):
        windows(zl, zc, zr, mask, taps, t)
        cols = pl.ds(t * SUB, SUB)
        product = dot(conv[...], taps[:, cols], NN)
        for j in range(SUB // LANES):
            dy[:, pl.ds(t * SUB + j * LANES, LANES)] = product[:, j * LANES : (j + 1) * LANES] + out3[0]

    def finish(t):
        rows = pl.ds(t * SUB, SUB)
        product = dot(act3[:, rows], up[...], TN)
        y[rows, :] = (x[rows, :].astype(WIDE) + product + up_bias[...].reshape(1, width)).astype(LOW)

    tiles = span // SUB
    for t in range(tiles):
        convolve(t)
        if t:
            finish(t - 1)
        for j in range(SUB // LANES):
            third(t * SUB // LANES + j)
    finish(tiles - 1)
    grad_up[...] += dot(act3[...], e[...], NN)


def taps_kernel(parts, *refs):
    steps = pl.num_programs(0)
    step = pl.program_id(0)
    per = steps // parts
    out, total, taps = refs[5 * parts :]
    inner = out.shape[-1]

    @pl.when(step == 0)
    def _():
        total[...] = jnp.zeros_like(total)

    def add(zl, zc, zr, mask, gy):
        for t in range(zc.shape[1] // SUB):
            windows(zl, zc, zr, mask, taps, t)
        right = gy[...]
        for k in range(out.shape[0]):
            total[k] += dot(taps[k * inner : (k + 1) * inner, :], right, NT)

    for part in range(parts):

        @pl.when((step >= part * per) & (step < (part + 1) * per))
        def _():
            add(*refs[5 * part : 5 * part + 5])

    @pl.when(step == steps - 1)
    def _():
        out[...] = total[...].astype(out.dtype)


def inner_kernel(begun, *refs):
    gl, gc, gr, mask, straight, s2, xh2, r2, mid, a1 = refs[:10]
    refs = refs[10:]
    if begun:
        before, refs = refs[0], refs[1:]
    gh, grad_down, vec, conv, taps, gz = refs
    inner, span = gc.shape

    @pl.when(pl.program_id(0) == 0)
    def _():
        grad_down[...] = before[...] if begun else jnp.zeros_like(grad_down)
        vec[...] = jnp.zeros_like(vec)
        count = straight.shape[0]
        for k in range(count):
            conv[:, k * inner : (k + 1) * inner] = straight[count - 1 - k]

    def convolve(t):
        windows(gl, gc, gr, mask, taps, t)
        cols = pl.ds(t * SUB, SUB)
        gz[:, cols] = dot(conv[...], taps[:, cols], NN)

    def second(j):
        cols = pl.ds(j * LANES, LANES)
        sum_one = jnp.zeros((8, LANES), WIDE)
        sum_two = jnp.zeros((8, LANES), WIDE)
        for i in range(inner // 32):
            rows = pl.ds(i * 32, 32)
            xh = xh2[rows, cols].astype(WIDE)
            d = gz[rows, cols] * s2[rows, cols].astype(WIDE)
            vec[0, rows, :] += d
            vec[1, rows, :] += d * xh
            d = d * mid[1, rows, :]
            sum_one = sum_one + fold(d)
            sum_two = sum_two + fold(d * xh)
            gz[rows, cols] = d
        one = jnp.sum(sum_one, axis=0, keepdims=True) * (1.0 / inner)
        two = jnp.sum(sum_two, axis=0, keepdims=True) * (1.0 / inner)
        r = r2[0:1, cols]
        for i in range(inner // 32):
            rows = pl.ds(i * 32, 32)
            low = (r * (gz[rows, cols] - one - xh2[rows, cols].astype(WIDE) * two)).astype(LOW)
            gh[rows, cols] = low
            vec[2, rows, :] += low.astype(WIDE)

    for t in range(span // SUB):
        convolve(t)
        for j in range(SUB // LANES):
            second(t * SUB // LANES + j)
    grad_down[...] += dot(gh[...], a1[...], NN)


def leave_kernel(gh, down, s1, xh1, r1, gain, e, *refs):
    gx, vec, ga = refs[-3:]
    span, width = e.shape
    gain_row = gain[...].reshape(1, width)

    @pl.when(pl.program_id(0) == 0)
    def _():
        vec[...] = jnp.zeros_like(vec)

    def project(t):
        rows = pl.ds(t * SUB, SUB)
        ga[rows, :] = dot(gh[:, rows], down[...], TN)

    def first(i):
        rows = pl.ds(i * 16, 16)
        xh = xh1[rows, :].astype(WIDE)
        d = ga[rows, :] * s1[rows, :].astype(WIDE)
        vec[0] += fold(d)
        vec[1] += fold(d * xh)
        d = d * gain_row
        one = jnp.sum(d, axis=-1, keepdims=True) * (1.0 / width)
        two = jnp.sum(d * xh, axis=-1, keepdims=True) * (1.0 / width)
        r = r1[rows, 0:1]
        cot = e[rows, :].astype(WIDE)
        vec[2] += fold(cot)
        gx[rows, :] = (cot + r * (d - one - xh * two)).astype(LOW)

    for t in range(span // SUB):
        project(t)
        for i in range(SUB // 16):
            first(t * SUB // 16 + i)


def call(kernel, steps, ins, outs, scratch, flops, vmem, args, aliases={}):
    return pl.pallas_call(
        kernel,
        grid=(steps,),
        in_specs=ins,
        out_specs=[spec for spec, _ in outs],
        out_shape=[shape for _, shape in outs],
        scratch_shapes=scratch,
        cost_estimate=pl.CostEstimate(flops=flops, bytes_accessed=24 << 20, transcendentals=0),
        compiler_params=pltpu.CompilerParams(vmem_limit_bytes=vmem << 20),
        input_output_aliases=aliases,
    )(*args)


def whole(*shape):
    return pl.BlockSpec(shape, lambda i: (0,) * len(shape), pipeline_mode=pl.Buffered(1))


def held(*shape):
    return pl.BlockSpec(shape, lambda i: (0,) * len(shape))


def halo(cells, width):
    count = lax.axis_size("seq")
    head = cells[..., :width]
    tail = cells[..., cells.shape[-1] - width :]
    ends = count - 1
    left = lax.ppermute(tail, "seq", [(i, (i + 1) % count) for i in range(ends)])
    right = lax.ppermute(head, "seq", [((i + 1) % count, i) for i in range(ends)])
    return left, cells, right


def local(
    inputs,
    starts,
    types,
    norm_gain_in,
    norm_bias_in,
    proj_down,
    proj_down_bias,
    norm_gain_mid,
    norm_bias_mid,
    conv_weight,
    conv_bias,
    norm_gain_out,
    norm_bias_out,
    proj_up,
    proj_up_bias,
    cotangent,
):
    groups, span, width = inputs.shape
    taps, inner, _ = conv_weight.shape
    reach = taps // 2 * DILATION_STEP
    row_length = span * lax.axis_size("seq")
    first = lax.axis_index("seq") * span
    places = first - reach + jnp.arange(span + 2 * reach, dtype=jnp.int32)
    protein = jnp.sum((starts[:, None, :] <= places[None, :, None]).astype(jnp.int32), axis=2)
    inside = (places >= 0) & (places < row_length)
    centre = protein[:, reach : reach + span]
    masks = []
    for k in range(taps):
        window = slice(k * DILATION_STEP, k * DILATION_STEP + span)
        masks.append((protein[:, window] == centre) & inside[None, window])
    full = functools.reduce(jnp.logical_and, masks)
    kinds = types[:, :, None] == jnp.arange(TYPES, dtype=jnp.int32)[None, None, :]
    tally = jnp.sum((kinds & full[:, :, None]).astype(WIDE), axis=(0, 1))
    mask = jnp.stack([masks[k] for k in range(taps) if k != taps // 2]).astype(LOW)
    mask = jnp.broadcast_to(mask.reshape(taps - 1, 1, groups * span), (taps - 1, 16, groups * span))

    x = inputs.reshape(groups * span, width)
    e = cotangent.reshape(groups * span, width)

    parts = 2 if groups % 2 == 0 else 1
    per = groups // parts
    shape = jax.ShapeDtypeStruct

    def rows_of(part, size):
        return pl.BlockSpec((span, size), lambda i: (i + part * per, 0))

    def own_rows(size, kind=LOW):
        return pl.BlockSpec((span, size), lambda i: (i, 0)), shape((per * span, size), kind)

    def all_rows(part, size, kind=LOW):
        return rows_of(part, size), shape((groups * span, size), kind)

    def turned(size, length=span, kind=LOW):
        return pl.BlockSpec((None, size, length), lambda i: (i, 0, 0)), shape((per, size, length), kind)

    def mask_of(part):
        return pl.BlockSpec((taps - 1, 16, span), lambda i: (0, 0, i + part * per))

    def sums(*dims):
        return held(*dims), shape(dims, WIDE)

    flops = 2 * per * span * inner * width
    anywhere = pl.BlockSpec(memory_space=pl.ANY)
    entered = []
    down_t = mid = ahead = None
    for part in range(parts):
        begun = part > 0
        done = call(
            functools.partial(enter_kernel, begun, per),
            per,
            [rows_of(part, width)] * 2
            + [whole(width)] * 2
            + [whole(inner, width)]
            + (
                [whole(inner, width), whole(3, inner, LANES)]
                if begun
                else [whole(width, inner), whole(taps, inner, inner)] + [whole(inner)] * 3
            ),
            [own_rows(width)] * 3
            + [own_rows(LANES, WIDE)]
            + [turned(inner)] * 3
            + [turned(8, kind=WIDE), turned(inner, kind=WIDE)]
            + (
                []
                if begun
                else [
                    (held(inner, width), shape((inner, width), LOW)),
                    sums(3, inner, LANES),
                    (held(inner, taps * inner), shape((inner, taps * inner), LOW)),
                ]
            ),
            [pltpu.VMEM((inner, span), WIDE)],
            3 * flops,
            48,
            (x, e, norm_gain_in, norm_bias_in, proj_up)
            + (
                (down_t, mid)
                if begun
                else (proj_down, conv_weight, proj_down_bias, norm_gain_mid, norm_bias_mid)
            ),
        )
        if not begun:
            down_t, mid, ahead = done[9:]
        entered.append(done[:9])
    z_rows = [halo(item[4], reach) for item in entered]

    grads_y, vec_out = [], []
    output = grad_up = None
    for part in range(parts):
        begun = part > 0
        output, grad_y, grad_up, vec = call(
            functools.partial(turn_kernel, begun),
            per,
            [turned(inner, reach)[0], turned(inner)[0], turned(inner, reach)[0], mask_of(part)]
            + [whole(inner, taps * inner), turned(inner)[0]]
            + [rows_of(part, width)] * 2
            + [whole(inner, width), whole(width)]
            + [whole(inner)] * 3
            + [anywhere, whole(inner, width)] * begun,
            [all_rows(part, width), turned(inner), sums(inner, width), sums(3, inner, LANES)],
            [
                pltpu.VMEM((taps * inner, span), LOW),
                pltpu.VMEM((inner, span), LOW),
                pltpu.VMEM((inner, span), WIDE),
                pltpu.VMEM((inner, span), WIDE),
                pltpu.VMEM((3, inner, LANES), WIDE),
            ],
            5 * flops,
            48,
            (*z_rows[part], mask, ahead, entered[part][8], x, e, proj_up, proj_up_bias)
            + (conv_bias, norm_gain_out, norm_bias_out)
            + (output, grad_up) * begun,
            {13: 0} if begun else {},
        )
        grads_y.append(grad_y)
        vec_out.append(vec)
    y_rows = [halo(item, reach) for item in grads_y]

    def clamped(part, size, length):
        def place(i):
            return (jnp.clip(i - part * per, 0, per - 1), 0, 0)

        return pl.BlockSpec((None, size, length), place)

    grad_conv = call(
        functools.partial(taps_kernel, parts),
        groups,
        [
            spec
            for part in range(parts)
            for spec in (
                clamped(part, inner, reach),
                clamped(part, inner, span),
                clamped(part, inner, reach),
                mask_of(0),
                clamped(part, inner, span),
            )
        ],
        [sums(taps, inner, inner)],
        [pltpu.VMEM((taps, inner, inner), WIDE), pltpu.VMEM((taps * inner, span), LOW)],
        5 * flops,
        48,
        [item for part in range(parts) for item in (*z_rows[part], mask, grads_y[part])],
    )[0]

    grads_h, vec_mid = [], []
    grad_down = None
    for part in range(parts):
        begun = part > 0
        done = call(
            functools.partial(inner_kernel, begun),
            per,
            [turned(inner, reach)[0], turned(inner)[0], turned(inner, reach)[0], mask_of(part)]
            + [whole(taps, inner, inner), turned(inner)[0], turned(inner)[0], turned(8)[0]]
            + [whole(3, inner, LANES), own_rows(width)[0]]
            + [whole(inner, width)] * begun,
            [turned(inner), sums(inner, width), sums(3, inner, LANES)],
            [
                pltpu.VMEM((inner, taps * inner), LOW),
                pltpu.VMEM((taps * inner, span), LOW),
                pltpu.VMEM((inner, span), WIDE),
            ],
            4 * flops,
            48,
            (*y_rows[part], mask, conv_weight, entered[part][5], entered[part][6], entered[part][7])
            + (mid, entered[part][0])
            + (grad_down,) * begun,
        )
        grads_h.append(done[0])
        grad_down = done[1]
        vec_mid.append(done[2])

    vec_in = []
    input_grad = None
    for part in range(parts):
        begun = part > 0
        input_grad, vec = call(
            leave_kernel,
            per,
            [turned(inner)[0], whole(inner, width), own_rows(width)[0], own_rows(width)[0]]
            + [own_rows(LANES)[0], whole(width), rows_of(part, width)]
            + [anywhere] * begun,
            [all_rows(part, width), sums(3, 8, width)],
            [pltpu.VMEM((span, width), WIDE)],
            2 * flops,
            32,
            (grads_h[part], down_t, entered[part][1], entered[part][2], entered[part][3], norm_gain_in, e)
            + (input_grad,) * begun,
            {7: 0} if begun else {},
        )
        vec_in.append(vec)

    plan = exchange_plan()
    total_up = sum_everywhere(grad_up, plan)
    total_conv = sum_everywhere(grad_conv.reshape(-1, inner), plan).reshape(taps, inner, inner)
    total_down = sum_everywhere(grad_down, plan).T
    small_in = sum(vec_in).sum(1)
    small_mid = sum(vec_mid).sum(2)
    small_out = sum(vec_out).sum(2)
    vectors = [small_in[1], small_in[0], small_mid[2], small_mid[1], small_mid[0]]
    vectors += [small_out[2], small_out[1], small_out[0], small_in[2], tally]
    ends = [0]
    for item in vectors:
        ends.append(ends[-1] + item.shape[0])
    flat = jnp.concatenate(vectors)
    flat = jnp.pad(flat, (0, -flat.shape[0] % 1024)).reshape(-1, LANES)
    flat = sum_small(flat, plan).reshape(-1)
    totals = [flat[begin:end] for begin, end in zip(ends, ends[1:])]
    return (
        output.reshape(inputs.shape),
        input_grad.reshape(inputs.shape),
        totals[0],
        totals[1],
        total_down,
        *totals[2:5],
        total_conv,
        *totals[5:8],
        total_up,
        totals[8],
        totals[9].astype(jnp.int32),
    )


def solution(mesh):
    return jax.shard_map(
        local,
        mesh=mesh,
        in_specs=(
            P("rows", "seq", None),
            P("rows", None),
            P("rows", "seq"),
            P(),
            P(),
            P(),
            P(),
            P(),
            P(),
            P(),
            P(),
            P(),
            P(),
            P(),
            P(),
            P("rows", "seq", None),
        ),
        out_specs=(
            P("rows", "seq", None),
            P("rows", "seq", None),
            P(),
            P(),
            P(),
            P(),
            P(),
            P(),
            P(),
            P(),
            P(),
            P(),
            P(),
            P(),
            P(),
        ),
        check_vma=False,
    )
```

```python
import functools

import jax
import jax.numpy as jnp
from jax import lax
from jax.experimental import pallas as pl
from jax.experimental.pallas import tpu as pltpu
from jax.sharding import PartitionSpec as P

DILATION_STEP = 128
TYPES = 30
LANES = 128
SUB = 256
VMEM = 60 << 20
LOW = jnp.bfloat16
WIDE = jnp.float32
NN = (((1,), (0,)), ((), ()))
NT = (((1,), (1,)), ((), ()))
TN = (((0,), (0,)), ((), ()))
TT = (((0,), (1,)), ((), ()))


def bits_of(size):
    count = size.bit_length() - 1
    assert size == 1 << count
    return [1 << place for place in range(count)]


def xor_pairs(size, bit):
    return [(i, i ^ bit) for i in range(size)]


def exchange_plan(direct):
    seq, rows = lax.axis_size("seq"), lax.axis_size("rows")
    here, row = lax.axis_index("seq"), lax.axis_index("rows")
    plan = [("seq", [xor_pairs(seq, 1)], here & 1)]
    bits = bits_of(seq)[1:]
    if direct and len(bits) == 2:
        plan.append(("seq", [xor_pairs(seq, 2 * m) for m in range(1, 4)], here >> 1))
    else:
        for first, second in zip(bits, bits[::-1]):
            pairs = [(i, i ^ (second if i & 1 else first)) for i in range(seq)]
            place = jnp.where(here & 1 == 1, (here & second) != 0, (here & first) != 0)
            plan.append(("seq", [pairs], place.astype(jnp.int32)))
    plan.append(("rows", [xor_pairs(rows, m) for m in range(1, rows)], row))
    return plan


def cut(cells, place, count):
    size = cells.shape[0] // count
    return lax.dynamic_slice_in_dim(cells, place * size, size, axis=0)


def sum_steps(sent, own, plan):
    sent = [sent]
    for step, (axis, pairs, _) in enumerate(plan):
        got = yield sent, axis, pairs
        if step == 0:
            (kept,) = own
        terms = [kept, *got]
        if step + 1 < len(plan):
            _, coming, place = plan[step + 1]
            count = len(coming) + 1

            def part(at):
                return sum(cut(term, at, count).astype(WIDE) for term in terms)

            sent = [part(place ^ m).astype(LOW) for m in range(1, count)]
            kept = part(place)
    cells = sum(term.astype(WIDE) for term in terms).astype(LOW)
    for axis, pairs, place in plan[:0:-1]:
        got = yield [cells] * len(pairs), axis, pairs
        pieces = [cells, *got]
        ordered = []
        for j in range(len(pieces)):
            piece = pieces[-1]
            for m in range(len(pieces) - 2, -1, -1):
                piece = jnp.where(place ^ j == m, pieces[m], piece)
            ordered.append(piece)
        cells = jnp.concatenate(ordered, axis=0)
    axis, pairs, _ = plan[0]
    (got,) = yield [cells], axis, pairs
    return cells, got


def small_steps(cells):
    for axis in ("seq", "rows"):
        size = lax.axis_size(axis)
        for bit in bits_of(size):
            (got,) = yield [cells], axis, [xor_pairs(size, bit)]
            cells = cells + got
    return cells


class Sums:
    def __init__(self):
        self.open = {}
        self.done = {}

    def add(self, name, steps):
        self.open[name] = (steps, next(steps))

    def turn(self, names, work=None, gate=(), own=None):
        names = [name for name in names if name in self.open]
        sent = [self.open[name][1][0] for name in names]
        sent, gate = lax.optimization_barrier((sent, gate))
        got = []
        for name, cells in zip(names, sent):
            _, axis, pairs = self.open[name][1]
            got.append([lax.ppermute(cell, axis, pair) for cell, pair in zip(cells, pairs)])
        made = work(*gate) if work else ()
        got, made = lax.optimization_barrier((got, made))
        if own is not None:
            own.extend(made)
        for name, cells in zip(names, got):
            steps = self.open.pop(name)[0]
            try:
                self.open[name] = (steps, steps.send(cells))
            except StopIteration as end:
                self.done[name] = end.value
        return made


def dot(left, right, dims):
    return lax.dot_general(left, right, dims, preferred_element_type=WIDE)


def gelu_parts(u):
    phi = 0.5 + 0.5 * lax.erf(u * 0.7071067811865476)
    bell = jnp.exp2(u * u * -0.7213475204444817)
    return u * phi, phi + (u * 0.3989422804014327) * bell


def fold(values):
    return jnp.sum(values.reshape(-1, 8, values.shape[-1]), axis=0)


def column_mean(rows, count):
    total = jnp.zeros((8, LANES), WIDE)
    for i in range(count // 64):
        total = total + fold(rows(i))
    return jnp.sum(total, axis=0, keepdims=True) * (1.0 / count)


def column(vector):
    size = vector.shape[0]
    return jnp.broadcast_to(vector[...].reshape(1, size), (LANES, size)).T


def enter_kernel(*refs):
    x, e, odd, gain, bias, up, down, down_bias, gain_mid, bias_mid = refs[:10]
    a1, s1, xh1, r1, s2, xh2, r2, ga3, z_one, z_two, h, z, mid = refs[-13:]
    span, width = x.shape
    inner = h.shape[0]
    gain_row, bias_row = gain[...].reshape(1, width), bias[...].reshape(1, width)

    @pl.when(pl.program_id(0) == 0)
    def _():
        mid[0] = column(down_bias)
        mid[1] = column(gain_mid)
        mid[2] = column(bias_mid)

    def first(i):
        rows = pl.ds(i * 16, 16)
        v = x[rows, :].astype(WIDE)
        v = v - jnp.sum(v, axis=-1, keepdims=True) * (1.0 / width)
        r = lax.rsqrt(jnp.sum(v * v, axis=-1, keepdims=True) * (1.0 / width) + 1e-05)
        xh = v * r
        act, slope = gelu_parts(xh * gain_row + bias_row)
        a1[rows, :] = act.astype(LOW)
        s1[rows, :] = slope.astype(LOW)
        xh1[rows, :] = xh.astype(LOW)
        r1[rows, :] = jnp.broadcast_to(r, (16, LANES))

    def project(t):
        cols = pl.ds(t * SUB, SUB)
        product = dot(down[...], a1[cols, :], TT)
        for j in range(SUB // LANES):
            h[:, pl.ds(t * SUB + j * LANES, LANES)] = product[:, j * LANES : (j + 1) * LANES] + mid[0]
        ga3[:, cols] = dot(up[...], e[cols, :], NT)

    def second(j):
        cols = pl.ds(j * LANES, LANES)
        m = column_mean(lambda i: h[pl.ds(i * 64, 64), cols], inner)

        def squares(i):
            c = h[pl.ds(i * 64, 64), cols] - m
            return c * c

        r = lax.rsqrt(column_mean(squares, inner) + 1e-05)
        for i in range(inner // 32):
            rows = pl.ds(i * 32, 32)
            xh = (h[rows, cols] - m) * r
            act, slope = gelu_parts(xh * mid[1, rows, :] + mid[2, rows, :])
            z[rows, cols] = act.astype(LOW)
            s2[rows, cols] = slope.astype(LOW)
            xh2[rows, cols] = xh.astype(LOW)
        r2[:, cols] = jnp.broadcast_to(r, (8, LANES))

    for t in range(span // SUB):
        for i in range(SUB // 16):
            first(t * SUB // 16 + i)
        project(t)
        if t:
            for j in range(SUB // LANES):
                second((t - 1) * SUB // LANES + j)
    for j in range(SUB // LANES):
        second((span // SUB - 1) * SUB // LANES + j)
    part_ends(z, odd[0], z_one, z_two)


def at(place, size):
    return pl.ds(pl.multiple_of(place, LANES), size)


def part_ends(cells, odd, one, two):
    half = one.shape[1]
    one[...] = cells[:, at((1 - odd) * half, half)]
    two[...] = cells[:, at(odd * half, half)]


def join_ends(one, two, odd, out, begin):
    half = one.shape[1]
    out[:, at(begin + (1 - odd) * half, half)] = one[...]
    out[:, at(begin + odd * half, half)] = two[...]


def extend(one, two, got_one, got_two, odd, out):
    half = one.shape[1]
    join_ends(one, two, odd, out, half)
    out[:, at((1 - odd) * 3 * half, half)] = got_one[...]
    out[:, at(odd * 3 * half, half)] = got_two[...]


def windows(field, mask, out, t):
    inner = field.shape[0]
    cols = pl.ds(t * SUB, SUB)
    taps = mask.shape[0]
    for k in range(taps):
        source = field[:, pl.ds(t * SUB + k * LANES, SUB)]
        if k != taps // 2:
            source = (source.reshape(-1, 16, SUB) * mask[k, :, cols][None]).reshape(inner, SUB)
        out[k * inner : (k + 1) * inner, cols] = source


def turn_kernel(*refs):
    one, two, got_one, got_two, odd, mask, conv, ga3, conv_bias, gain_out, bias_out = refs[:11]
    act3, gy_one, gy_two, vec, field, taps, dy, xh3, out3, gy = refs[-10:]
    inner, span = gy.shape
    extend(one, two, got_one, got_two, odd[0], field)

    @pl.when(pl.program_id(0) == 0)
    def _():
        vec[...] = jnp.zeros_like(vec)
        out3[0] = column(conv_bias)
        out3[1] = column(gain_out)
        out3[2] = column(bias_out)

    def third(j):
        cols = pl.ds(j * LANES, LANES)
        m = column_mean(lambda i: dy[pl.ds(i * 64, 64), cols], inner)

        def squares(i):
            c = dy[pl.ds(i * 64, 64), cols] - m
            return c * c

        r = lax.rsqrt(column_mean(squares, inner) + 1e-05)
        sum_one = jnp.zeros((8, LANES), WIDE)
        sum_two = jnp.zeros((8, LANES), WIDE)
        for i in range(inner // 32):
            rows = pl.ds(i * 32, 32)
            gain = out3[1, rows, :]
            xh = (dy[rows, cols] - m) * r
            act, slope = gelu_parts(xh * gain + out3[2, rows, :])
            act3[rows, cols] = act.astype(LOW)
            d = ga3[rows, cols] * slope
            vec[0, rows, :] += d
            vec[1, rows, :] += d * xh
            d = d * gain
            sum_one = sum_one + fold(d)
            sum_two = sum_two + fold(d * xh)
            dy[rows, cols] = d
            xh3[rows, cols] = xh
        one = jnp.sum(sum_one, axis=0, keepdims=True) * (1.0 / inner)
        two = jnp.sum(sum_two, axis=0, keepdims=True) * (1.0 / inner)
        for i in range(inner // 32):
            rows = pl.ds(i * 32, 32)
            low = (r * (dy[rows, cols] - one - xh3[rows, cols] * two)).astype(LOW)
            gy[rows, cols] = low
            vec[2, rows, :] += low.astype(WIDE)

    def convolve(t):
        windows(field, mask, taps, t)
        cols = pl.ds(t * SUB, SUB)
        product = dot(conv[...], taps[:, cols], TN)
        for j in range(SUB // LANES):
            dy[:, pl.ds(t * SUB + j * LANES, LANES)] = product[:, j * LANES : (j + 1) * LANES] + out3[0]

    for t in range(span // SUB):
        convolve(t)
        for j in range(SUB // LANES):
            third(t * SUB // LANES + j)
    part_ends(gy, odd[0], gy_one, gy_two)


def by_part(parts, refs, body):
    step = pl.program_id(0)
    per = pl.num_programs(0) // parts
    count = len(refs) // parts
    for part in range(parts):

        @pl.when((step >= part * per) & (step < (part + 1) * per))
        def _():
            body(*refs[part * count : (part + 1) * count])


def hand_over(total, side, sent, kept):
    half = kept.shape[0]
    sent[...] = total[pl.ds(pl.multiple_of((1 - side) * half, half), half), :].astype(LOW)
    kept[...] = total[pl.ds(pl.multiple_of(side * half, half), half), :].astype(kept.dtype)


def up_kernel(begin, act3, e, side, _, sent, kept, total, low_one, low_two, sem):
    half, width = total.shape[0] // 2, low_one.shape[1]

    @pl.when(pl.program_id(0) == 0)
    def _():
        total[...] = jnp.zeros_like(total)

    total[...] += dot(act3[...], e[...], NN)

    @pl.when(pl.program_id(0) == pl.num_programs(0) - 1)
    def _():
        mine = side[0]
        for j in range(total.shape[1] // width):
            cols = pl.ds(j * width, width)
            rows = pl.ds(j * half, half)
            low_one[rows, :] = total[pl.ds(pl.multiple_of((1 - mine) * half, half), half), cols].astype(LOW)
            low_two[rows, :] = total[pl.ds(pl.multiple_of(mine * half, half), half), cols].astype(LOW)
        place = pl.ds(begin, low_one.shape[0])
        first = pltpu.make_async_copy(low_one, sent.at[place], sem.at[0])
        second = pltpu.make_async_copy(low_two, kept.at[place], sem.at[1])
        first.start()
        second.start()
        first.wait()
        second.wait()


def output_kernel(act3, x, up, up_bias, y):
    span, width = x.shape
    for t in range(span // SUB):
        rows = pl.ds(t * SUB, SUB)
        product = dot(act3[:, rows], up[...], TN)
        y[rows, :] = (x[rows, :].astype(WIDE) + product + up_bias[...].reshape(1, width)).astype(LOW)


def taps_kernel(parts, *refs):
    mask, odd, which = refs[6 * parts : 6 * parts + 3]
    out, total, field, gy, taps = refs[-5:]
    inner, span = gy.shape
    half = inner // 2
    count = mask.shape[0] // 2
    h = which[0]

    @pl.when(pl.program_id(0) == 0)
    def _():
        total[...] = jnp.zeros_like(total)

    def place(rows, source, tap):
        cells = field[source, at(tap * LANES, span)]
        size = cells.shape[0]
        taps[rows, :] = (cells.reshape(-1, 16, span) * mask[tap][None]).reshape(size, span)

    def body(one, two, got_one, got_two, gy_one, gy_two):
        extend(one, two, got_one, got_two, odd[0], field)
        join_ends(gy_one, gy_two, odd[0], gy, 0)

    by_part(parts, refs[: 6 * parts], body)
    for j in range(count):
        rows = pl.ds(pl.multiple_of(h * half + j * inner, 16), inner)
        place(rows, slice(None), h * (count + 1) + j)
    rows = pl.ds(pl.multiple_of((1 - h) * count * inner, 16), half)
    place(rows, pl.ds(pl.multiple_of(h * half, 16), half), jnp.int32(count))
    total[...] += dot(taps[...], gy[...], NT)

    @pl.when(pl.program_id(0) == pl.num_programs(0) - 1)
    def _():
        out[...] = total[...].astype(out.dtype)


def inner_kernel(parts, *refs):
    odd, side, mask, straight, s2, xh2, r2, gain_mid, a1 = refs[4 * parts : 4 * parts + 9]
    gh, sent, kept, vec, grad_down, field, conv, taps, gz, gain = refs[-10:]
    inner, span = gh.shape

    @pl.when(pl.program_id(0) == 0)
    def _():
        grad_down[...] = jnp.zeros_like(grad_down)
        vec[...] = jnp.zeros_like(vec)
        gain[...] = column(gain_mid)
        count = straight.shape[0]
        for k in range(count):
            conv[:, k * inner : (k + 1) * inner] = straight[count - 1 - k]

    def body(one, two, got_one, got_two):
        extend(one, two, got_one, got_two, odd[0], field)

    by_part(parts, refs[: 4 * parts], body)

    def convolve(t):
        windows(field, mask, taps, t)
        cols = pl.ds(t * SUB, SUB)
        gz[:, cols] = dot(conv[...], taps[:, cols], NN)

    def second(j):
        cols = pl.ds(j * LANES, LANES)
        sum_one = jnp.zeros((8, LANES), WIDE)
        sum_two = jnp.zeros((8, LANES), WIDE)
        for i in range(inner // 32):
            rows = pl.ds(i * 32, 32)
            xh = xh2[rows, cols].astype(WIDE)
            d = gz[rows, cols] * s2[rows, cols].astype(WIDE)
            vec[0, rows, :] += d
            vec[1, rows, :] += d * xh
            d = d * gain[rows, :]
            sum_one = sum_one + fold(d)
            sum_two = sum_two + fold(d * xh)
            gz[rows, cols] = d
        one = jnp.sum(sum_one, axis=0, keepdims=True) * (1.0 / inner)
        two = jnp.sum(sum_two, axis=0, keepdims=True) * (1.0 / inner)
        r = r2[0:1, cols]
        for i in range(inner // 32):
            rows = pl.ds(i * 32, 32)
            low = (r * (gz[rows, cols] - one - xh2[rows, cols].astype(WIDE) * two)).astype(LOW)
            gh[rows, cols] = low
            vec[2, rows, :] += low.astype(WIDE)

    for t in range(span // SUB):
        convolve(t)
        for j in range(SUB // LANES):
            second(t * SUB // LANES + j)
    grad_down[...] += dot(a1[...], gh[...], TT)

    @pl.when(pl.program_id(0) == pl.num_programs(0) - 1)
    def _():
        hand_over(grad_down, side[0], sent, kept)


def leave_kernel(gh, down, s1, xh1, r1, gain, e, gx, vec, ga):
    span, width = e.shape
    gain_row = gain[...].reshape(1, width)

    @pl.when(pl.program_id(0) == 0)
    def _():
        vec[...] = jnp.zeros_like(vec)

    def project(t):
        rows = pl.ds(t * SUB, SUB)
        ga[rows, :] = dot(gh[:, rows], down[...], TT)

    def first(i):
        rows = pl.ds(i * 16, 16)
        xh = xh1[rows, :].astype(WIDE)
        d = ga[rows, :] * s1[rows, :].astype(WIDE)
        vec[0] += fold(d)
        vec[1] += fold(d * xh)
        d = d * gain_row
        one = jnp.sum(d, axis=-1, keepdims=True) * (1.0 / width)
        two = jnp.sum(d * xh, axis=-1, keepdims=True) * (1.0 / width)
        r = r1[rows, 0:1]
        cot = e[rows, :].astype(WIDE)
        vec[2] += fold(cot)
        gx[rows, :] = (cot + r * (d - one - xh * two)).astype(LOW)

    for t in range(span // SUB):
        project(t)
        for i in range(SUB // 16):
            first(t * SUB // 16 + i)


def join_kernel(side, *refs):
    refs[-1][...] = refs[1][...].astype(WIDE) if len(refs) > 2 else refs[0][...].astype(WIDE)


def join(cells, side, size, begin, deep, wide, before=None):
    width = cells.shape[1]

    def place(i, side):
        return (side[0] * deep + i % deep, i // deep)

    late = before is not None
    return pl.pallas_call(
        join_kernel,
        grid_spec=pltpu.PrefetchScalarGridSpec(
            num_scalar_prefetch=1,
            grid=(deep * wide,),
            in_specs=[pl.BlockSpec(memory_space=pl.ANY)] * late
            + [pl.BlockSpec((size, width), lambda i, side: (begin + i, 0))],
            out_specs=pl.BlockSpec((size, width), place),
        ),
        out_shape=jax.ShapeDtypeStruct((2 * deep * size, wide * width), WIDE),
        input_output_aliases={1: 0} if late else {},
    )(side, *([before] if late else []), cells)


def call(kernel, steps, ins, outs, scratch, flops, args, aliases={}):
    return pl.pallas_call(
        kernel,
        grid=(steps,),
        in_specs=ins,
        out_specs=[spec for spec, _ in outs],
        out_shape=[shape for _, shape in outs],
        scratch_shapes=scratch,
        cost_estimate=pl.CostEstimate(flops=flops, bytes_accessed=24 << 20, transcendentals=0),
        compiler_params=pltpu.CompilerParams(vmem_limit_bytes=VMEM),
        input_output_aliases=aliases,
    )(*args)


def whole(*shape):
    return pl.BlockSpec(shape, lambda i: (0,) * len(shape), pipeline_mode=pl.Buffered(1))


def held(*shape):
    return pl.BlockSpec(shape, lambda i: (0,) * len(shape))


def swap_ends(one, two):
    count = lax.axis_size("seq")
    pairs = [(i, i ^ 1) for i in range(count)]
    other = [(i, ((i + 1) ^ 1) - 1) for i in range(1, count - 1)]
    return one, two, lax.ppermute(one, "seq", pairs), lax.ppermute(two, "seq", other)


def local(
    inputs,
    starts,
    types,
    norm_gain_in,
    norm_bias_in,
    proj_down,
    proj_down_bias,
    norm_gain_mid,
    norm_bias_mid,
    conv_weight,
    conv_bias,
    norm_gain_out,
    norm_bias_out,
    proj_up,
    proj_up_bias,
    cotangent,
):
    groups, span, width = inputs.shape
    taps, inner, _ = conv_weight.shape
    reach = taps // 2 * DILATION_STEP
    row_length = span * lax.axis_size("seq")
    first = lax.axis_index("seq") * span
    places = first - reach + jnp.arange(span + 2 * reach, dtype=jnp.int32)
    protein = jnp.sum((starts[:, None, :] <= places[None, :, None]).astype(jnp.int32), axis=2)
    inside = (places >= 0) & (places < row_length)
    centre = protein[:, reach : reach + span]
    masks = []
    for k in range(taps):
        window = slice(k * DILATION_STEP, k * DILATION_STEP + span)
        masks.append((protein[:, window] == centre) & inside[None, window])
    full = functools.reduce(jnp.logical_and, masks)
    kinds = types[:, :, None] == jnp.arange(TYPES, dtype=jnp.int32)[None, None, :]
    tally = jnp.sum((kinds & full[:, :, None]).astype(WIDE), axis=(0, 1))
    mask = jnp.stack(masks).astype(LOW).reshape(taps, 1, groups * span)
    mask = jnp.broadcast_to(mask, (taps, 16, groups * span))

    x = inputs.reshape(groups * span, width)
    e = cotangent.reshape(groups * span, width)

    parts = 2 if groups % 2 == 0 else 1
    per = groups // parts
    shape = jax.ShapeDtypeStruct

    def rows_of(size, part=0):
        return pl.BlockSpec((span, size), lambda i: (i + part * per, 0))

    def turned(size, part=0):
        return pl.BlockSpec((None, size, span), lambda i: (i + part * per, 0, 0))

    def mask_of(part=0):
        return pl.BlockSpec((taps, 16, span), lambda i: (0, 0, i + part * per))

    def clamped(part):
        def place(i):
            return (jnp.clip(i - part * per, 0, per - 1), 0, 0)

        return pl.BlockSpec((None, inner, reach), place)

    def all_rows(size, kind=LOW, part=0):
        return rows_of(size, part), shape((groups * span, size), kind)

    def all_turned(size, kind=LOW, part=0):
        return turned(size, part), shape((groups, size, span), kind)

    def sums(*dims):
        return held(*dims), shape(dims, WIDE)

    anywhere = pl.BlockSpec(memory_space=pl.ANY)
    scalar = pl.BlockSpec(memory_space=pltpu.SMEM)
    odd = (lax.axis_index("seq") & 1).reshape(1)
    core = odd
    end = pl.BlockSpec((None, inner, reach), lambda i: (i, 0, 0))
    ends = [(end, shape((per, inner, reach), LOW))] * 2
    field = pltpu.VMEM((inner, span + 2 * reach), LOW)
    block = pltpu.VMEM((inner, span), LOW)
    wide_block = pltpu.VMEM((inner, span), WIDE)
    columns = pltpu.VMEM((3, inner, LANES), WIDE)
    flops = 2 * span * inner * width

    z_rows = []
    entered = []
    for part in range(parts):
        begun = part > 0
        *entered, one, two = call(
            enter_kernel,
            per,
            [rows_of(width, part)] * 2
            + [scalar]
            + [whole(width)] * 2
            + [whole(inner, width), whole(width, inner)]
            + [whole(inner)] * 3
            + [anywhere] * len(entered),
            [all_rows(width, part=part)] * 3
            + [all_rows(LANES, WIDE, part)]
            + [all_turned(inner, part=part)] * 2
            + [all_turned(8, WIDE, part), all_turned(inner, WIDE, part)]
            + ends,
            [wide_block, block, columns],
            3 * per * flops,
            (x, e, odd, norm_gain_in, norm_bias_in, proj_up, proj_down)
            + (proj_down_bias, norm_gain_mid, norm_bias_mid, *entered),
            {10 + i: i for i in range(8)} if begun else {},
        )
        z_rows, entered, one, two = lax.optimization_barrier((z_rows, entered, one, two))
        z_rows.append(swap_ends(one, two))
    a1, s1, xh1, r1, s2, xh2, r2, ga3 = entered

    y_ends, y_rows, vec_out = [], [], []
    conv = conv_weight.reshape(taps * inner, inner)
    act3 = None
    for part in range(parts):
        begun = part > 0
        act3, one, two, vec = call(
            turn_kernel,
            per,
            [end] * 4
            + [scalar, mask_of(part)]
            + [whole(taps * inner, inner), turned(inner, part)]
            + [whole(inner)] * 3
            + [anywhere] * begun,
            [all_turned(inner, part=part)] + ends + [sums(3, inner, LANES)],
            [field, pltpu.VMEM((taps * inner, span), LOW), wide_block, wide_block, columns, block],
            3 * per * flops,
            (*z_rows[part], odd, mask, conv, ga3, conv_bias, norm_gain_out, norm_bias_out) + (act3,) * begun,
            {11: 0} if begun else {},
        )
        y_rows, act3, one, two = lax.optimization_barrier((y_rows, act3, one, two))
        y_rows.append(swap_ends(one, two))
        y_ends.append((one, two))
        vec_out.append(vec)

    half = taps * inner // 2
    extra = inner // 2 * (width // inner)
    rows_main = -(-(half + extra) // 256) * 256

    def grad_taps(which):
        def work(y_parts, buffers=()):
            return call(
                functools.partial(taps_kernel, parts),
                groups,
                [clamped(part) for part in range(parts) for _ in range(6)]
                + [mask_of(), scalar, scalar]
                + [anywhere] * len(buffers),
                [(held(half, inner), shape((rows_main, inner), LOW))],
                [pltpu.VMEM((half, inner), WIDE), field, block, pltpu.VMEM((half, span), LOW)],
                5 * groups * flops // 4,
                [item for part in range(parts) for item in (*z_rows[part], *y_parts[2 * part : 2 * part + 2])]
                + [mask, odd, which, *buffers],
                {6 * parts + 3: 0} if buffers else {},
            )

        return work

    def grad_project(sent):
        return call(
            functools.partial(up_kernel, half),
            groups,
            [turned(inner), rows_of(width), scalar, anywhere],
            [(anywhere, shape((rows_main, inner), LOW))] * 2,
            [pltpu.VMEM((inner, width), WIDE)]
            + [pltpu.VMEM((extra, inner), LOW)] * 2
            + [pltpu.SemaphoreType.DMA((2,))],
            groups * flops,
            (act3, e, core, sent),
            {3: 0},
        )

    def back(rows):
        return call(
            functools.partial(inner_kernel, parts),
            groups,
            [clamped(part) for part in range(parts) for _ in range(4)]
            + [scalar, scalar, mask_of()]
            + [whole(taps, inner, inner), turned(inner), turned(inner), turned(8)]
            + [whole(inner), rows_of(width)],
            [all_turned(inner)]
            + [(held(width // 2, inner), shape((width // 2, inner), LOW))] * 2
            + [sums(3, inner, LANES)],
            [pltpu.VMEM((width, inner), WIDE), field, pltpu.VMEM((inner, taps * inner), LOW)]
            + [pltpu.VMEM((taps * inner, span), LOW), wide_block, pltpu.VMEM((inner, LANES), WIDE)],
            4 * groups * flops,
            (*[item for row in rows for item in row], odd, core, mask, conv_weight, s2, xh2, r2)
            + (norm_gain_mid, a1),
        )

    def leave(grad_h):
        return call(
            leave_kernel,
            groups,
            [turned(inner), whole(width, inner), rows_of(width), rows_of(width)]
            + [rows_of(LANES), whole(width), rows_of(width)],
            [all_rows(width), sums(3, 8, width)],
            [pltpu.VMEM((span, width), WIDE)],
            groups * flops,
            (grad_h, proj_down, s1, xh1, r1, norm_gain_in, e),
        )

    def project(act3):
        return call(
            output_kernel,
            groups,
            [turned(inner), rows_of(width), whole(inner, width), whole(width)],
            [all_rows(width)],
            [],
            groups * flops,
            (act3, x, proj_up, proj_up_bias),
        )

    under_way = Sums()
    y_flat = [item for pair in y_ends for item in pair]
    (sent,) = grad_taps(1 - core)(y_flat)
    y_flat, y_rows[-1], sent = lax.optimization_barrier((y_flat, y_rows[-1], sent))
    sent, kept = grad_project(sent)
    own = []
    under_way.add("main", sum_steps(sent, own, exchange_plan(False)))
    under_way.turn(["main"], grad_taps(core), (y_flat, [kept]), own)
    grad_h, sent, kept, vec_mid = under_way.turn(["main"], back, (y_rows,))
    under_way.add("down", sum_steps(sent, [kept], exchange_plan(True)))
    input_grad, vec_in = under_way.turn(["main", "down"], leave, (grad_h,))

    small_in = vec_in.sum(1)
    small_mid = vec_mid.sum(2)
    small_out = sum(vec_out).sum(2)
    vectors = [small_in[1], small_in[0], small_mid[2], small_mid[1], small_mid[0]]
    vectors += [small_out[2], small_out[1], small_out[0], small_in[2], tally]
    ends = [0]
    for item in vectors:
        ends.append(ends[-1] + item.shape[0])
    flat = jnp.concatenate(vectors)
    flat = jnp.pad(flat, (0, -flat.shape[0] % 1024)).reshape(-1, LANES)
    under_way.add("small", small_steps(flat))
    names = ["main", "down", "small"]
    (output,) = under_way.turn(names, project, (act3,))
    while under_way.open:
        under_way.turn(names)

    def widen(cells, size, begin, deep, wide):
        own, got = cells
        return join(got, 1 - core, size, begin, deep, wide, join(own, core, size, begin, deep, wide))

    main = under_way.done["main"]
    total_conv = widen(main, inner * 5 // 4, 0, 2, 1).reshape(taps, inner, inner)
    total_up = widen(main, inner // 2, half * 2 // inner, 1, width // inner)
    total_down = widen(under_way.done["down"], width // 4, 0, 2, 1)
    flat = under_way.done["small"].reshape(-1)
    totals = [flat[begin:end] for begin, end in zip(ends, ends[1:])]
    return (
        output.reshape(inputs.shape),
        input_grad.reshape(inputs.shape),
        totals[0],
        totals[1],
        total_down,
        *totals[2:5],
        total_conv,
        *totals[5:8],
        total_up,
        totals[8],
        totals[9].astype(jnp.int32),
    )


def solution(mesh):
    return jax.shard_map(
        local,
        mesh=mesh,
        in_specs=(
            P("rows", "seq", None),
            P("rows", None),
            P("rows", "seq"),
            P(),
            P(),
            P(),
            P(),
            P(),
            P(),
            P(),
            P(),
            P(),
            P(),
            P(),
            P(),
            P("rows", "seq", None),
        ),
        out_specs=(
            P("rows", "seq", None),
            P("rows", "seq", None),
            P(),
            P(),
            P(),
            P(),
            P(),
            P(),
            P(),
            P(),
            P(),
            P(),
            P(),
            P(),
            P(),
        ),
        check_vma=False,
    )
```

```python
import functools

import jax
import jax.numpy as jnp
from jax import lax
from jax.experimental import pallas as pl
from jax.experimental.pallas import tpu as pltpu
from jax.sharding import PartitionSpec as P

DILATION_STEP = 128
TYPES = 30
LANES = 128
SUB = 256
VMEM = 60 << 20
LOW = jnp.bfloat16
WIDE = jnp.float32
NN = (((1,), (0,)), ((), ()))
NT = (((1,), (1,)), ((), ()))
TN = (((0,), (0,)), ((), ()))
TT = (((0,), (1,)), ((), ()))


def bits_of(size):
    count = size.bit_length() - 1
    assert size == 1 << count
    return [1 << place for place in range(count)]


def xor_pairs(size, bit):
    return [(i, i ^ bit) for i in range(size)]


def exchange_plan(direct):
    seq, rows = lax.axis_size("seq"), lax.axis_size("rows")
    here, row = lax.axis_index("seq"), lax.axis_index("rows")
    plan = [("seq", [xor_pairs(seq, 1)], here & 1)]
    bits = bits_of(seq)[1:]
    if direct and len(bits) == 2:
        plan.append(("seq", [xor_pairs(seq, 2 * m) for m in range(1, 4)], here >> 1))
    else:
        for first, second in zip(bits, bits[::-1]):
            pairs = [(i, i ^ (second if i & 1 else first)) for i in range(seq)]
            place = jnp.where(here & 1 == 1, (here & second) != 0, (here & first) != 0)
            plan.append(("seq", [pairs], place.astype(jnp.int32)))
    plan.append(("rows", [xor_pairs(rows, m) for m in range(1, rows)], row))
    return plan


def cut(cells, place, count):
    size = cells.shape[0] // count
    return lax.dynamic_slice_in_dim(cells, place * size, size, axis=0)


def in_order(pieces, place):
    ordered = []
    for j in range(len(pieces)):
        piece = pieces[-1]
        for m in range(len(pieces) - 2, -1, -1):
            piece = jnp.where(place ^ j == m, pieces[m], piece)
        ordered.append(piece)
    return jnp.concatenate(ordered, axis=0)


def sum_steps(sent, own, plan, early=False):
    sent = [sent]
    for step, (axis, pairs, _) in enumerate(plan):
        got = yield sent, axis, pairs
        if step == 0:
            (kept,) = own
        terms = [kept, *got]
        if step + 1 < len(plan):
            _, coming, place = plan[step + 1]
            count = len(coming) + 1

            def part(at):
                return sum(cut(term, at, count).astype(WIDE) for term in terms)

            sent = [part(place ^ m).astype(LOW) for m in range(1, count)]
            kept = part(place)
    cells = sum(term.astype(WIDE) for term in terms).astype(LOW)
    for axis, pairs, place in plan[:1:-1]:
        got = yield [cells] * len(pairs), axis, pairs
        cells = in_order([cells, *got], place)
    core_axis, (core_pairs,), _ = plan[0]
    axis, pairs, place = plan[1]
    if early:
        first, second = yield [cells, cells], axis, [*pairs, core_pairs]
        own.append((cells, first))
        (third,) = yield [first], core_axis, [core_pairs]
        return second, third
    got = yield [cells] * len(pairs), axis, pairs
    cells = in_order([cells, *got], place)
    own.append(cells)
    (got,) = yield [cells], core_axis, [core_pairs]
    return got


def small_steps(cells, plan):
    for axis, pairs, _ in plan:
        got = yield [cells] * len(pairs), axis, pairs
        terms = [cells, *got]
        while len(terms) > 1:
            terms = [sum(terms[i : i + 2]) for i in range(0, len(terms), 2)]
        (cells,) = terms
    return cells


class Sums:
    def __init__(self):
        self.open = {}
        self.done = {}

    def add(self, name, steps):
        self.open[name] = (steps, next(steps))

    def turn(self, names, work=None, gate=(), own=None):
        names = [name for name in names if name in self.open]
        sent = [self.open[name][1][0] for name in names]
        sent, gate = lax.optimization_barrier((sent, gate))
        got = []
        for name, cells in zip(names, sent):
            _, axis, pairs = self.open[name][1]
            got.append([lax.ppermute(cell, axis, pair) for cell, pair in zip(cells, pairs)])
        made = work(*gate) if work else ()
        got, made = lax.optimization_barrier((got, made))
        if own is not None:
            own.extend(made)
        for name, cells in zip(names, got):
            steps = self.open.pop(name)[0]
            try:
                self.open[name] = (steps, steps.send(cells))
            except StopIteration as end:
                self.done[name] = end.value
        return made


def dot(left, right, dims):
    return lax.dot_general(left, right, dims, preferred_element_type=WIDE)


def gelu_parts(u):
    phi = 0.5 + 0.5 * lax.erf(u * 0.7071067811865476)
    bell = jnp.exp2(u * u * -0.7213475204444817)
    return u * phi, phi + (u * 0.3989422804014327) * bell


def fold(values):
    return jnp.sum(values.reshape(-1, 8, values.shape[-1]), axis=0)


def column_mean(rows, count):
    total = jnp.zeros((8, LANES), WIDE)
    for i in range(count // 64):
        total = total + fold(rows(i))
    return jnp.sum(total, axis=0, keepdims=True) * (1.0 / count)


def column(vector):
    size = vector.shape[0]
    return jnp.broadcast_to(vector[...].reshape(1, size), (LANES, size)).T


def enter_kernel(*refs):
    x, e, odd, gain, bias, up, down, down_bias, gain_mid, bias_mid = refs[:10]
    a1, s1, xh1, r1, s2, xh2, r2, ga3, z_one, z_two, h, z, mid = refs[-13:]
    span, width = x.shape
    inner = h.shape[0]
    gain_row, bias_row = gain[...].reshape(1, width), bias[...].reshape(1, width)

    @pl.when(pl.program_id(0) == 0)
    def _():
        mid[0] = column(down_bias)
        mid[1] = column(gain_mid)
        mid[2] = column(bias_mid)

    def first(i):
        rows = pl.ds(i * 16, 16)
        v = x[rows, :].astype(WIDE)
        v = v - jnp.sum(v, axis=-1, keepdims=True) * (1.0 / width)
        r = lax.rsqrt(jnp.sum(v * v, axis=-1, keepdims=True) * (1.0 / width) + 1e-05)
        xh = v * r
        act, slope = gelu_parts(xh * gain_row + bias_row)
        a1[rows, :] = act.astype(LOW)
        s1[rows, :] = slope.astype(LOW)
        xh1[rows, :] = xh.astype(LOW)
        r1[rows, :] = jnp.broadcast_to(r, (16, LANES))

    def project(t):
        cols = pl.ds(t * SUB, SUB)
        product = dot(down[...], a1[cols, :], TT)
        for j in range(SUB // LANES):
            h[:, pl.ds(t * SUB + j * LANES, LANES)] = product[:, j * LANES : (j + 1) * LANES] + mid[0]
        ga3[:, cols] = dot(up[...], e[cols, :], NT)

    def second(j):
        cols = pl.ds(j * LANES, LANES)
        m = column_mean(lambda i: h[pl.ds(i * 64, 64), cols], inner)

        def squares(i):
            c = h[pl.ds(i * 64, 64), cols] - m
            return c * c

        r = lax.rsqrt(column_mean(squares, inner) + 1e-05)
        for i in range(inner // 32):
            rows = pl.ds(i * 32, 32)
            xh = (h[rows, cols] - m) * r
            act, slope = gelu_parts(xh * mid[1, rows, :] + mid[2, rows, :])
            z[rows, cols] = act.astype(LOW)
            s2[rows, cols] = slope.astype(LOW)
            xh2[rows, cols] = xh.astype(LOW)
        r2[:, cols] = jnp.broadcast_to(r, (8, LANES))

    for t in range(span // SUB):
        for i in range(SUB // 16):
            first(t * SUB // 16 + i)
        project(t)
        if t:
            for j in range(SUB // LANES):
                second((t - 1) * SUB // LANES + j)
    for j in range(SUB // LANES):
        second((span // SUB - 1) * SUB // LANES + j)
    part_ends(z, odd[0], z_one, z_two)


def at(place, size):
    return pl.ds(pl.multiple_of(place, LANES), size)


def part_ends(cells, odd, one, two):
    half = one.shape[1]
    one[...] = cells[:, at((1 - odd) * half, half)]
    two[...] = cells[:, at(odd * half, half)]


def join_ends(one, two, odd, out, begin):
    half = one.shape[1]
    out[:, at(begin + (1 - odd) * half, half)] = one[...]
    out[:, at(begin + odd * half, half)] = two[...]


def extend(one, two, got_one, got_two, odd, out):
    half = one.shape[1]
    join_ends(one, two, odd, out, half)
    out[:, at((1 - odd) * 3 * half, half)] = got_one[...]
    out[:, at(odd * 3 * half, half)] = got_two[...]


def windows(field, mask, first, out, t):
    inner = field.shape[0]
    taps = mask.shape[0]
    for k in range(taps):
        source = field[:, pl.ds(t * SUB + k * LANES, SUB)]
        if k != taps // 2:
            source = (source.reshape(-1, 16, SUB) * mask[k, :, pl.ds(first, SUB)][None]).reshape(inner, SUB)
        out[k * inner : (k + 1) * inner, :] = source


def lane_sums(vec, out):
    for k in range(vec.shape[0]):
        out[k : k + 1, :] = jnp.sum(vec[k].T, axis=0, keepdims=True)


def in_blocks(count, always, body):
    for i in range(count):

        @pl.when(always)
        def _():
            body(i)


def turn_kernel(begun, *refs):
    sources = refs[:7]
    odd, conv_bias, gain_out, bias_out = refs[7:11]
    refs = refs[11 + begun :]
    act_out, one_out, two_out, vec_out = refs[:4]
    one, two, got_one, got_two, mask, conv, ga3, *refs = refs[4:]
    act3, gy, gy_one, gy_two, vec, out3, sem = refs[:7]
    fields, taps, dys, xhs = refs[7:9], refs[9:11], refs[11:13], refs[13:15]
    part = int(begun)
    rows_here, inner, span = gy.shape
    tiles = span // SUB
    count = rows_here * tiles

    def load(i, source, out):
        return pltpu.make_async_copy(source, out, sem.at[i])

    first_row = part * rows_here
    end_refs = (one, two, got_one, got_two)
    ends = [
        [load(4 * row + i, source.at[row], out.at[row]) for i, (source, out) in enumerate(zip(sources[:4], end_refs))]
        for row in range(rows_here)
    ]
    others = [
        load(4 * rows_here, sources[4].at[:, :, pl.ds(first_row * span, rows_here * span)], mask),
        load(4 * rows_here + 1, sources[5], conv),
        load(4 * rows_here + 2, sources[6].at[pl.ds(first_row, rows_here)], ga3),
    ]
    for copy in [*ends[0], *others[:2]] + [copy for row in ends[1:] for copy in row] + others[2:]:
        copy.start()
    vec[...] = jnp.zeros_like(vec)
    out3[0] = column(conv_bias)
    out3[1] = column(gain_out)
    out3[2] = column(bias_out)
    others[0].wait()

    def lay(n):
        row, t = divmod(n, tiles)
        windows(fields[row % 2], mask, n * SUB, taps[n % 2], t)

    def convolve(n):
        product = dot(conv[...], taps[n % 2][...], TN)
        for j in range(SUB // LANES):
            dys[n % 2][:, pl.ds(j * LANES, LANES)] = product[:, j * LANES : (j + 1) * LANES] + out3[0]

    def third(n, j):
        row, t = divmod(n, tiles)
        dy, xh3 = dys[n % 2], xhs[n % 2]
        cols = pl.ds(j * LANES, LANES)
        place = pl.ds(t * SUB + j * LANES, LANES)
        m = column_mean(lambda i: dy[pl.ds(i * 64, 64), cols], inner)

        def squares(i):
            c = dy[pl.ds(i * 64, 64), cols] - m
            return c * c

        r = lax.rsqrt(column_mean(squares, inner) + 1e-05)
        sum_one = jnp.zeros((8, LANES), WIDE)
        sum_two = jnp.zeros((8, LANES), WIDE)
        for i in range(inner // 32):
            rows = pl.ds(i * 32, 32)
            gain = out3[1, rows, :]
            xh = (dy[rows, cols] - m) * r
            act, slope = gelu_parts(xh * gain + out3[2, rows, :])
            act3[row, rows, place] = act.astype(LOW)
            d = ga3[row, rows, place] * slope
            vec[0, rows, :] += d
            vec[1, rows, :] += d * xh
            d = d * gain
            sum_one = sum_one + fold(d)
            sum_two = sum_two + fold(d * xh)
            dy[rows, cols] = d
            xh3[rows, cols] = xh
        one_mean = jnp.sum(sum_one, axis=0, keepdims=True) * (1.0 / inner)
        two_mean = jnp.sum(sum_two, axis=0, keepdims=True) * (1.0 / inner)
        for i in range(inner // 32):
            rows = pl.ds(i * 32, 32)
            low = (r * (dy[rows, cols] - one_mean - xh3[rows, cols] * two_mean)).astype(LOW)
            gy[row, rows, place] = low
            vec[2, rows, :] += low.astype(WIDE)

    stores = []

    def block(i):
        if i < count:
            lay(i)
        if 2 <= i:
            for j in range(SUB // LANES):
                third(i - 2, j)
        if 1 <= i <= count:
            convolve(i - 1)

    for i in range(count + 2):
        if i < count and i % tiles == 0:
            row = i // tiles
            for copy in ends[row]:
                copy.wait()
            extend(one.at[row], two.at[row], got_one.at[row], got_two.at[row], odd[0], fields[row % 2])
        if i == 1:
            others[1].wait()
        if i == 2:
            others[2].wait()

        @pl.when(odd[0] >= 0)
        def _():
            block(i)

        if i >= 2 and (i - 1) % tiles == 0:
            row = (i - 2) // tiles
            part_ends(gy.at[row], odd[0], gy_one.at[row], gy_two.at[row])
            for k, (source, out) in enumerate(
                ((act3, act_out.at[first_row + row]), (gy_one, one_out.at[row]), (gy_two, two_out.at[row]))
            ):
                stores.append(load(4 * rows_here + 3 + 3 * row + k, source.at[row], out))
                stores[-1].start()
    lane_sums(vec, vec_out)
    for copy in stores:
        copy.wait()


def by_part(parts, refs, body):
    step = pl.program_id(0)
    per = pl.num_programs(0) // parts
    count = len(refs) // parts
    for part in range(parts):

        @pl.when((step >= part * per) & (step < (part + 1) * per))
        def _():
            body(*refs[part * count : (part + 1) * count])


def hand_over(total, side, sent, kept):
    half = kept.shape[0]
    sent[...] = total[pl.ds(pl.multiple_of((1 - side) * half, half), half), :].astype(LOW)
    kept[...] = total[pl.ds(pl.multiple_of(side * half, half), half), :].astype(kept.dtype)


def up_kernel(begin, act3, e, side, _, sent, kept, total, low_one, low_two, sem):
    half, width = total.shape[0] // 2, low_one.shape[1]

    @pl.when(pl.program_id(0) == 0)
    def _():
        total[...] = jnp.zeros_like(total)

    total[...] += dot(act3[...], e[...], NN)

    @pl.when(pl.program_id(0) == pl.num_programs(0) - 1)
    def _():
        mine = side[0]
        for j in range(total.shape[1] // width):
            cols = pl.ds(j * width, width)
            rows = pl.ds(j * half, half)
            low_one[rows, :] = total[pl.ds(pl.multiple_of((1 - mine) * half, half), half), cols].astype(LOW)
            low_two[rows, :] = total[pl.ds(pl.multiple_of(mine * half, half), half), cols].astype(LOW)
        place = pl.ds(begin, low_one.shape[0])
        first = pltpu.make_async_copy(low_one, sent.at[place], sem.at[0])
        second = pltpu.make_async_copy(low_two, kept.at[place], sem.at[1])
        first.start()
        second.start()
        first.wait()
        second.wait()


def output_kernel(act3, x, up, up_bias, y):
    span, width = x.shape
    for t in range(span // SUB):
        rows = pl.ds(t * SUB, SUB)
        product = dot(act3[:, rows], up[...], TN)
        y[rows, :] = (x[rows, :].astype(WIDE) + product + up_bias[...].reshape(1, width)).astype(LOW)


def taps_kernel(parts, *refs):
    mask, odd, which = refs[6 * parts : 6 * parts + 3]
    out, total, field, gy, taps = refs[-5:]
    inner, span = gy.shape
    half = inner // 2
    count = mask.shape[0] // 2
    h = which[0]

    @pl.when(pl.program_id(0) == 0)
    def _():
        total[...] = jnp.zeros_like(total)

    def place(rows, source, tap):
        cells = field[source, at(tap * LANES, span)]
        size = cells.shape[0]
        taps[rows, :] = (cells.reshape(-1, 16, span) * mask[tap][None]).reshape(size, span)

    def body(one, two, got_one, got_two, gy_one, gy_two):
        extend(one, two, got_one, got_two, odd[0], field)
        join_ends(gy_one, gy_two, odd[0], gy, 0)

    by_part(parts, refs[: 6 * parts], body)
    for j in range(count):
        rows = pl.ds(pl.multiple_of(h * half + j * inner, 16), inner)
        place(rows, slice(None), h * (count + 1) + j)
    rows = pl.ds(pl.multiple_of((1 - h) * count * inner, 16), half)
    place(rows, pl.ds(pl.multiple_of(h * half, 16), half), jnp.int32(count))
    total[...] += dot(taps[...], gy[...], NT)

    @pl.when(pl.program_id(0) == pl.num_programs(0) - 1)
    def _():
        out[...] = total[...].astype(out.dtype)


def inner_kernel(parts, *refs):
    per = refs[0].shape[0]
    here = 4 * parts
    sources = refs[here : here + 6]
    odd, side, gain_mid = refs[here + 6 : here + 9]
    gh_out, sent, kept, vec_out = refs[here + 9 : here + 13]
    end_sources = [refs[4 * part : 4 * part + 4] for part in range(parts)]
    one, two, got_one, got_two, mask, straight, s2, xh2, r2, a1, *refs = refs[here + 13 :]
    conv, vec, gain, grad_down, sem = refs[:5]
    fields, taps, gzs, ghs = refs[5:7], refs[7:9], refs[9:11], refs[11:]
    groups, inner, span = s2.shape
    tiles = span // SUB
    count = groups * tiles

    end_refs = (one, two, got_one, got_two)
    ends = [
        [
            pltpu.make_async_copy(source.at[row % per], out.at[row], sem.at[4 * row + i])
            for i, (source, out) in enumerate(zip(end_sources[row // per], end_refs))
        ]
        for row in range(groups)
    ]
    others = [
        pltpu.make_async_copy(source, out, sem.at[4 * groups + i])
        for i, (source, out) in enumerate(zip(sources, (mask, straight, s2, xh2, r2, a1)))
    ]
    for copy in [*ends[0], *others[:2], *ends[1], *others[2:]] + [copy for row in ends[2:] for copy in row]:
        copy.start()
    vec[...] = jnp.zeros_like(vec)
    gain[...] = column(gain_mid)
    grad_down[...] = jnp.zeros_like(grad_down)
    others[0].wait()
    number = straight.shape[0]

    def lay(n):
        row, t = divmod(n, tiles)
        windows(fields[row % 2], mask, n * SUB, taps[n % 2], t)

    def convolve(n):
        for m in range(0, inner, inner // 2):
            rows = pl.ds(m, inner // 2)
            gzs[n % 2][rows, :] = dot(conv[rows, :], taps[n % 2][...], NN)

    def second(n, j):
        row, t = divmod(n, tiles)
        gz = gzs[n % 2]
        cols = pl.ds(j * LANES, LANES)
        place = pl.ds(t * SUB + j * LANES, LANES)
        sum_one = jnp.zeros((8, LANES), WIDE)
        sum_two = jnp.zeros((8, LANES), WIDE)
        for i in range(inner // 32):
            rows = pl.ds(i * 32, 32)
            xh = xh2[row, rows, place].astype(WIDE)
            d = gz[rows, cols] * s2[row, rows, place].astype(WIDE)
            vec[0, rows, :] += d
            vec[1, rows, :] += d * xh
            d = d * gain[rows, :]
            sum_one = sum_one + fold(d)
            sum_two = sum_two + fold(d * xh)
            gz[rows, cols] = d
        one_mean = jnp.sum(sum_one, axis=0, keepdims=True) * (1.0 / inner)
        two_mean = jnp.sum(sum_two, axis=0, keepdims=True) * (1.0 / inner)
        r = r2[row, 0:1, place]
        for i in range(inner // 32):
            rows = pl.ds(i * 32, 32)
            low = (r * (gz[rows, cols] - one_mean - xh2[row, rows, place].astype(WIDE) * two_mean)).astype(LOW)
            ghs[row][rows, place] = low
            vec[2, rows, :] += low.astype(WIDE)

    def weigh(row, part):
        size = grad_down.shape[0] // tiles
        cols = pl.ds(part * size, size)
        grad_down[cols, :] += dot(a1[pl.ds(row * span, span), cols], ghs[row][...], TT)

    def block(i):
        if i < count:
            lay(i)
        if 2 <= i < count + 2:
            for j in range(SUB // LANES):
                second(i - 2, j)
        if 1 <= i <= count:
            convolve(i - 1)
        done = i - 2 - tiles
        if done >= 0:
            weigh(*divmod(done, tiles))

    stores = []
    for i in range(count + 2 + tiles):
        if i < count and i % tiles == 0:
            row = i // tiles
            for copy in ends[row]:
                copy.wait()
            extend(one.at[row], two.at[row], got_one.at[row], got_two.at[row], odd[0], fields[row % 2])
        if i == 1:
            others[1].wait()
            for k in range(number):
                conv[:, k * inner : (k + 1) * inner] = straight[number - 1 - k]
        if i == 2:
            for copy in others[2:]:
                copy.wait()

        @pl.when(odd[0] >= 0)
        def _():
            block(i)

        if 2 <= i < count + 2 and (i - 1) % tiles == 0:
            row = (i - 2) // tiles
            stores.append(pltpu.make_async_copy(ghs[row], gh_out.at[row], sem.at[4 * groups + 6 + row]))
            stores[-1].start()
    hand_over(grad_down, side[0], sent, kept)
    lane_sums(vec, vec_out)
    for copy in stores:
        copy.wait()


def leave_kernel(gh, down, s1, xh1, r1, gain, e, gx, vec, ga):
    span, width = e.shape
    gain_row = gain[...].reshape(1, width)

    @pl.when(pl.program_id(0) == 0)
    def _():
        vec[...] = jnp.zeros_like(vec)

    def project(t):
        rows = pl.ds(t * SUB, SUB)
        ga[rows, :] = dot(gh[:, rows], down[...], TT)

    def first(i):
        rows = pl.ds(i * 16, 16)
        xh = xh1[rows, :].astype(WIDE)
        d = ga[rows, :] * s1[rows, :].astype(WIDE)
        vec[0] += fold(d)
        vec[1] += fold(d * xh)
        d = d * gain_row
        one = jnp.sum(d, axis=-1, keepdims=True) * (1.0 / width)
        two = jnp.sum(d * xh, axis=-1, keepdims=True) * (1.0 / width)
        r = r1[rows, 0:1]
        cot = e[rows, :].astype(WIDE)
        vec[2] += fold(cot)
        gx[rows, :] = (cot + r * (d - one - xh * two)).astype(LOW)

    for t in range(span // SUB):
        project(t)
        for i in range(SUB // 16):
            first(t * SUB // 16 + i)


def settle_kernel(late, *refs):
    where, one, two, source = refs[:4]
    conv, up, down = refs[4 + 3 * late : 7 + 3 * late]
    low, wide, low_down, wide_down, sem = refs[-5:]
    side, place = where[0], where[1]
    size, width = one.shape
    half, extra = conv.shape[0] // 2, up.shape[0] // 2
    rest = half - size

    loads = [
        pltpu.make_async_copy(one, low.at[place], sem.at[0]),
        pltpu.make_async_copy(two, low.at[1 - place], sem.at[1]),
        pltpu.make_async_copy(source, low_down, sem.at[2]),
    ]
    for copy in loads:
        copy.start()

    def rows(begin, count):
        return pl.ds(pl.multiple_of(begin, 64), count)

    loads[0].wait()
    loads[1].wait()
    stores = []

    def store(source, out):
        stores.append(pltpu.make_async_copy(source, out, sem.at[3 + len(stores)]))
        stores[-1].start()

    wide[0] = low[0].astype(WIDE)
    store(wide.at[0], conv.at[rows(side * half, size)])
    wide[1] = low[1].astype(WIDE)
    store(wide.at[1, pl.ds(0, rest)], conv.at[rows(side * half + size, rest)])
    for j in range(up.shape[1] // width):
        store(
            wide.at[1, pl.ds(rest + j * extra, extra)],
            up.at[rows(side * extra, extra), pl.ds(j * width, width)],
        )
    loads[2].wait()
    wide_down[...] = low_down[...].astype(WIDE)
    store(wide_down, down.at[rows(side * source.shape[0], source.shape[0])])
    for copy in stores:
        copy.wait()


def settle(pieces, down, where, half, before=()):
    size, width = pieces[0].shape
    anywhere = pl.BlockSpec(memory_space=pl.ANY)
    kinds = [jax.ShapeDtypeStruct(dims, WIDE) for dims in ((2 * half, width), (width, 2 * width), (2 * down.shape[0], width))]
    return call_once(
        functools.partial(settle_kernel, bool(before)),
        [pl.BlockSpec(memory_space=pltpu.SMEM)] + [anywhere] * (3 + len(before)),
        [(anywhere, kind) for kind in kinds],
        [pltpu.VMEM((2, size, width), LOW), pltpu.VMEM((2, size, width), WIDE)]
        + [pltpu.VMEM(down.shape, LOW), pltpu.VMEM(down.shape, WIDE), pltpu.SemaphoreType.DMA((8,))],
        1 << 30,
        (jnp.stack(where).astype(jnp.int32), *pieces, down, *before),
        {4 + i: i for i in range(len(before))},
    )


def call_once(kernel, ins, outs, scratch, flops, args, aliases={}):
    return pl.pallas_call(
        kernel,
        in_specs=ins,
        out_specs=[spec for spec, _ in outs],
        out_shape=[shape for _, shape in outs],
        scratch_shapes=scratch,
        cost_estimate=pl.CostEstimate(flops=flops, bytes_accessed=24 << 20, transcendentals=0),
        compiler_params=pltpu.CompilerParams(vmem_limit_bytes=VMEM),
        input_output_aliases=aliases,
    )(*args)


def call(kernel, steps, ins, outs, scratch, flops, args, aliases={}):
    return pl.pallas_call(
        kernel,
        grid=(steps,),
        in_specs=ins,
        out_specs=[spec for spec, _ in outs],
        out_shape=[shape for _, shape in outs],
        scratch_shapes=scratch,
        cost_estimate=pl.CostEstimate(flops=flops, bytes_accessed=24 << 20, transcendentals=0),
        compiler_params=pltpu.CompilerParams(vmem_limit_bytes=VMEM),
        input_output_aliases=aliases,
    )(*args)


def whole(*shape):
    return pl.BlockSpec(shape, lambda i: (0,) * len(shape), pipeline_mode=pl.Buffered(1))


def held(*shape):
    return pl.BlockSpec(shape, lambda i: (0,) * len(shape))


def swap_ends(one, two):
    count = lax.axis_size("seq")
    pairs = [(i, i ^ 1) for i in range(count)]
    other = [(i, ((i + 1) ^ 1) - 1) for i in range(1, count - 1)]
    return one, two, lax.ppermute(one, "seq", pairs), lax.ppermute(two, "seq", other)


def local(
    inputs,
    starts,
    types,
    norm_gain_in,
    norm_bias_in,
    proj_down,
    proj_down_bias,
    norm_gain_mid,
    norm_bias_mid,
    conv_weight,
    conv_bias,
    norm_gain_out,
    norm_bias_out,
    proj_up,
    proj_up_bias,
    cotangent,
):
    groups, span, width = inputs.shape
    taps, inner, _ = conv_weight.shape
    reach = taps // 2 * DILATION_STEP
    row_length = span * lax.axis_size("seq")
    first = lax.axis_index("seq") * span
    places = first - reach + jnp.arange(span + 2 * reach, dtype=jnp.int32)
    protein = jnp.sum((starts[:, None, :] <= places[None, :, None]).astype(jnp.int32), axis=2)
    inside = (places >= 0) & (places < row_length)
    centre = protein[:, reach : reach + span]
    masks = []
    for k in range(taps):
        window = slice(k * DILATION_STEP, k * DILATION_STEP + span)
        masks.append((protein[:, window] == centre) & inside[None, window])
    full = functools.reduce(jnp.logical_and, masks)
    kinds = types[:, :, None] == jnp.arange(TYPES, dtype=jnp.int32)[None, None, :]
    tally = jnp.sum((kinds & full[:, :, None]).astype(WIDE), axis=(0, 1))
    mask = jnp.stack(masks).astype(LOW).reshape(taps, 1, groups * span)
    mask = jnp.broadcast_to(mask, (taps, 16, groups * span))

    x = inputs.reshape(groups * span, width)
    e = cotangent.reshape(groups * span, width)

    parts = 2 if groups % 2 == 0 else 1
    per = groups // parts
    shape = jax.ShapeDtypeStruct

    def rows_of(size, part=0):
        return pl.BlockSpec((span, size), lambda i: (i + part * per, 0))

    def turned(size, part=0):
        return pl.BlockSpec((None, size, span), lambda i: (i + part * per, 0, 0))

    def mask_of(part=0):
        return pl.BlockSpec((taps, 16, span), lambda i: (0, 0, i + part * per))

    def clamped(part):
        def place(i):
            return (jnp.clip(i - part * per, 0, per - 1), 0, 0)

        return pl.BlockSpec((None, inner, reach), place)

    def all_rows(size, kind=LOW, part=0):
        return rows_of(size, part), shape((groups * span, size), kind)

    def all_turned(size, kind=LOW, part=0):
        return turned(size, part), shape((groups, size, span), kind)

    def sums(*dims):
        return held(*dims), shape(dims, WIDE)

    anywhere = pl.BlockSpec(memory_space=pl.ANY)
    scalar = pl.BlockSpec(memory_space=pltpu.SMEM)
    odd = (lax.axis_index("seq") & 1).reshape(1)
    core = odd
    end = pl.BlockSpec((None, inner, reach), lambda i: (i, 0, 0))
    ends = [(end, shape((per, inner, reach), LOW))] * 2
    field = pltpu.VMEM((inner, span + 2 * reach), LOW)
    block = pltpu.VMEM((inner, span), LOW)
    wide_block = pltpu.VMEM((inner, span), WIDE)
    columns = pltpu.VMEM((3, inner, LANES), WIDE)
    flops = 2 * span * inner * width

    z_rows = []
    entered = []
    for part in range(parts):
        begun = part > 0
        *entered, one, two = call(
            enter_kernel,
            per,
            [rows_of(width, part)] * 2
            + [scalar]
            + [whole(width)] * 2
            + [whole(inner, width), whole(width, inner)]
            + [whole(inner)] * 3
            + [anywhere] * len(entered),
            [all_rows(width, part=part)] * 3
            + [all_rows(LANES, WIDE, part)]
            + [all_turned(inner, part=part)] * 2
            + [all_turned(8, WIDE, part), all_turned(inner, WIDE, part)]
            + ends,
            [wide_block, block, columns],
            3 * per * flops,
            (x, e, odd, norm_gain_in, norm_bias_in, proj_up, proj_down)
            + (proj_down_bias, norm_gain_mid, norm_bias_mid, *entered),
            {10 + i: i for i in range(8)} if begun else {},
        )
        z_rows, entered, one, two = lax.optimization_barrier((z_rows, entered, one, two))
        z_rows.append(swap_ends(one, two))
    a1, s1, xh1, r1, s2, xh2, r2, ga3 = entered

    vec_out = []
    conv = conv_weight.reshape(taps * inner, inner)
    vector = pl.BlockSpec(memory_space=pltpu.VMEM)
    small_sums = [(vector, shape((3, inner), WIDE))]

    def low(*dims):
        return pltpu.VMEM(dims, LOW)

    def wide(*dims):
        return pltpu.VMEM(dims, WIDE)

    part_ends_out = [(anywhere, shape((per, inner, reach), LOW))] * 2
    act3 = None
    y_rows = []
    for part in range(parts):
        begun = part > 0
        act3, one, two, vec = call_once(
            functools.partial(turn_kernel, part),
            [anywhere] * 7 + [scalar] + [vector] * 3 + [anywhere] * begun,
            [(anywhere, shape((groups, inner, span), LOW))] + part_ends_out + small_sums,
            [low(per, inner, reach)] * 4
            + [low(taps, 16, per * span), low(taps * inner, inner), wide(per, inner, span)]
            + [low(per, inner, span)] * 2
            + [low(per, inner, reach)] * 2
            + [columns, columns, pltpu.SemaphoreType.DMA((3 + 7 * per,))]
            + [low(inner, span + 2 * reach)] * 2
            + [low(taps * inner, SUB)] * 2
            + [wide(inner, SUB)] * 4,
            3 * per * flops,
            (*z_rows[part], mask, conv, ga3, odd, conv_bias, norm_gain_out, norm_bias_out)
            + (act3,) * begun,
            {11: 0} if begun else {},
        )
        y_rows, act3, one, two = lax.optimization_barrier((y_rows, act3, one, two))
        y_rows.append(swap_ends(one, two))
        vec_out.append(vec)

    half = taps * inner // 2
    extra = inner // 2 * (width // inner)
    rows_main = -(-(half + extra) // 256) * 256

    def grad_taps(which):
        def work(y_ends, buffers=()):
            return call(
                functools.partial(taps_kernel, parts),
                groups,
                [clamped(part) for part in range(parts) for _ in range(6)]
                + [mask_of(), scalar, scalar]
                + [anywhere] * len(buffers),
                [(held(half, inner), shape((rows_main, inner), LOW))],
                [pltpu.VMEM((half, inner), WIDE), field, block, pltpu.VMEM((half, span), LOW)],
                5 * groups * flops // 4,
                [item for z_row, y_end in zip(z_rows, y_ends) for item in (*z_row, *y_end)]
                + [mask, odd, which, *buffers],
                {6 * parts + 3: 0} if buffers else {},
            )

        return work

    def grad_project(sent):
        return call(
            functools.partial(up_kernel, half),
            groups,
            [turned(inner), rows_of(width), scalar, anywhere],
            [(anywhere, shape((rows_main, inner), LOW))] * 2,
            [pltpu.VMEM((inner, width), WIDE)]
            + [pltpu.VMEM((extra, inner), LOW)] * 2
            + [pltpu.SemaphoreType.DMA((2,))],
            groups * flops,
            (act3, e, core, sent),
            {3: 0},
        )

    def back(*rows):
        halves = (vector, shape((width // 2, inner), LOW))
        return call_once(
            functools.partial(inner_kernel, parts),
            [anywhere] * (4 * parts + 6) + [scalar] * 2 + [vector],
            [(anywhere, shape((groups, inner, span), LOW)), halves, halves] + small_sums,
            [low(groups, inner, reach)] * 4
            + [low(taps, 16, groups * span), low(taps, inner, inner)]
            + [low(groups, inner, span)] * 2
            + [wide(groups, 8, span), low(groups * span, width)]
            + [low(inner, taps * inner), columns, wide(inner, LANES), wide(width, inner)]
            + [pltpu.SemaphoreType.DMA((6 + 5 * groups,))]
            + [low(inner, span + 2 * reach)] * 2
            + [low(taps * inner, SUB)] * 2
            + [wide(inner, SUB)] * 2
            + [low(inner, span)] * groups,
            4 * groups * flops,
            (*[item for row in rows for item in row], mask, conv_weight, s2, xh2, r2, a1, odd, core, norm_gain_mid),
        )

    def leave(grad_h):
        return call(
            leave_kernel,
            groups,
            [turned(inner), whole(width, inner), rows_of(width), rows_of(width)]
            + [rows_of(LANES), whole(width), rows_of(width)],
            [all_rows(width), sums(3, 8, width)],
            [pltpu.VMEM((span, width), WIDE)],
            groups * flops,
            (grad_h, proj_down, s1, xh1, r1, norm_gain_in, e),
        )

    def project(act3):
        return call(
            output_kernel,
            groups,
            [turned(inner), rows_of(width), whole(inner, width), whole(width)],
            [all_rows(width)],
            [],
            groups * flops,
            (act3, x, proj_up, proj_up_bias),
        )

    under_way = Sums()
    y_ends = [row[:2] for row in y_rows]
    (sent,) = grad_taps(1 - core)(y_ends)
    act3, y_ends, sent = lax.optimization_barrier((act3, y_ends, sent))
    sent, kept = grad_project(sent)
    own = []
    plan = exchange_plan(False)
    bits = bits_of(lax.axis_size("seq"))
    here = lax.axis_index("seq")
    other = (jnp.where(here & 1 == 1, here & bits[1], here & bits[-1]) != 0).astype(jnp.int32)
    under_way.add("main", sum_steps(sent, own, plan, True))
    under_way.turn(["main"], grad_taps(core), (y_ends, [kept]), own)
    grad_h, sent, kept, vec_mid = under_way.turn(["main"], back, y_rows)
    own_down = [kept]
    under_way.add("down", sum_steps(sent, own_down, exchange_plan(True)))
    under_way.turn(["main", "down"])
    input_grad, vec_in = under_way.turn(["main", "down"], leave, (grad_h,))

    small_in = vec_in.sum(1)
    small_mid = vec_mid
    small_out = sum(vec_out)
    vectors = [small_in[1], small_in[0], small_mid[2], small_mid[1], small_mid[0]]
    vectors += [small_out[2], small_out[1], small_out[0], small_in[2], tally]
    ends = [0]
    for item in vectors:
        ends.append(ends[-1] + item.shape[0])
    flat = jnp.concatenate(vectors)
    flat = jnp.pad(flat, (0, -flat.shape[0] % 1024)).reshape(-1, LANES)
    under_way.add("small", small_steps(flat, exchange_plan(True)))
    names = ["main", "down", "small"]
    (output,) = under_way.turn(names, project, (act3,))
    sides = here & 1, plan[1][2], other

    def settle_own(pieces, down):
        return settle(pieces, down, (sides[0], sides[1]), half)

    while len(own_down) == 1 or len(own) == 1:
        under_way.turn(names)
    settled = under_way.turn(names, settle_own, (own[1], own_down[1]))
    while under_way.open:
        under_way.turn(names)
    settled = settle(under_way.done["main"], under_way.done["down"], (1 - sides[0], sides[2]), half, settled)
    total_conv = settled[0].reshape(taps, inner, inner)
    total_up, total_down = settled[1:]
    flat = under_way.done["small"].reshape(-1)
    totals = [flat[begin:end] for begin, end in zip(ends, ends[1:])]
    return (
        output.reshape(inputs.shape),
        input_grad.reshape(inputs.shape),
        totals[0],
        totals[1],
        total_down,
        *totals[2:5],
        total_conv,
        *totals[5:8],
        total_up,
        totals[8],
        totals[9].astype(jnp.int32),
    )


def solution(mesh):
    return jax.shard_map(
        local,
        mesh=mesh,
        in_specs=(
            P("rows", "seq", None),
            P("rows", None),
            P("rows", "seq"),
            P(),
            P(),
            P(),
            P(),
            P(),
            P(),
            P(),
            P(),
            P(),
            P(),
            P(),
            P(),
            P("rows", "seq", None),
        ),
        out_specs=(
            P("rows", "seq", None),
            P("rows", "seq", None),
            P(),
            P(),
            P(),
            P(),
            P(),
            P(),
            P(),
            P(),
            P(),
            P(),
            P(),
            P(),
            P(),
        ),
        check_vma=False,
    )
```

```python
import functools

import jax
import jax.numpy as jnp
from jax import lax
from jax.experimental import pallas as pl
from jax.experimental.pallas import tpu as pltpu
from jax.sharding import PartitionSpec as P

DILATION_STEP = 128
TYPES = 30
LANES = 128
SUB = 256
VMEM = {"enter": 60, "turn": 52, "taps": 52, "inner": 52, "leave": 52}
LOW = jnp.bfloat16
WIDE = jnp.float32
NN = (((1,), (0,)), ((), ()))
NT = (((1,), (1,)), ((), ()))
TN = (((0,), (0,)), ((), ()))
TT = (((0,), (1,)), ((), ()))


def bits_of(size):
    count = size.bit_length() - 1
    assert size == 1 << count
    return [1 << place for place in range(count)]


def xor_pairs(size, bit):
    return [(i, i ^ bit) for i in range(size)]


def exchange_plan(direct):
    seq, rows = lax.axis_size("seq"), lax.axis_size("rows")
    here, row = lax.axis_index("seq"), lax.axis_index("rows")
    plan = [("seq", [xor_pairs(seq, 1)], here & 1)]
    bits = bits_of(seq)[1:]
    if direct and len(bits) == 2:
        plan.append(("seq", [xor_pairs(seq, 2 * m) for m in range(1, 4)], here >> 1))
    else:
        for first, second in zip(bits, bits[::-1]):
            pairs = [(i, i ^ (second if i & 1 else first)) for i in range(seq)]
            place = jnp.where(here & 1 == 1, (here & second) != 0, (here & first) != 0)
            plan.append(("seq", [pairs], place.astype(jnp.int32)))
    plan.append(("rows", [xor_pairs(rows, m) for m in range(1, rows)], row))
    return plan


def cut(cells, place, count):
    size = cells.shape[0] // count
    return lax.dynamic_slice_in_dim(cells, place * size, size, axis=0)


def in_order(pieces, place, axis=0):
    ordered = []
    for j in range(len(pieces)):
        piece = pieces[-1]
        for m in range(len(pieces) - 2, -1, -1):
            piece = jnp.where(place ^ j == m, pieces[m], piece)
        ordered.append(piece)
    return jnp.concatenate(ordered, axis=axis)


def sum_steps(sent, own, plan, early=False):
    sent = [sent]
    for step, (axis, pairs, _) in enumerate(plan):
        got = yield sent, axis, pairs
        if step == 0:
            (kept,) = own
        terms = [kept, *got]
        if step + 1 < len(plan):
            _, coming, place = plan[step + 1]
            count = len(coming) + 1

            def part(at):
                return sum(cut(term, at, count).astype(WIDE) for term in terms)

            sent = [part(place ^ m).astype(LOW) for m in range(1, count)]
            kept = part(place)
    cells = sum(term.astype(WIDE) for term in terms).astype(LOW)
    core_axis, (core_pairs,), _ = plan[0]
    if early:
        for axis, pairs, place in plan[:1:-1]:
            got = yield [cells] * len(pairs), axis, pairs
            cells = in_order([cells, *got], place)
        axis, pairs, place = plan[1]
        first, second = yield [cells, cells], axis, [*pairs, core_pairs]
        own.append((cells, first))
        (third,) = yield [first], core_axis, [core_pairs]
        return second, third
    width = cells.shape[-1]
    cells = cells[None]
    for axis, pairs, place in plan[1:]:
        lead, size, _ = cells.shape
        got = yield [cells.reshape(-1, width)] * len(pairs), axis, pairs
        cells = in_order([cells, *[piece.reshape(cells.shape) for piece in got]], place, 1)
        cells = cells.reshape(-1, size, width)
    cells = cells.reshape(-1, width)
    own.append(cells)
    (got,) = yield [cells], core_axis, [core_pairs]
    return got


def small_steps(cells):
    first, *others = [("seq", bit) for bit in bits_of(lax.axis_size("seq"))]
    for axis, bit in [first, *[("rows", bit) for bit in bits_of(lax.axis_size("rows"))], *others]:
        (got,) = yield [cells], axis, [xor_pairs(lax.axis_size(axis), bit)]
        cells = cells + got
    return cells


class Sums:
    def __init__(self):
        self.open = {}
        self.done = {}

    def add(self, name, steps):
        self.open[name] = (steps, next(steps))

    def turn(self, names, work=None, gate=(), own=None):
        names = [name for name in names if name in self.open]
        sent = [self.open[name][1][0] for name in names]
        sent, gate = lax.optimization_barrier((sent, gate))
        got = []
        for name, cells in zip(names, sent):
            _, axis, pairs = self.open[name][1]
            got.append([lax.ppermute(cell, axis, pair) for cell, pair in zip(cells, pairs)])
        made = work(*gate) if work else ()
        got, made = lax.optimization_barrier((got, made))
        if own is not None:
            own.extend(made)
        for name, cells in zip(names, got):
            steps = self.open.pop(name)[0]
            try:
                self.open[name] = (steps, steps.send(cells))
            except StopIteration as end:
                self.done[name] = end.value
        return made


def dot(left, right, dims):
    return lax.dot_general(left, right, dims, preferred_element_type=WIDE)


def gelu_parts(u):
    phi = 0.5 + 0.5 * lax.erf(u * 0.7071067811865476)
    bell = jnp.exp2(u * u * -0.7213475204444817)
    return u * phi, phi + (u * 0.3989422804014327) * bell


def fold(values):
    return jnp.sum(values.reshape(-1, 8, values.shape[-1]), axis=0)


def column_mean(rows, count):
    total = jnp.zeros((8, LANES), WIDE)
    for i in range(count // 64):
        total = total + fold(rows(i))
    return jnp.sum(total, axis=0, keepdims=True) * (1.0 / count)


def column(vector):
    size = vector.shape[0]
    return jnp.broadcast_to(vector[...].reshape(1, size), (LANES, size)).T


def enter_kernel(*refs):
    x, e, odd, gain, bias, up, down, down_bias, gain_mid, bias_mid = refs[:10]
    a1, s1, xh1, r1, s2, xh2, r2, ga3, z_one, z_two, h, z, mid = refs[-13:]
    span, width = x.shape
    inner = h.shape[0]
    gain_row, bias_row = gain[...].reshape(1, width), bias[...].reshape(1, width)

    @pl.when(pl.program_id(0) == 0)
    def _():
        mid[0] = column(down_bias)
        mid[1] = column(gain_mid)
        mid[2] = column(bias_mid)

    def first(i):
        rows = pl.ds(i * 16, 16)
        v = x[rows, :].astype(WIDE)
        v = v - jnp.sum(v, axis=-1, keepdims=True) * (1.0 / width)
        r = lax.rsqrt(jnp.sum(v * v, axis=-1, keepdims=True) * (1.0 / width) + 1e-05)
        xh = v * r
        act, slope = gelu_parts(xh * gain_row + bias_row)
        a1[rows, :] = act.astype(LOW)
        s1[rows, :] = slope.astype(LOW)
        xh1[rows, :] = xh.astype(LOW)
        r1[rows, :] = jnp.broadcast_to(r, (16, LANES))

    def project(t):
        cols = pl.ds(t * SUB, SUB)
        product = dot(down[...], a1[cols, :], TT)
        for j in range(SUB // LANES):
            h[:, pl.ds(t * SUB + j * LANES, LANES)] = product[:, j * LANES : (j + 1) * LANES] + mid[0]
        ga3[:, cols] = dot(up[...], e[cols, :], NT)

    def second(j):
        cols = pl.ds(j * LANES, LANES)
        m = column_mean(lambda i: h[pl.ds(i * 64, 64), cols], inner)

        def squares(i):
            c = h[pl.ds(i * 64, 64), cols] - m
            return c * c

        r = lax.rsqrt(column_mean(squares, inner) + 1e-05)
        for i in range(inner // 32):
            rows = pl.ds(i * 32, 32)
            xh = (h[rows, cols] - m) * r
            act, slope = gelu_parts(xh * mid[1, rows, :] + mid[2, rows, :])
            z[rows, cols] = act.astype(LOW)
            s2[rows, cols] = slope.astype(LOW)
            xh2[rows, cols] = xh.astype(LOW)
        r2[:, cols] = jnp.broadcast_to(r, (8, LANES))

    for t in range(span // SUB):
        for i in range(SUB // 16):
            first(t * SUB // 16 + i)
        project(t)
        if t:
            for j in range(SUB // LANES):
                second((t - 1) * SUB // LANES + j)
    for j in range(SUB // LANES):
        second((span // SUB - 1) * SUB // LANES + j)
    part_ends(z, odd[0], z_one, z_two)


def at(place, size):
    return pl.ds(pl.multiple_of(place, LANES), size)


def part_ends(cells, odd, one, two):
    half = one.shape[1]
    one[...] = cells[:, at((1 - odd) * half, half)]
    two[...] = cells[:, at(odd * half, half)]


def join_ends(one, two, odd, out, begin):
    half = one.shape[1]
    out[:, at(begin + (1 - odd) * half, half)] = one[...]
    out[:, at(begin + odd * half, half)] = two[...]


def extend(one, two, got_one, got_two, odd, out):
    half = one.shape[1]
    join_ends(one, two, odd, out, half)
    out[:, at((1 - odd) * 3 * half, half)] = got_one[...]
    out[:, at(odd * 3 * half, half)] = got_two[...]


def windows(field, mask, first, out, t):
    inner = field.shape[0]
    taps = mask.shape[0]
    for k in range(taps):
        source = field[:, pl.ds(t * SUB + k * LANES, SUB)]
        if k != taps // 2:
            source = (source.reshape(-1, 16, SUB) * mask[k, :, pl.ds(first, SUB)][None]).reshape(inner, SUB)
        out[k * inner : (k + 1) * inner, :] = source


def lane_sums(vec, out):
    for k in range(vec.shape[0]):
        out[k : k + 1, :] = jnp.sum(vec[k].T, axis=0, keepdims=True)


def in_blocks(count, always, body):
    for i in range(count):

        @pl.when(always)
        def _():
            body(i)


def turn_kernel(begun, *refs):
    sources = refs[:7]
    odd, conv_bias, gain_out, bias_out = refs[7:11]
    refs = refs[11 + begun :]
    act_out, one_out, two_out, vec_out = refs[:4]
    one, two, got_one, got_two, mask, conv, ga3, *refs = refs[4:]
    act3, gy, gy_one, gy_two, vec, out3, sem = refs[:7]
    fields, taps, dys, xhs = refs[7:9], refs[9:11], refs[11:13], refs[13:15]
    part = int(begun)
    rows_here, inner, span = gy.shape
    tiles = span // SUB
    count = rows_here * tiles

    def load(i, source, out):
        return pltpu.make_async_copy(source, out, sem.at[i])

    first_row = part * rows_here
    end_refs = (one, two, got_one, got_two)
    ends = [
        [load(4 * row + i, source.at[row], out.at[row]) for i, (source, out) in enumerate(zip(sources[:4], end_refs))]
        for row in range(rows_here)
    ]
    others = [
        load(4 * rows_here, sources[4].at[:, :, pl.ds(first_row * span, rows_here * span)], mask),
        load(4 * rows_here + 1, sources[5], conv),
        load(4 * rows_here + 2, sources[6].at[pl.ds(first_row, rows_here)], ga3),
    ]
    for copy in [*ends[0], *others[:2]] + [copy for row in ends[1:] for copy in row] + others[2:]:
        copy.start()
    vec[...] = jnp.zeros_like(vec)
    out3[0] = column(conv_bias)
    out3[1] = column(gain_out)
    out3[2] = column(bias_out)
    others[0].wait()

    def lay(n):
        row, t = divmod(n, tiles)
        windows(fields[row % 2], mask, n * SUB, taps[n % 2], t)

    def convolve(n):
        product = dot(conv[...], taps[n % 2][...], TN)
        for j in range(SUB // LANES):
            dys[n % 2][:, pl.ds(j * LANES, LANES)] = product[:, j * LANES : (j + 1) * LANES] + out3[0]

    def third(n, j):
        row, t = divmod(n, tiles)
        dy, xh3 = dys[n % 2], xhs[n % 2]
        cols = pl.ds(j * LANES, LANES)
        place = pl.ds(t * SUB + j * LANES, LANES)
        m = column_mean(lambda i: dy[pl.ds(i * 64, 64), cols], inner)

        def squares(i):
            c = dy[pl.ds(i * 64, 64), cols] - m
            return c * c

        r = lax.rsqrt(column_mean(squares, inner) + 1e-05)
        sum_one = jnp.zeros((8, LANES), WIDE)
        sum_two = jnp.zeros((8, LANES), WIDE)
        for i in range(inner // 32):
            rows = pl.ds(i * 32, 32)
            gain = out3[1, rows, :]
            xh = (dy[rows, cols] - m) * r
            act, slope = gelu_parts(xh * gain + out3[2, rows, :])
            act3[row, rows, place] = act.astype(LOW)
            d = ga3[row, rows, place] * slope
            vec[0, rows, :] += d
            vec[1, rows, :] += d * xh
            d = d * gain
            sum_one = sum_one + fold(d)
            sum_two = sum_two + fold(d * xh)
            dy[rows, cols] = d
            xh3[rows, cols] = xh
        one_mean = jnp.sum(sum_one, axis=0, keepdims=True) * (1.0 / inner)
        two_mean = jnp.sum(sum_two, axis=0, keepdims=True) * (1.0 / inner)
        for i in range(inner // 32):
            rows = pl.ds(i * 32, 32)
            low = (r * (dy[rows, cols] - one_mean - xh3[rows, cols] * two_mean)).astype(LOW)
            gy[row, rows, place] = low
            vec[2, rows, :] += low.astype(WIDE)

    stores = []

    def block(i):
        if i < count:
            lay(i)
        if 2 <= i:
            for j in range(SUB // LANES):
                third(i - 2, j)
        if 1 <= i <= count:
            convolve(i - 1)

    for i in range(count + 2):
        if i < count and i % tiles == 0:
            row = i // tiles
            for copy in ends[row]:
                copy.wait()
            extend(one.at[row], two.at[row], got_one.at[row], got_two.at[row], odd[0], fields[row % 2])
        if i == 1:
            others[1].wait()
        if i == 2:
            others[2].wait()

        @pl.when(odd[0] >= 0)
        def _():
            block(i)

        if i >= 2 and (i - 1) % tiles == 0:
            row = (i - 2) // tiles
            part_ends(gy.at[row], odd[0], gy_one.at[row], gy_two.at[row])
            for k, (source, out) in enumerate(
                ((act3, act_out.at[first_row + row]), (gy_one, one_out.at[row]), (gy_two, two_out.at[row]))
            ):
                stores.append(load(4 * rows_here + 3 + 3 * row + k, source.at[row], out))
                stores[-1].start()
    lane_sums(vec, vec_out)
    for copy in stores:
        copy.wait()


def by_part(parts, refs, body):
    step = pl.program_id(0)
    per = pl.num_programs(0) // parts
    count = len(refs) // parts
    for part in range(parts):

        @pl.when((step >= part * per) & (step < (part + 1) * per))
        def _():
            body(*refs[part * count : (part + 1) * count])


def hand_over(total, side, sent, kept):
    half = kept.shape[0]
    sent[...] = total[pl.ds(pl.multiple_of((1 - side) * half, half), half), :].astype(LOW)
    kept[...] = total[pl.ds(pl.multiple_of(side * half, half), half), :].astype(kept.dtype)


def output_kernel(act3, x, up, up_bias, y):
    span, width = x.shape
    for t in range(span // SUB):
        rows = pl.ds(t * SUB, SUB)
        product = dot(act3[:, rows], up[...], TN)
        y[rows, :] = (x[rows, :].astype(WIDE) + product + up_bias[...].reshape(1, width)).astype(LOW)


def taps_step(parts, ends, mask, odd, which, total, field, gy, taps):
    inner, span = gy.shape
    half = inner // 2
    count = mask.shape[0] // 2
    h = which[0]

    def place(rows, source, tap):
        cells = field[source, at(tap * LANES, span)]
        size = cells.shape[0]
        taps[rows, :] = (cells.reshape(-1, 16, span) * mask[tap][None]).reshape(size, span)

    def body(one, two, got_one, got_two, gy_one, gy_two):
        extend(one, two, got_one, got_two, odd[0], field)
        join_ends(gy_one, gy_two, odd[0], gy, 0)

    by_part(parts, ends, body)
    for j in range(count):
        rows = pl.ds(pl.multiple_of(h * half + j * inner, 16), inner)
        place(rows, slice(None), h * (count + 1) + j)
    rows = pl.ds(pl.multiple_of((1 - h) * count * inner, 16), half)
    place(rows, pl.ds(pl.multiple_of(h * half, 16), half), jnp.int32(count))
    total[...] += dot(taps[...], gy[...], NT)


def first_taps_kernel(parts, *refs):
    mask, odd, which, act3, e = refs[6 * parts : 6 * parts + 5]
    sent, kept, total, field, gy, taps, total_up, low, low_one, low_two, sem = refs[-11:]
    half, width = total_up.shape[0] // 2, low_one.shape[1]

    @pl.when(pl.program_id(0) == 0)
    def _():
        total[...] = jnp.zeros_like(total)
        total_up[...] = jnp.zeros_like(total_up)

    taps_step(parts, refs[: 6 * parts], mask, odd, which, total, field, gy, taps)
    total_up[...] += dot(act3[...], e[...], NN)

    @pl.when(pl.program_id(0) == pl.num_programs(0) - 1)
    def _():
        other = which[0]
        low[...] = total[...].astype(LOW)
        rows = low.shape[0]
        copies = [pltpu.make_async_copy(low, sent.at[pl.ds(0, rows)], sem.at[0])]
        copies[0].start()
        for j in range(total_up.shape[1] // width):
            cols = pl.ds(j * width, width)
            place = pl.ds(j * half, half)
            low_one[place, :] = total_up[pl.ds(pl.multiple_of(other * half, half), half), cols].astype(LOW)
            low_two[place, :] = total_up[pl.ds(pl.multiple_of((1 - other) * half, half), half), cols].astype(LOW)
        place = pl.ds(rows, low_one.shape[0])
        copies.append(pltpu.make_async_copy(low_one, sent.at[place], sem.at[1]))
        copies.append(pltpu.make_async_copy(low_two, kept.at[place], sem.at[2]))
        for copy in copies[1:]:
            copy.start()
        for copy in copies:
            copy.wait()


def second_taps_kernel(parts, *refs):
    mask, odd, which = refs[6 * parts : 6 * parts + 3]
    out, total, field, gy, taps = refs[-5:]

    @pl.when(pl.program_id(0) == 0)
    def _():
        total[...] = jnp.zeros_like(total)

    taps_step(parts, refs[: 6 * parts], mask, odd, which, total, field, gy, taps)

    @pl.when(pl.program_id(0) == pl.num_programs(0) - 1)
    def _():
        out[...] = total[...].astype(out.dtype)


def inner_kernel(parts, *refs):
    per = refs[0].shape[0]
    here = 4 * parts
    sources = refs[here : here + 6]
    odd, side, gain_mid = refs[here + 6 : here + 9]
    gh_out, sent, kept, vec_out = refs[here + 9 : here + 13]
    end_sources = [refs[4 * part : 4 * part + 4] for part in range(parts)]
    one, two, got_one, got_two, mask, straight, s2, xh2, r2, a1, *refs = refs[here + 13 :]
    conv, vec, gain, grad_down, sem = refs[:5]
    fields, taps, gzs, ghs = refs[5:7], refs[7:9], refs[9:11], refs[11:]
    groups, inner, span = s2.shape
    tiles = span // SUB
    count = groups * tiles

    end_refs = (one, two, got_one, got_two)
    ends = [
        [
            pltpu.make_async_copy(source.at[row % per], out.at[row], sem.at[4 * row + i])
            for i, (source, out) in enumerate(zip(end_sources[row // per], end_refs))
        ]
        for row in range(groups)
    ]
    others = [
        pltpu.make_async_copy(source, out, sem.at[4 * groups + i])
        for i, (source, out) in enumerate(zip(sources, (mask, straight, s2, xh2, r2, a1)))
    ]
    for copy in [*ends[0], *others[:2], *ends[1], *others[2:]] + [copy for row in ends[2:] for copy in row]:
        copy.start()
    vec[...] = jnp.zeros_like(vec)
    gain[...] = column(gain_mid)
    grad_down[...] = jnp.zeros_like(grad_down)
    others[0].wait()
    number = straight.shape[0]

    def lay(n):
        row, t = divmod(n, tiles)
        windows(fields[row % 2], mask, n * SUB, taps[n % 2], t)

    def convolve(n):
        for m in range(0, inner, inner // 2):
            rows = pl.ds(m, inner // 2)
            gzs[n % 2][rows, :] = dot(conv[rows, :], taps[n % 2][...], NN)

    def second(n, j):
        row, t = divmod(n, tiles)
        gz = gzs[n % 2]
        cols = pl.ds(j * LANES, LANES)
        place = pl.ds(t * SUB + j * LANES, LANES)
        sum_one = jnp.zeros((8, LANES), WIDE)
        sum_two = jnp.zeros((8, LANES), WIDE)
        for i in range(inner // 32):
            rows = pl.ds(i * 32, 32)
            xh = xh2[row, rows, place].astype(WIDE)
            d = gz[rows, cols] * s2[row, rows, place].astype(WIDE)
            vec[0, rows, :] += d
            vec[1, rows, :] += d * xh
            d = d * gain[rows, :]
            sum_one = sum_one + fold(d)
            sum_two = sum_two + fold(d * xh)
            gz[rows, cols] = d
        one_mean = jnp.sum(sum_one, axis=0, keepdims=True) * (1.0 / inner)
        two_mean = jnp.sum(sum_two, axis=0, keepdims=True) * (1.0 / inner)
        r = r2[row, 0:1, place]
        for i in range(inner // 32):
            rows = pl.ds(i * 32, 32)
            low = (r * (gz[rows, cols] - one_mean - xh2[row, rows, place].astype(WIDE) * two_mean)).astype(LOW)
            ghs[row][rows, place] = low
            vec[2, rows, :] += low.astype(WIDE)

    def weigh(row, part):
        size = grad_down.shape[0] // tiles
        cols = pl.ds(part * size, size)
        grad_down[cols, :] += dot(a1[pl.ds(row * span, span), cols], ghs[row][...], TT)

    def block(i):
        if i < count:
            lay(i)
        if 2 <= i < count + 2:
            for j in range(SUB // LANES):
                second(i - 2, j)
        if 1 <= i <= count:
            convolve(i - 1)
        done = i - 2 - tiles
        if done >= 0:
            weigh(*divmod(done, tiles))

    stores = []
    for i in range(count + 2 + tiles):
        if i < count and i % tiles == 0:
            row = i // tiles
            for copy in ends[row]:
                copy.wait()
            extend(one.at[row], two.at[row], got_one.at[row], got_two.at[row], odd[0], fields[row % 2])
        if i == 1:
            others[1].wait()
            for k in range(number):
                conv[:, k * inner : (k + 1) * inner] = straight[number - 1 - k]
        if i == 2:
            for copy in others[2:]:
                copy.wait()

        @pl.when(odd[0] >= 0)
        def _():
            block(i)

        if 2 <= i < count + 2 and (i - 1) % tiles == 0:
            row = (i - 2) // tiles
            stores.append(pltpu.make_async_copy(ghs[row], gh_out.at[row], sem.at[4 * groups + 6 + row]))
            stores[-1].start()
    hand_over(grad_down, side[0], sent, kept)
    lane_sums(vec, vec_out)
    for copy in stores:
        copy.wait()


def leave_kernel(gh, down, s1, xh1, r1, gain, e, gx, vec, ga):
    span, width = e.shape
    gain_row = gain[...].reshape(1, width)

    @pl.when(pl.program_id(0) == 0)
    def _():
        vec[...] = jnp.zeros_like(vec)

    def project(t):
        rows = pl.ds(t * SUB, SUB)
        ga[rows, :] = dot(gh[:, rows], down[...], TT)

    def first(i):
        rows = pl.ds(i * 16, 16)
        xh = xh1[rows, :].astype(WIDE)
        d = ga[rows, :] * s1[rows, :].astype(WIDE)
        vec[0] += fold(d)
        vec[1] += fold(d * xh)
        d = d * gain_row
        one = jnp.sum(d, axis=-1, keepdims=True) * (1.0 / width)
        two = jnp.sum(d * xh, axis=-1, keepdims=True) * (1.0 / width)
        r = r1[rows, 0:1]
        cot = e[rows, :].astype(WIDE)
        vec[2] += fold(cot)
        gx[rows, :] = (cot + r * (d - one - xh * two)).astype(LOW)

    for t in range(span // SUB):
        project(t)
        for i in range(SUB // 16):
            first(t * SUB // 16 + i)


def settle_kernel(late, *refs):
    where, one, two, source = refs[:4]
    conv, up, down = refs[4 + 3 * late : 7 + 3 * late]
    low, wide, low_down, wide_down, sem = refs[-5:]
    side, place = where[0], where[1]
    size, width = one.shape
    half, extra = conv.shape[0] // 2, up.shape[0] // 2
    rest = half - size

    loads = [
        pltpu.make_async_copy(one, low.at[place], sem.at[0]),
        pltpu.make_async_copy(two, low.at[1 - place], sem.at[1]),
        pltpu.make_async_copy(source, low_down, sem.at[2]),
    ]
    for copy in loads:
        copy.start()

    def rows(begin, count):
        return pl.ds(pl.multiple_of(begin, 64), count)

    loads[0].wait()
    loads[1].wait()
    stores = []

    def store(source, out):
        stores.append(pltpu.make_async_copy(source, out, sem.at[3 + len(stores)]))
        stores[-1].start()

    wide[0] = low[0].astype(WIDE)
    store(wide.at[0], conv.at[rows(side * half, size)])
    wide[1] = low[1].astype(WIDE)
    store(wide.at[1, pl.ds(0, rest)], conv.at[rows(side * half + size, rest)])
    for j in range(up.shape[1] // width):
        store(
            wide.at[1, pl.ds(rest + j * extra, extra)],
            up.at[rows(side * extra, extra), pl.ds(j * width, width)],
        )
    loads[2].wait()
    wide_down[...] = low_down[...].astype(WIDE)
    store(wide_down, down.at[rows(side * source.shape[0], source.shape[0])])
    for copy in stores:
        copy.wait()


def settle(pieces, down, where, half, before=()):
    size, width = pieces[0].shape
    anywhere = pl.BlockSpec(memory_space=pl.ANY)
    kinds = [jax.ShapeDtypeStruct(dims, WIDE) for dims in ((2 * half, width), (width, 2 * width), (2 * down.shape[0], width))]
    return call_once(
        "leave",
        functools.partial(settle_kernel, bool(before)),
        [pl.BlockSpec(memory_space=pltpu.SMEM)] + [anywhere] * (3 + len(before)),
        [(anywhere, kind) for kind in kinds],
        [pltpu.VMEM((2, size, width), LOW), pltpu.VMEM((2, size, width), WIDE)]
        + [pltpu.VMEM(down.shape, LOW), pltpu.VMEM(down.shape, WIDE), pltpu.SemaphoreType.DMA((8,))],
        1 << 30,
        (jnp.stack(where).astype(jnp.int32), *pieces, down, *before),
        {4 + i: i for i in range(len(before))},
    )


def call_once(name, kernel, ins, outs, scratch, flops, args, aliases={}):
    return pl.pallas_call(
        kernel,
        in_specs=ins,
        out_specs=[spec for spec, _ in outs],
        out_shape=[shape for _, shape in outs],
        scratch_shapes=scratch,
        cost_estimate=pl.CostEstimate(flops=flops, bytes_accessed=24 << 20, transcendentals=0),
        compiler_params=pltpu.CompilerParams(vmem_limit_bytes=VMEM[name] << 20),
        input_output_aliases=aliases,
    )(*args)


def call(name, kernel, steps, ins, outs, scratch, flops, args, aliases={}):
    return pl.pallas_call(
        kernel,
        grid=(steps,),
        in_specs=ins,
        out_specs=[spec for spec, _ in outs],
        out_shape=[shape for _, shape in outs],
        scratch_shapes=scratch,
        cost_estimate=pl.CostEstimate(flops=flops, bytes_accessed=24 << 20, transcendentals=0),
        compiler_params=pltpu.CompilerParams(vmem_limit_bytes=VMEM[name] << 20),
        input_output_aliases=aliases,
    )(*args)


def whole(*shape):
    return pl.BlockSpec(shape, lambda i: (0,) * len(shape), pipeline_mode=pl.Buffered(1))


def held(*shape):
    return pl.BlockSpec(shape, lambda i: (0,) * len(shape))


def swap_ends(one, two):
    count = lax.axis_size("seq")
    pairs = [(i, i ^ 1) for i in range(count)]
    other = [(i, ((i + 1) ^ 1) - 1) for i in range(1, count - 1)]
    return one, two, lax.ppermute(one, "seq", pairs), lax.ppermute(two, "seq", other)


def local(
    inputs,
    starts,
    types,
    norm_gain_in,
    norm_bias_in,
    proj_down,
    proj_down_bias,
    norm_gain_mid,
    norm_bias_mid,
    conv_weight,
    conv_bias,
    norm_gain_out,
    norm_bias_out,
    proj_up,
    proj_up_bias,
    cotangent,
):
    groups, span, width = inputs.shape
    taps, inner, _ = conv_weight.shape
    reach = taps // 2 * DILATION_STEP
    row_length = span * lax.axis_size("seq")
    first = lax.axis_index("seq") * span
    places = first - reach + jnp.arange(span + 2 * reach, dtype=jnp.int32)
    protein = jnp.sum((starts[:, None, :] <= places[None, :, None]).astype(jnp.int32), axis=2)
    inside = (places >= 0) & (places < row_length)
    centre = protein[:, reach : reach + span]
    masks = []
    for k in range(taps):
        window = slice(k * DILATION_STEP, k * DILATION_STEP + span)
        masks.append((protein[:, window] == centre) & inside[None, window])
    full = functools.reduce(jnp.logical_and, masks)
    kinds = types[:, :, None] == jnp.arange(TYPES, dtype=jnp.int32)[None, None, :]
    tally = jnp.sum((kinds & full[:, :, None]).astype(WIDE), axis=(0, 1))
    mask = jnp.stack(masks).astype(LOW).reshape(taps, 1, groups * span)
    mask = jnp.broadcast_to(mask, (taps, 16, groups * span))

    x = inputs.reshape(groups * span, width)
    e = cotangent.reshape(groups * span, width)

    parts = 2 if groups % 2 == 0 else 1
    per = groups // parts
    shape = jax.ShapeDtypeStruct

    def rows_of(size, part=0):
        return pl.BlockSpec((span, size), lambda i: (i + part * per, 0))

    def turned(size, part=0):
        return pl.BlockSpec((None, size, span), lambda i: (i + part * per, 0, 0))

    def mask_of(part=0):
        return pl.BlockSpec((taps, 16, span), lambda i: (0, 0, i + part * per))

    def clamped(part):
        def place(i):
            return (jnp.clip(i - part * per, 0, per - 1), 0, 0)

        return pl.BlockSpec((None, inner, reach), place)

    def all_rows(size, kind=LOW, part=0):
        return rows_of(size, part), shape((groups * span, size), kind)

    def all_turned(size, kind=LOW, part=0):
        return turned(size, part), shape((groups, size, span), kind)

    def sums(*dims):
        return held(*dims), shape(dims, WIDE)

    anywhere = pl.BlockSpec(memory_space=pl.ANY)
    scalar = pl.BlockSpec(memory_space=pltpu.SMEM)
    odd = (lax.axis_index("seq") & 1).reshape(1)
    core = odd
    end = pl.BlockSpec((None, inner, reach), lambda i: (i, 0, 0))
    ends = [(end, shape((per, inner, reach), LOW))] * 2
    field = pltpu.VMEM((inner, span + 2 * reach), LOW)
    block = pltpu.VMEM((inner, span), LOW)
    wide_block = pltpu.VMEM((inner, span), WIDE)
    columns = pltpu.VMEM((3, inner, LANES), WIDE)
    flops = 2 * span * inner * width

    z_rows = []
    entered = []
    for part in range(parts):
        begun = part > 0
        *entered, one, two = call(
            "enter",
            enter_kernel,
            per,
            [rows_of(width, part)] * 2
            + [scalar]
            + [whole(width)] * 2
            + [whole(inner, width), whole(width, inner)]
            + [whole(inner)] * 3
            + [anywhere] * len(entered),
            [all_rows(width, part=part)] * 3
            + [all_rows(LANES, WIDE, part)]
            + [all_turned(inner, part=part)] * 2
            + [all_turned(8, WIDE, part), all_turned(inner, WIDE, part)]
            + ends,
            [wide_block, block, columns],
            3 * per * flops,
            (x, e, odd, norm_gain_in, norm_bias_in, proj_up, proj_down)
            + (proj_down_bias, norm_gain_mid, norm_bias_mid, *entered),
            {10 + i: i for i in range(8)} if begun else {},
        )
        z_rows, entered, one, two = lax.optimization_barrier((z_rows, entered, one, two))
        z_rows.append(swap_ends(one, two))
    a1, s1, xh1, r1, s2, xh2, r2, ga3 = entered

    vec_out = []
    conv = conv_weight.reshape(taps * inner, inner)
    vector = pl.BlockSpec(memory_space=pltpu.VMEM)
    small_sums = [(vector, shape((3, inner), WIDE))]

    def low(*dims):
        return pltpu.VMEM(dims, LOW)

    def wide(*dims):
        return pltpu.VMEM(dims, WIDE)

    part_ends_out = [(anywhere, shape((per, inner, reach), LOW))] * 2
    act3 = None
    y_rows = []
    for part in range(parts):
        begun = part > 0
        act3, one, two, vec = call_once(
            "turn",
            functools.partial(turn_kernel, part),
            [anywhere] * 7 + [scalar] + [vector] * 3 + [anywhere] * begun,
            [(anywhere, shape((groups, inner, span), LOW))] + part_ends_out + small_sums,
            [low(per, inner, reach)] * 4
            + [low(taps, 16, per * span), low(taps * inner, inner), wide(per, inner, span)]
            + [low(per, inner, span)] * 2
            + [low(per, inner, reach)] * 2
            + [columns, columns, pltpu.SemaphoreType.DMA((3 + 7 * per,))]
            + [low(inner, span + 2 * reach)] * 2
            + [low(taps * inner, SUB)] * 2
            + [wide(inner, SUB)] * 4,
            3 * per * flops,
            (*z_rows[part], mask, conv, ga3, odd, conv_bias, norm_gain_out, norm_bias_out)
            + (act3,) * begun,
            {11: 0} if begun else {},
        )
        y_rows, act3, one, two = lax.optimization_barrier((y_rows, act3, one, two))
        y_rows.append(swap_ends(one, two))
        vec_out.append(vec)

    half = taps * inner // 2
    extra = inner // 2 * (width // inner)
    rows_main = -(-(half + extra) // 256) * 256

    tap_blocks = [clamped(part) for part in range(parts) for _ in range(6)] + [mask_of(), scalar, scalar]
    tap_scratch = [pltpu.VMEM((half, inner), WIDE), field, block, pltpu.VMEM((half, span), LOW)]
    main_rows = (anywhere, shape((rows_main, inner), LOW))

    def tap_args(y_ends, which):
        return [item for z_row, y_end in zip(z_rows, y_ends) for item in (*z_row, *y_end)] + [mask, odd, which]

    def grad_first(y_ends, act3):
        return call(
            "taps",
            functools.partial(first_taps_kernel, parts),
            groups,
            tap_blocks + [turned(inner), rows_of(width)],
            [main_rows] * 2,
            tap_scratch
            + [pltpu.VMEM((inner, width), WIDE), pltpu.VMEM((half, inner), LOW)]
            + [pltpu.VMEM((extra, inner), LOW)] * 2
            + [pltpu.SemaphoreType.DMA((3,))],
            2 * groups * flops,
            [*tap_args(y_ends, 1 - core), act3, e],
        )

    def grad_second(y_ends, kept):
        return call(
            "taps",
            functools.partial(second_taps_kernel, parts),
            groups,
            tap_blocks + [anywhere],
            [(held(half, inner), shape((rows_main, inner), LOW))],
            tap_scratch,
            5 * groups * flops // 4,
            [*tap_args(y_ends, core), kept],
            {6 * parts + 3: 0},
        )

    def project(act3):
        return call(
            "leave",
            output_kernel,
            groups,
            [turned(inner), rows_of(width), whole(inner, width), whole(width)],
            [all_rows(width)],
            [],
            groups * flops,
            (act3, x, proj_up, proj_up_bias),
        )

    def back(*rows):
        halves = (vector, shape((width // 2, inner), LOW))
        return call_once(
            "inner",
            functools.partial(inner_kernel, parts),
            [anywhere] * (4 * parts + 6) + [scalar] * 2 + [vector],
            [(anywhere, shape((groups, inner, span), LOW)), halves, halves] + small_sums,
            [low(groups, inner, reach)] * 4
            + [low(taps, 16, groups * span), low(taps, inner, inner)]
            + [low(groups, inner, span)] * 2
            + [wide(groups, 8, span), low(groups * span, width)]
            + [low(inner, taps * inner), columns, wide(inner, LANES), wide(width, inner)]
            + [pltpu.SemaphoreType.DMA((6 + 5 * groups,))]
            + [low(inner, span + 2 * reach)] * 2
            + [low(taps * inner, SUB)] * 2
            + [wide(inner, SUB)] * 2
            + [low(inner, span)] * groups,
            4 * groups * flops,
            (*[item for row in rows for item in row], mask, conv_weight, s2, xh2, r2, a1, odd, core, norm_gain_mid),
        )

    def leave(grad_h):
        return call(
            "leave",
            leave_kernel,
            groups,
            [turned(inner), whole(width, inner), rows_of(width), rows_of(width)]
            + [rows_of(LANES), whole(width), rows_of(width)],
            [all_rows(width), sums(3, 8, width)],
            [pltpu.VMEM((span, width), WIDE)],
            groups * flops,
            (grad_h, proj_down, s1, xh1, r1, norm_gain_in, e),
        )

    under_way = Sums()
    y_ends = [row[:2] for row in y_rows]
    sent, kept = grad_first(y_ends, act3)
    act3, y_ends, sent, kept = lax.optimization_barrier((act3, y_ends, sent, kept))
    own = []
    plan = exchange_plan(False)
    bits = bits_of(lax.axis_size("seq"))
    here = lax.axis_index("seq")
    other = (jnp.where(here & 1 == 1, here & bits[1], here & bits[-1]) != 0).astype(jnp.int32)
    under_way.add("main", sum_steps(sent, own, plan, True))
    under_way.turn(["main"], grad_second, (y_ends, kept), own)
    grad_h, sent, kept, vec_mid = under_way.turn(["main"], back, y_rows)
    own_down = [kept]
    under_way.add("down", sum_steps(sent, own_down, exchange_plan(True)))
    under_way.turn(["main", "down"])
    input_grad, vec_in = under_way.turn(["main", "down"], leave, (grad_h,))

    small_in = vec_in.sum(1)
    small_mid = vec_mid
    small_out = sum(vec_out)
    vectors = [small_in[1], small_in[0], small_mid[2], small_mid[1], small_mid[0]]
    vectors += [small_out[2], small_out[1], small_out[0], small_in[2], tally]
    ends = [0]
    for item in vectors:
        ends.append(ends[-1] + item.shape[0])
    flat = jnp.concatenate(vectors)
    flat = jnp.pad(flat, (0, -flat.shape[0] % 1024)).reshape(-1, LANES)
    under_way.add("small", small_steps(flat))
    names = ["main", "down", "small"]
    (output,) = under_way.turn(names, project, (act3,))
    sides = here & 1, plan[1][2], other

    def settle_own(pieces, down):
        return settle(pieces, down, (sides[0], sides[1]), half)

    while len(own_down) == 1 or len(own) == 1:
        under_way.turn(names)
    settled = under_way.turn(names, settle_own, (own[1], own_down[1]))

    def settle_other(pieces, down, settled):
        return settle(pieces, down, (1 - sides[0], sides[2]), half, settled)

    rest = under_way.done["main"], under_way.done["down"], settled
    settled = under_way.turn(names, settle_other, rest)
    while under_way.open:
        under_way.turn(names)
    total_conv = settled[0].reshape(taps, inner, inner)
    total_up, total_down = settled[1:]
    flat = under_way.done["small"].reshape(-1)
    totals = [flat[begin:end] for begin, end in zip(ends, ends[1:])]
    return (
        output.reshape(inputs.shape),
        input_grad.reshape(inputs.shape),
        totals[0],
        totals[1],
        total_down,
        *totals[2:5],
        total_conv,
        *totals[5:8],
        total_up,
        totals[8],
        totals[9].astype(jnp.int32),
    )


def solution(mesh):
    return jax.shard_map(
        local,
        mesh=mesh,
        in_specs=(
            P("rows", "seq", None),
            P("rows", None),
            P("rows", "seq"),
            P(),
            P(),
            P(),
            P(),
            P(),
            P(),
            P(),
            P(),
            P(),
            P(),
            P(),
            P(),
            P("rows", "seq", None),
        ),
        out_specs=(
            P("rows", "seq", None),
            P("rows", "seq", None),
            P(),
            P(),
            P(),
            P(),
            P(),
            P(),
            P(),
            P(),
            P(),
            P(),
            P(),
            P(),
            P(),
        ),
        check_vma=False,
    )
```

```python
import functools

import jax
import jax.numpy as jnp
from jax import lax
from jax.experimental import pallas as pl
from jax.experimental.pallas import tpu as pltpu
from jax.sharding import PartitionSpec as P

DILATION_STEP = 128
TYPES = 30
LANES = 128
SUB = 256
VMEM = {"enter": 60, "turn": 52, "taps": 52, "inner": 52, "leave": 52}
LOW = jnp.bfloat16
WIDE = jnp.float32
NN = (((1,), (0,)), ((), ()))
NT = (((1,), (1,)), ((), ()))
TN = (((0,), (0,)), ((), ()))
TT = (((0,), (1,)), ((), ()))


def bits_of(size):
    count = size.bit_length() - 1
    assert size == 1 << count
    return [1 << place for place in range(count)]


def xor_pairs(size, bit):
    return [(i, i ^ bit) for i in range(size)]


def exchange_plan(direct):
    seq, rows = lax.axis_size("seq"), lax.axis_size("rows")
    here, row = lax.axis_index("seq"), lax.axis_index("rows")
    plan = [("seq", [xor_pairs(seq, 1)], here & 1)]
    bits = bits_of(seq)[1:]
    if direct and len(bits) == 2:
        plan.append(("seq", [xor_pairs(seq, 2 * m) for m in range(1, 4)], here >> 1))
    else:
        for first, second in zip(bits, bits[::-1]):
            pairs = [(i, i ^ (second if i & 1 else first)) for i in range(seq)]
            place = jnp.where(here & 1 == 1, (here & second) != 0, (here & first) != 0)
            plan.append(("seq", [pairs], place.astype(jnp.int32)))
    plan.append(("rows", [xor_pairs(rows, m) for m in range(1, rows)], row))
    return plan


def in_order(pieces, place, axis=0):
    ordered = []
    for j in range(len(pieces)):
        piece = pieces[-1]
        for m in range(len(pieces) - 2, -1, -1):
            piece = jnp.where(place ^ j == m, pieces[m], piece)
        ordered.append(piece)
    return jnp.concatenate(ordered, axis=axis)


def sum_steps(sent, own, plan, early=False):
    sent = [sent]
    terms = []

    def total(begin, rows):
        return sum(lax.dynamic_slice_in_dim(term, at + begin, rows).astype(WIDE) for term, at in terms)

    for step, (axis, pairs, _) in enumerate(plan):
        got = yield sent, axis, pairs
        if step == 0:
            terms.append((own[0], 0))
            rows = own[0].shape[0]
        terms.extend((piece, 0) for piece in got)
        if step + 1 < len(plan):
            _, coming, place = plan[step + 1]
            rows //= len(coming) + 1
            sent = [total((place ^ m) * rows, rows).astype(LOW) for m in range(1, len(coming) + 1)]
            terms = [(term, at + place * rows) for term, at in terms]
    cells = total(0, rows).astype(LOW)
    core_axis, (core_pairs,), _ = plan[0]
    if early:
        for axis, pairs, place in plan[:1:-1]:
            got = yield [cells] * len(pairs), axis, pairs
            cells = in_order([cells, *got], place)
        axis, pairs, place = plan[1]
        first, second = yield [cells, cells], axis, [*pairs, core_pairs]
        own.append((cells, first))
        (third,) = yield [first], core_axis, [core_pairs]
        return second, third
    width = cells.shape[-1]
    cells = cells[None]
    for axis, pairs, place in plan[1:]:
        lead, size, _ = cells.shape
        got = yield [cells.reshape(-1, width)] * len(pairs), axis, pairs
        cells = in_order([cells, *[piece.reshape(cells.shape) for piece in got]], place, 1)
        cells = cells.reshape(-1, size, width)
    cells = cells.reshape(-1, width)
    own.append(cells)
    (got,) = yield [cells], core_axis, [core_pairs]
    return got


def small_steps(cells):
    first, *others = [("seq", bit) for bit in bits_of(lax.axis_size("seq"))]
    for axis, bit in [first, *[("rows", bit) for bit in bits_of(lax.axis_size("rows"))], *others]:
        (got,) = yield [cells], axis, [xor_pairs(lax.axis_size(axis), bit)]
        cells = cells + got
    return cells


class Sums:
    def __init__(self):
        self.open = {}
        self.done = {}

    def add(self, name, steps):
        self.open[name] = (steps, next(steps))

    def turn(self, names, work=None, gate=(), own=None):
        names = [name for name in names if name in self.open]
        sent = [self.open[name][1][0] for name in names]
        sent, gate = lax.optimization_barrier((sent, gate))
        got = []
        for name, cells in zip(names, sent):
            _, axis, pairs = self.open[name][1]
            got.append([lax.ppermute(cell, axis, pair) for cell, pair in zip(cells, pairs)])
        made = work(*gate) if work else ()
        got, made = lax.optimization_barrier((got, made))
        if own is not None:
            own.extend(made)
        for name, cells in zip(names, got):
            steps = self.open.pop(name)[0]
            try:
                self.open[name] = (steps, steps.send(cells))
            except StopIteration as end:
                self.done[name] = end.value
        return made


def dot(left, right, dims):
    return lax.dot_general(left, right, dims, preferred_element_type=WIDE)


def gelu_parts(u):
    phi = 0.5 + 0.5 * lax.erf(u * 0.7071067811865476)
    bell = jnp.exp2(u * u * -0.7213475204444817)
    return u * phi, phi + (u * 0.3989422804014327) * bell


def fold(values):
    return jnp.sum(values.reshape(-1, 8, values.shape[-1]), axis=0)


def column_mean(rows, count):
    total = jnp.zeros((8, LANES), WIDE)
    for i in range(count // 64):
        total = total + fold(rows(i))
    return jnp.sum(total, axis=0, keepdims=True) * (1.0 / count)


def column(vector):
    size = vector.shape[0]
    return jnp.broadcast_to(vector[...].reshape(1, size), (LANES, size)).T


def enter_kernel(*refs):
    x, e, odd, gain, bias, up, down, down_bias, gain_mid, bias_mid = refs[:10]
    a1, s1, xh1, r1, s2, xh2, r2, ga3, z_one, z_two, h, z, mid = refs[-13:]
    span, width = x.shape
    inner = h.shape[0]
    gain_row, bias_row = gain[...].reshape(1, width), bias[...].reshape(1, width)

    @pl.when(pl.program_id(0) == 0)
    def _():
        mid[0] = column(down_bias)
        mid[1] = column(gain_mid)
        mid[2] = column(bias_mid)

    def first(i):
        rows = pl.ds(i * 16, 16)
        v = x[rows, :].astype(WIDE)
        v = v - jnp.sum(v, axis=-1, keepdims=True) * (1.0 / width)
        r = lax.rsqrt(jnp.sum(v * v, axis=-1, keepdims=True) * (1.0 / width) + 1e-05)
        xh = v * r
        act, slope = gelu_parts(xh * gain_row + bias_row)
        a1[rows, :] = act.astype(LOW)
        s1[rows, :] = slope.astype(LOW)
        xh1[rows, :] = xh.astype(LOW)
        r1[rows, :] = jnp.broadcast_to(r, (16, LANES))

    def project(t):
        cols = pl.ds(t * SUB, SUB)
        product = dot(down[...], a1[cols, :], TT)
        for j in range(SUB // LANES):
            h[:, pl.ds(t * SUB + j * LANES, LANES)] = product[:, j * LANES : (j + 1) * LANES] + mid[0]
        ga3[:, cols] = dot(up[...], e[cols, :], NT)

    def second(j):
        cols = pl.ds(j * LANES, LANES)
        m = column_mean(lambda i: h[pl.ds(i * 64, 64), cols], inner)

        def squares(i):
            c = h[pl.ds(i * 64, 64), cols] - m
            return c * c

        r = lax.rsqrt(column_mean(squares, inner) + 1e-05)
        for i in range(inner // 32):
            rows = pl.ds(i * 32, 32)
            xh = (h[rows, cols] - m) * r
            act, slope = gelu_parts(xh * mid[1, rows, :] + mid[2, rows, :])
            z[rows, cols] = act.astype(LOW)
            s2[rows, cols] = slope.astype(LOW)
            xh2[rows, cols] = xh.astype(LOW)
        r2[:, cols] = jnp.broadcast_to(r, (8, LANES))

    for t in range(span // SUB):
        for i in range(SUB // 16):
            first(t * SUB // 16 + i)
        project(t)
        if t:
            for j in range(SUB // LANES):
                second((t - 1) * SUB // LANES + j)
    for j in range(SUB // LANES):
        second((span // SUB - 1) * SUB // LANES + j)
    part_ends(z, odd[0], z_one, z_two)


def at(place, size):
    return pl.ds(pl.multiple_of(place, LANES), size)


def part_ends(cells, odd, one, two):
    half = one.shape[1]
    one[...] = cells[:, at((1 - odd) * half, half)]
    two[...] = cells[:, at(odd * half, half)]


def join_ends(one, two, odd, out, begin):
    half = one.shape[1]
    out[:, at(begin + (1 - odd) * half, half)] = one[...]
    out[:, at(begin + odd * half, half)] = two[...]


def extend(one, two, got_one, got_two, odd, out):
    half = one.shape[1]
    join_ends(one, two, odd, out, half)
    out[:, at((1 - odd) * 3 * half, half)] = got_one[...]
    out[:, at(odd * 3 * half, half)] = got_two[...]


def windows(field, mask, first, out, t):
    inner = field.shape[0]
    taps = mask.shape[0]
    for k in range(taps):
        source = field[:, pl.ds(t * SUB + k * LANES, SUB)]
        if k != taps // 2:
            source = (source.reshape(-1, 16, SUB) * mask[k, :, pl.ds(first, SUB)][None]).reshape(inner, SUB)
        out[k * inner : (k + 1) * inner, :] = source


def lane_sums(vec, out):
    for k in range(vec.shape[0]):
        out[k : k + 1, :] = jnp.sum(vec[k].T, axis=0, keepdims=True)


def in_blocks(count, always, body):
    for i in range(count):

        @pl.when(always)
        def _():
            body(i)


def turn_kernel(begun, *refs):
    sources = refs[:7]
    odd, conv_bias, gain_out, bias_out = refs[7:11]
    refs = refs[11 + begun :]
    act_out, one_out, two_out, vec_out = refs[:4]
    one, two, got_one, got_two, mask, conv, ga3, *refs = refs[4:]
    act3, gy, gy_one, gy_two, vec, out3, sem = refs[:7]
    fields, taps, dys, xhs = refs[7:9], refs[9:11], refs[11:13], refs[13:15]
    part = int(begun)
    rows_here, inner, span = gy.shape
    tiles = span // SUB
    count = rows_here * tiles

    def load(i, source, out):
        return pltpu.make_async_copy(source, out, sem.at[i])

    first_row = part * rows_here
    end_refs = (one, two, got_one, got_two)
    ends = [
        [load(4 * row + i, source.at[row], out.at[row]) for i, (source, out) in enumerate(zip(sources[:4], end_refs))]
        for row in range(rows_here)
    ]
    others = [
        load(4 * rows_here, sources[4].at[:, :, pl.ds(first_row * span, rows_here * span)], mask),
        load(4 * rows_here + 1, sources[5], conv),
        load(4 * rows_here + 2, sources[6].at[pl.ds(first_row, rows_here)], ga3),
    ]
    for copy in [*ends[0], *others[:2]] + [copy for row in ends[1:] for copy in row] + others[2:]:
        copy.start()
    vec[...] = jnp.zeros_like(vec)
    out3[0] = column(conv_bias)
    out3[1] = column(gain_out)
    out3[2] = column(bias_out)
    others[0].wait()

    def lay(n):
        row, t = divmod(n, tiles)
        windows(fields[row % 2], mask, n * SUB, taps[n % 2], t)

    def convolve(n):
        product = dot(conv[...], taps[n % 2][...], TN)
        for j in range(SUB // LANES):
            dys[n % 2][:, pl.ds(j * LANES, LANES)] = product[:, j * LANES : (j + 1) * LANES] + out3[0]

    def third(n, j):
        row, t = divmod(n, tiles)
        dy, xh3 = dys[n % 2], xhs[n % 2]
        cols = pl.ds(j * LANES, LANES)
        place = pl.ds(t * SUB + j * LANES, LANES)
        m = column_mean(lambda i: dy[pl.ds(i * 64, 64), cols], inner)

        def squares(i):
            c = dy[pl.ds(i * 64, 64), cols] - m
            return c * c

        r = lax.rsqrt(column_mean(squares, inner) + 1e-05)
        sum_one = jnp.zeros((8, LANES), WIDE)
        sum_two = jnp.zeros((8, LANES), WIDE)
        for i in range(inner // 32):
            rows = pl.ds(i * 32, 32)
            gain = out3[1, rows, :]
            xh = (dy[rows, cols] - m) * r
            act, slope = gelu_parts(xh * gain + out3[2, rows, :])
            act3[row, rows, place] = act.astype(LOW)
            d = ga3[row, rows, place] * slope
            vec[0, rows, :] += d
            vec[1, rows, :] += d * xh
            d = d * gain
            sum_one = sum_one + fold(d)
            sum_two = sum_two + fold(d * xh)
            dy[rows, cols] = d
            xh3[rows, cols] = xh
        one_mean = jnp.sum(sum_one, axis=0, keepdims=True) * (1.0 / inner)
        two_mean = jnp.sum(sum_two, axis=0, keepdims=True) * (1.0 / inner)
        for i in range(inner // 32):
            rows = pl.ds(i * 32, 32)
            low = (r * (dy[rows, cols] - one_mean - xh3[rows, cols] * two_mean)).astype(LOW)
            gy[row, rows, place] = low
            vec[2, rows, :] += low.astype(WIDE)

    stores = []

    def block(i):
        if i < count:
            lay(i)
        if 2 <= i:
            for j in range(SUB // LANES):
                third(i - 2, j)
        if 1 <= i <= count:
            convolve(i - 1)

    for i in range(count + 2):
        if i < count and i % tiles == 0:
            row = i // tiles
            for copy in ends[row]:
                copy.wait()
            extend(one.at[row], two.at[row], got_one.at[row], got_two.at[row], odd[0], fields[row % 2])
        if i == 1:
            others[1].wait()
        if i == 2:
            others[2].wait()

        @pl.when(odd[0] >= 0)
        def _():
            block(i)

        if i >= 2 and (i - 1) % tiles == 0:
            row = (i - 2) // tiles
            part_ends(gy.at[row], odd[0], gy_one.at[row], gy_two.at[row])
            for k, (source, out) in enumerate(
                ((act3, act_out.at[first_row + row]), (gy_one, one_out.at[row]), (gy_two, two_out.at[row]))
            ):
                stores.append(load(4 * rows_here + 3 + 3 * row + k, source.at[row], out))
                stores[-1].start()
    lane_sums(vec, vec_out)
    for copy in stores:
        copy.wait()


def by_part(parts, refs, body):
    step = pl.program_id(0)
    per = pl.num_programs(0) // parts
    count = len(refs) // parts
    for part in range(parts):

        @pl.when((step >= part * per) & (step < (part + 1) * per))
        def _():
            body(*refs[part * count : (part + 1) * count])


def hand_over(total, side, sent, kept):
    half = kept.shape[0]
    sent[...] = total[pl.ds(pl.multiple_of((1 - side) * half, half), half), :].astype(LOW)
    kept[...] = total[pl.ds(pl.multiple_of(side * half, half), half), :].astype(kept.dtype)


def output_kernel(act3, x, up, up_bias, y):
    span, width = x.shape
    for t in range(span // SUB):
        rows = pl.ds(t * SUB, SUB)
        product = dot(act3[:, rows], up[...], TN)
        y[rows, :] = (x[rows, :].astype(WIDE) + product + up_bias[...].reshape(1, width)).astype(LOW)


def taps_step(parts, ends, mask, odd, which, total, field, gy, taps):
    inner, span = gy.shape
    half = inner // 2
    count = mask.shape[0] // 2
    h = which[0]

    def place(rows, source, tap):
        cells = field[source, at(tap * LANES, span)]
        size = cells.shape[0]
        taps[rows, :] = (cells.reshape(-1, 16, span) * mask[tap][None]).reshape(size, span)

    def body(one, two, got_one, got_two, gy_one, gy_two):
        extend(one, two, got_one, got_two, odd[0], field)
        join_ends(gy_one, gy_two, odd[0], gy, 0)

    by_part(parts, ends, body)
    for j in range(count):
        rows = pl.ds(pl.multiple_of(h * half + j * inner, 16), inner)
        place(rows, slice(None), h * (count + 1) + j)
    rows = pl.ds(pl.multiple_of((1 - h) * count * inner, 16), half)
    place(rows, pl.ds(pl.multiple_of(h * half, 16), half), jnp.int32(count))
    total[...] += dot(taps[...], gy[...], NT)


def first_taps_kernel(parts, *refs):
    mask, odd, which, act3, e = refs[6 * parts : 6 * parts + 5]
    sent, kept, total, field, gy, taps, total_up, low, low_one, low_two, sem = refs[-11:]
    half, width = total_up.shape[0] // 2, low_one.shape[1]

    @pl.when(pl.program_id(0) == 0)
    def _():
        total[...] = jnp.zeros_like(total)
        total_up[...] = jnp.zeros_like(total_up)

    taps_step(parts, refs[: 6 * parts], mask, odd, which, total, field, gy, taps)
    total_up[...] += dot(act3[...], e[...], NN)

    @pl.when(pl.program_id(0) == pl.num_programs(0) - 1)
    def _():
        other = which[0]
        low[...] = total[...].astype(LOW)
        rows = low.shape[0]
        copies = [pltpu.make_async_copy(low, sent.at[pl.ds(0, rows)], sem.at[0])]
        copies[0].start()
        for j in range(total_up.shape[1] // width):
            cols = pl.ds(j * width, width)
            place = pl.ds(j * half, half)
            low_one[place, :] = total_up[pl.ds(pl.multiple_of(other * half, half), half), cols].astype(LOW)
            low_two[place, :] = total_up[pl.ds(pl.multiple_of((1 - other) * half, half), half), cols].astype(LOW)
        place = pl.ds(rows, low_one.shape[0])
        copies.append(pltpu.make_async_copy(low_one, sent.at[place], sem.at[1]))
        copies.append(pltpu.make_async_copy(low_two, kept.at[place], sem.at[2]))
        for copy in copies[1:]:
            copy.start()
        for copy in copies:
            copy.wait()


def second_taps_kernel(parts, *refs):
    mask, odd, which = refs[6 * parts : 6 * parts + 3]
    out, total, field, gy, taps = refs[-5:]

    @pl.when(pl.program_id(0) == 0)
    def _():
        total[...] = jnp.zeros_like(total)

    taps_step(parts, refs[: 6 * parts], mask, odd, which, total, field, gy, taps)

    @pl.when(pl.program_id(0) == pl.num_programs(0) - 1)
    def _():
        out[...] = total[...].astype(out.dtype)


def inner_kernel(parts, *refs):
    per = refs[0].shape[0]
    here = 4 * parts
    sources = refs[here : here + 6]
    odd, side, gain_mid = refs[here + 6 : here + 9]
    gh_out, sent, kept, vec_out = refs[here + 9 : here + 13]
    end_sources = [refs[4 * part : 4 * part + 4] for part in range(parts)]
    one, two, got_one, got_two, mask, straight, s2, xh2, r2, a1, *refs = refs[here + 13 :]
    conv, vec, gain, grad_down, sem = refs[:5]
    fields, taps, gzs, ghs = refs[5:7], refs[7:9], refs[9:11], refs[11:]
    groups, inner, span = s2.shape
    tiles = span // SUB
    count = groups * tiles

    end_refs = (one, two, got_one, got_two)
    ends = [
        [
            pltpu.make_async_copy(source.at[row % per], out.at[row], sem.at[4 * row + i])
            for i, (source, out) in enumerate(zip(end_sources[row // per], end_refs))
        ]
        for row in range(groups)
    ]
    others = [
        pltpu.make_async_copy(source, out, sem.at[4 * groups + i])
        for i, (source, out) in enumerate(zip(sources, (mask, straight, s2, xh2, r2, a1)))
    ]
    for copy in [*ends[0], *others[:2], *ends[1], *others[2:]] + [copy for row in ends[2:] for copy in row]:
        copy.start()
    vec[...] = jnp.zeros_like(vec)
    gain[...] = column(gain_mid)
    grad_down[...] = jnp.zeros_like(grad_down)
    others[0].wait()
    number = straight.shape[0]

    def lay(n):
        row, t = divmod(n, tiles)
        windows(fields[row % 2], mask, n * SUB, taps[n % 2], t)

    def convolve(n):
        for m in range(0, inner, inner // 2):
            rows = pl.ds(m, inner // 2)
            gzs[n % 2][rows, :] = dot(conv[rows, :], taps[n % 2][...], NN)

    def second(n, j):
        row, t = divmod(n, tiles)
        gz = gzs[n % 2]
        cols = pl.ds(j * LANES, LANES)
        place = pl.ds(t * SUB + j * LANES, LANES)
        sum_one = jnp.zeros((8, LANES), WIDE)
        sum_two = jnp.zeros((8, LANES), WIDE)
        for i in range(inner // 32):
            rows = pl.ds(i * 32, 32)
            xh = xh2[row, rows, place].astype(WIDE)
            d = gz[rows, cols] * s2[row, rows, place].astype(WIDE)
            vec[0, rows, :] += d
            vec[1, rows, :] += d * xh
            d = d * gain[rows, :]
            sum_one = sum_one + fold(d)
            sum_two = sum_two + fold(d * xh)
            gz[rows, cols] = d
        one_mean = jnp.sum(sum_one, axis=0, keepdims=True) * (1.0 / inner)
        two_mean = jnp.sum(sum_two, axis=0, keepdims=True) * (1.0 / inner)
        r = r2[row, 0:1, place]
        for i in range(inner // 32):
            rows = pl.ds(i * 32, 32)
            low = (r * (gz[rows, cols] - one_mean - xh2[row, rows, place].astype(WIDE) * two_mean)).astype(LOW)
            ghs[row][rows, place] = low
            vec[2, rows, :] += low.astype(WIDE)

    def weigh(row, part):
        size = grad_down.shape[0] // tiles
        cols = pl.ds(part * size, size)
        grad_down[cols, :] += dot(a1[pl.ds(row * span, span), cols], ghs[row][...], TT)

    def block(i):
        if i < count:
            lay(i)
        if 2 <= i < count + 2:
            for j in range(SUB // LANES):
                second(i - 2, j)
        if 1 <= i <= count:
            convolve(i - 1)
        done = i - 2 - tiles
        if done >= 0:
            weigh(*divmod(done, tiles))

    stores = []
    for i in range(count + 2 + tiles):
        if i < count and i % tiles == 0:
            row = i // tiles
            for copy in ends[row]:
                copy.wait()
            extend(one.at[row], two.at[row], got_one.at[row], got_two.at[row], odd[0], fields[row % 2])
        if i == 1:
            others[1].wait()
            for k in range(number):
                conv[:, k * inner : (k + 1) * inner] = straight[number - 1 - k]
        if i == 2:
            for copy in others[2:]:
                copy.wait()

        @pl.when(odd[0] >= 0)
        def _():
            block(i)

        if 2 <= i < count + 2 and (i - 1) % tiles == 0:
            row = (i - 2) // tiles
            stores.append(pltpu.make_async_copy(ghs[row], gh_out.at[row], sem.at[4 * groups + 6 + row]))
            stores[-1].start()
    hand_over(grad_down, side[0], sent, kept)
    lane_sums(vec, vec_out)
    for copy in stores:
        copy.wait()


def leave_kernel(gh, down, s1, xh1, r1, gain, e, gx, vec, ga):
    span, width = e.shape
    gain_row = gain[...].reshape(1, width)

    @pl.when(pl.program_id(0) == 0)
    def _():
        vec[...] = jnp.zeros_like(vec)

    def project(t):
        rows = pl.ds(t * SUB, SUB)
        ga[rows, :] = dot(gh[:, rows], down[...], TT)

    def first(i):
        rows = pl.ds(i * 16, 16)
        xh = xh1[rows, :].astype(WIDE)
        d = ga[rows, :] * s1[rows, :].astype(WIDE)
        vec[0] += fold(d)
        vec[1] += fold(d * xh)
        d = d * gain_row
        one = jnp.sum(d, axis=-1, keepdims=True) * (1.0 / width)
        two = jnp.sum(d * xh, axis=-1, keepdims=True) * (1.0 / width)
        r = r1[rows, 0:1]
        cot = e[rows, :].astype(WIDE)
        vec[2] += fold(cot)
        gx[rows, :] = (cot + r * (d - one - xh * two)).astype(LOW)

    for t in range(span // SUB):
        project(t)
        for i in range(SUB // 16):
            first(t * SUB // 16 + i)


def settle_kernel(late, *refs):
    where, one, two, source = refs[:4]
    conv, up, down = refs[4 + 3 * late : 7 + 3 * late]
    low, wide, low_down, wide_down, sem = refs[-5:]
    side, place = where[0], where[1]
    size, width = one.shape
    half, extra = conv.shape[0] // 2, up.shape[0] // 2
    rest = half - size

    cut_at = size // 2

    def load(i, source, out, begin, count):
        piece = pl.ds(begin, count)
        return pltpu.make_async_copy(source.at[piece], out.at[piece], sem.at[i])

    loads = [
        load(0, one, low.at[place], 0, cut_at),
        load(1, two, low.at[1 - place], 0, cut_at),
        load(2, one, low.at[place], cut_at, size - cut_at),
        load(3, two, low.at[1 - place], cut_at, size - cut_at),
        load(4, source, low_down, 0, source.shape[0]),
    ]
    for copy in loads:
        copy.start()

    def rows(begin, count):
        return pl.ds(pl.multiple_of(begin, 64), count)

    stores = []

    def store(piece, begin, count, out):
        here = pl.ds(begin, count)
        if piece < 2:
            wide[piece, here, :] = low[piece, here, :].astype(WIDE)
            ready = wide.at[piece, here]
        else:
            wide_down[here, :] = low_down[here, :].astype(WIDE)
            ready = wide_down.at[here]
        stores.append(pltpu.make_async_copy(ready, out, sem.at[len(loads) + len(stores)]))
        stores[-1].start()

    loads[0].wait()
    loads[1].wait()
    store(0, 0, cut_at, conv.at[rows(side * half, cut_at)])
    store(1, 0, rest, conv.at[rows(side * half + size, rest)])
    loads[2].wait()
    loads[3].wait()
    store(0, cut_at, size - cut_at, conv.at[rows(side * half + cut_at, size - cut_at)])
    for j in range(up.shape[1] // width):
        place_up = up.at[rows(side * extra, extra), pl.ds(j * width, width)]
        store(1, rest + j * extra, extra, place_up)
    loads[4].wait()
    count = source.shape[0] // 2
    for j in range(2):
        store(2, j * count, count, down.at[rows(side * source.shape[0] + j * count, count)])
    for copy in stores:
        copy.wait()


def settle(pieces, down, where, half, before=()):
    size, width = pieces[0].shape
    anywhere = pl.BlockSpec(memory_space=pl.ANY)
    kinds = [jax.ShapeDtypeStruct(dims, WIDE) for dims in ((2 * half, width), (width, 2 * width), (2 * down.shape[0], width))]
    return call_once(
        "leave",
        functools.partial(settle_kernel, bool(before)),
        [pl.BlockSpec(memory_space=pltpu.SMEM)] + [anywhere] * (3 + len(before)),
        [(anywhere, kind) for kind in kinds],
        [pltpu.VMEM((2, size, width), LOW), pltpu.VMEM((2, size, width), WIDE)]
        + [pltpu.VMEM(down.shape, LOW), pltpu.VMEM(down.shape, WIDE), pltpu.SemaphoreType.DMA((12,))],
        1 << 30,
        (jnp.stack(where).astype(jnp.int32), *pieces, down, *before),
        {4 + i: i for i in range(len(before))},
    )


def call_once(name, kernel, ins, outs, scratch, flops, args, aliases={}):
    return pl.pallas_call(
        kernel,
        in_specs=ins,
        out_specs=[spec for spec, _ in outs],
        out_shape=[shape for _, shape in outs],
        scratch_shapes=scratch,
        cost_estimate=pl.CostEstimate(flops=flops, bytes_accessed=24 << 20, transcendentals=0),
        compiler_params=pltpu.CompilerParams(vmem_limit_bytes=VMEM[name] << 20),
        input_output_aliases=aliases,
    )(*args)


def call(name, kernel, steps, ins, outs, scratch, flops, args, aliases={}):
    return pl.pallas_call(
        kernel,
        grid=(steps,),
        in_specs=ins,
        out_specs=[spec for spec, _ in outs],
        out_shape=[shape for _, shape in outs],
        scratch_shapes=scratch,
        cost_estimate=pl.CostEstimate(flops=flops, bytes_accessed=24 << 20, transcendentals=0),
        compiler_params=pltpu.CompilerParams(vmem_limit_bytes=VMEM[name] << 20),
        input_output_aliases=aliases,
    )(*args)


def whole(*shape):
    return pl.BlockSpec(shape, lambda i: (0,) * len(shape), pipeline_mode=pl.Buffered(1))


def held(*shape):
    return pl.BlockSpec(shape, lambda i: (0,) * len(shape))


def swap_ends(one, two):
    count = lax.axis_size("seq")
    pairs = [(i, i ^ 1) for i in range(count)]
    other = [(i, ((i + 1) ^ 1) - 1) for i in range(1, count - 1)]
    return one, two, lax.ppermute(one, "seq", pairs), lax.ppermute(two, "seq", other)


def local(
    inputs,
    starts,
    types,
    norm_gain_in,
    norm_bias_in,
    proj_down,
    proj_down_bias,
    norm_gain_mid,
    norm_bias_mid,
    conv_weight,
    conv_bias,
    norm_gain_out,
    norm_bias_out,
    proj_up,
    proj_up_bias,
    cotangent,
):
    groups, span, width = inputs.shape
    taps, inner, _ = conv_weight.shape
    reach = taps // 2 * DILATION_STEP
    row_length = span * lax.axis_size("seq")
    first = lax.axis_index("seq") * span
    places = first - reach + jnp.arange(span + 2 * reach, dtype=jnp.int32)
    protein = jnp.sum((starts[:, None, :] <= places[None, :, None]).astype(jnp.int32), axis=2)
    inside = (places >= 0) & (places < row_length)
    centre = protein[:, reach : reach + span]
    masks = []
    for k in range(taps):
        window = slice(k * DILATION_STEP, k * DILATION_STEP + span)
        masks.append((protein[:, window] == centre) & inside[None, window])
    full = functools.reduce(jnp.logical_and, masks)
    kinds = types[:, :, None] == jnp.arange(TYPES, dtype=jnp.int32)[None, None, :]
    tally = jnp.sum((kinds & full[:, :, None]).astype(WIDE), axis=(0, 1))
    mask = jnp.stack(masks).astype(LOW).reshape(taps, 1, groups * span)
    mask = jnp.broadcast_to(mask, (taps, 16, groups * span))

    x = inputs.reshape(groups * span, width)
    e = cotangent.reshape(groups * span, width)

    parts = 2 if groups % 2 == 0 else 1
    per = groups // parts
    shape = jax.ShapeDtypeStruct

    def rows_of(size, part=0):
        return pl.BlockSpec((span, size), lambda i: (i + part * per, 0))

    def turned(size, part=0):
        return pl.BlockSpec((None, size, span), lambda i: (i + part * per, 0, 0))

    def mask_of(part=0):
        return pl.BlockSpec((taps, 16, span), lambda i: (0, 0, i + part * per))

    def clamped(part):
        def place(i):
            return (jnp.clip(i - part * per, 0, per - 1), 0, 0)

        return pl.BlockSpec((None, inner, reach), place)

    def all_rows(size, kind=LOW, part=0):
        return rows_of(size, part), shape((groups * span, size), kind)

    def all_turned(size, kind=LOW, part=0):
        return turned(size, part), shape((groups, size, span), kind)

    def sums(*dims):
        return held(*dims), shape(dims, WIDE)

    anywhere = pl.BlockSpec(memory_space=pl.ANY)
    scalar = pl.BlockSpec(memory_space=pltpu.SMEM)
    odd = (lax.axis_index("seq") & 1).reshape(1)
    core = odd
    end = pl.BlockSpec((None, inner, reach), lambda i: (i, 0, 0))
    ends = [(end, shape((per, inner, reach), LOW))] * 2
    field = pltpu.VMEM((inner, span + 2 * reach), LOW)
    block = pltpu.VMEM((inner, span), LOW)
    wide_block = pltpu.VMEM((inner, span), WIDE)
    columns = pltpu.VMEM((3, inner, LANES), WIDE)
    flops = 2 * span * inner * width

    z_rows = []
    entered = []
    for part in range(parts):
        begun = part > 0
        *entered, one, two = call(
            "enter",
            enter_kernel,
            per,
            [rows_of(width, part)] * 2
            + [scalar]
            + [whole(width)] * 2
            + [whole(inner, width), whole(width, inner)]
            + [whole(inner)] * 3
            + [anywhere] * len(entered),
            [all_rows(width, part=part)] * 3
            + [all_rows(LANES, WIDE, part)]
            + [all_turned(inner, part=part)] * 2
            + [all_turned(8, WIDE, part), all_turned(inner, WIDE, part)]
            + ends,
            [wide_block, block, columns],
            3 * per * flops,
            (x, e, odd, norm_gain_in, norm_bias_in, proj_up, proj_down)
            + (proj_down_bias, norm_gain_mid, norm_bias_mid, *entered),
            {10 + i: i for i in range(8)} if begun else {},
        )
        z_rows, entered, one, two = lax.optimization_barrier((z_rows, entered, one, two))
        z_rows.append(swap_ends(one, two))
    a1, s1, xh1, r1, s2, xh2, r2, ga3 = entered

    vec_out = []
    conv = conv_weight.reshape(taps * inner, inner)
    vector = pl.BlockSpec(memory_space=pltpu.VMEM)
    small_sums = [(vector, shape((3, inner), WIDE))]

    def low(*dims):
        return pltpu.VMEM(dims, LOW)

    def wide(*dims):
        return pltpu.VMEM(dims, WIDE)

    part_ends_out = [(anywhere, shape((per, inner, reach), LOW))] * 2
    act3 = None
    y_rows = []
    for part in range(parts):
        begun = part > 0
        act3, one, two, vec = call_once(
            "turn",
            functools.partial(turn_kernel, part),
            [anywhere] * 7 + [scalar] + [vector] * 3 + [anywhere] * begun,
            [(anywhere, shape((groups, inner, span), LOW))] + part_ends_out + small_sums,
            [low(per, inner, reach)] * 4
            + [low(taps, 16, per * span), low(taps * inner, inner), wide(per, inner, span)]
            + [low(per, inner, span)] * 2
            + [low(per, inner, reach)] * 2
            + [columns, columns, pltpu.SemaphoreType.DMA((3 + 7 * per,))]
            + [low(inner, span + 2 * reach)] * 2
            + [low(taps * inner, SUB)] * 2
            + [wide(inner, SUB)] * 4,
            3 * per * flops,
            (*z_rows[part], mask, conv, ga3, odd, conv_bias, norm_gain_out, norm_bias_out)
            + (act3,) * begun,
            {11: 0} if begun else {},
        )
        y_rows, act3, one, two = lax.optimization_barrier((y_rows, act3, one, two))
        y_rows.append(swap_ends(one, two))
        vec_out.append(vec)

    half = taps * inner // 2
    extra = inner // 2 * (width // inner)
    rows_main = -(-(half + extra) // 256) * 256

    tap_blocks = [clamped(part) for part in range(parts) for _ in range(6)] + [mask_of(), scalar, scalar]
    tap_scratch = [pltpu.VMEM((half, inner), WIDE), field, block, pltpu.VMEM((half, span), LOW)]
    main_rows = (anywhere, shape((rows_main, inner), LOW))

    def tap_args(y_ends, which):
        return [item for z_row, y_end in zip(z_rows, y_ends) for item in (*z_row, *y_end)] + [mask, odd, which]

    def grad_first(y_ends, act3):
        return call(
            "taps",
            functools.partial(first_taps_kernel, parts),
            groups,
            tap_blocks + [turned(inner), rows_of(width)],
            [main_rows] * 2,
            tap_scratch
            + [pltpu.VMEM((inner, width), WIDE), pltpu.VMEM((half, inner), LOW)]
            + [pltpu.VMEM((extra, inner), LOW)] * 2
            + [pltpu.SemaphoreType.DMA((3,))],
            2 * groups * flops,
            [*tap_args(y_ends, 1 - core), act3, e],
        )

    def grad_second(y_ends, kept):
        return call(
            "taps",
            functools.partial(second_taps_kernel, parts),
            groups,
            tap_blocks + [anywhere],
            [(held(half, inner), shape((rows_main, inner), LOW))],
            tap_scratch,
            5 * groups * flops // 4,
            [*tap_args(y_ends, core), kept],
            {6 * parts + 3: 0},
        )

    def project(act3):
        return call(
            "leave",
            output_kernel,
            groups,
            [turned(inner), rows_of(width), whole(inner, width), whole(width)],
            [all_rows(width)],
            [],
            groups * flops,
            (act3, x, proj_up, proj_up_bias),
        )

    def back(*rows):
        halves = (vector, shape((width // 2, inner), LOW))
        return call_once(
            "inner",
            functools.partial(inner_kernel, parts),
            [anywhere] * (4 * parts + 6) + [scalar] * 2 + [vector],
            [(anywhere, shape((groups, inner, span), LOW)), halves, halves] + small_sums,
            [low(groups, inner, reach)] * 4
            + [low(taps, 16, groups * span), low(taps, inner, inner)]
            + [low(groups, inner, span)] * 2
            + [wide(groups, 8, span), low(groups * span, width)]
            + [low(inner, taps * inner), columns, wide(inner, LANES), wide(width, inner)]
            + [pltpu.SemaphoreType.DMA((6 + 5 * groups,))]
            + [low(inner, span + 2 * reach)] * 2
            + [low(taps * inner, SUB)] * 2
            + [wide(inner, SUB)] * 2
            + [low(inner, span)] * groups,
            4 * groups * flops,
            (*[item for row in rows for item in row], mask, conv_weight, s2, xh2, r2, a1, odd, core, norm_gain_mid),
        )

    def leave(grad_h):
        return call(
            "leave",
            leave_kernel,
            groups,
            [turned(inner), whole(width, inner), rows_of(width), rows_of(width)]
            + [rows_of(LANES), whole(width), rows_of(width)],
            [all_rows(width), sums(3, 8, width)],
            [pltpu.VMEM((span, width), WIDE)],
            groups * flops,
            (grad_h, proj_down, s1, xh1, r1, norm_gain_in, e),
        )

    under_way = Sums()
    y_ends = [row[:2] for row in y_rows]
    sent, kept = grad_first(y_ends, act3)
    act3, y_ends, sent, kept = lax.optimization_barrier((act3, y_ends, sent, kept))
    own = []
    plan = exchange_plan(False)
    bits = bits_of(lax.axis_size("seq"))
    here = lax.axis_index("seq")
    other = (jnp.where(here & 1 == 1, here & bits[1], here & bits[-1]) != 0).astype(jnp.int32)
    under_way.add("main", sum_steps(sent, own, plan, True))
    under_way.turn(["main"], grad_second, (y_ends, kept), own)
    grad_h, sent, kept, vec_mid = under_way.turn(["main"], back, y_rows)
    own_down = [kept]
    under_way.add("down", sum_steps(sent, own_down, exchange_plan(True)))
    under_way.turn(["main", "down"])
    input_grad, vec_in = under_way.turn(["main", "down"], leave, (grad_h,))

    small_in = vec_in.sum(1)
    small_mid = vec_mid
    small_out = sum(vec_out)
    vectors = [small_in[1], small_in[0], small_mid[2], small_mid[1], small_mid[0]]
    vectors += [small_out[2], small_out[1], small_out[0], small_in[2], tally]
    ends = [0]
    for item in vectors:
        ends.append(ends[-1] + item.shape[0])
    flat = jnp.concatenate(vectors)
    flat = jnp.pad(flat, (0, -flat.shape[0] % 1024)).reshape(-1, LANES)
    under_way.add("small", small_steps(flat))
    names = ["main", "down", "small"]
    (output,) = under_way.turn(names, project, (act3,))
    sides = here & 1, plan[1][2], other

    def settle_own(pieces, down):
        return settle(pieces, down, (sides[0], sides[1]), half)

    while len(own_down) == 1 or len(own) == 1:
        under_way.turn(names)
    settled = under_way.turn(names, settle_own, (own[1], own_down[1]))

    def settle_other(pieces, down, settled):
        return settle(pieces, down, (1 - sides[0], sides[2]), half, settled)

    rest = under_way.done["main"], under_way.done["down"], settled
    settled = under_way.turn(names, settle_other, rest)
    while under_way.open:
        under_way.turn(names)
    total_conv = settled[0].reshape(taps, inner, inner)
    total_up, total_down = settled[1:]
    flat = under_way.done["small"].reshape(-1)
    totals = [flat[begin:end] for begin, end in zip(ends, ends[1:])]
    return (
        output.reshape(inputs.shape),
        input_grad.reshape(inputs.shape),
        totals[0],
        totals[1],
        total_down,
        *totals[2:5],
        total_conv,
        *totals[5:8],
        total_up,
        totals[8],
        totals[9].astype(jnp.int32),
    )


def solution(mesh):
    return jax.shard_map(
        local,
        mesh=mesh,
        in_specs=(
            P("rows", "seq", None),
            P("rows", None),
            P("rows", "seq"),
            P(),
            P(),
            P(),
            P(),
            P(),
            P(),
            P(),
            P(),
            P(),
            P(),
            P(),
            P(),
            P("rows", "seq", None),
        ),
        out_specs=(
            P("rows", "seq", None),
            P("rows", "seq", None),
            P(),
            P(),
            P(),
            P(),
            P(),
            P(),
            P(),
            P(),
            P(),
            P(),
            P(),
            P(),
            P(),
        ),
        check_vma=False,
    )
```
